1024 devices in a mesh: cols: 64 (over x, z), fld: 16 (over y, core).
Axes of the slice: x: 8, y: 8, z: 8, core: 2. Of those that a mesh axis runs over, the one named last changes fastest.
Arguments:
- atm_state: bfloat16 [16, 8, 229376], P('fld', None, 'cols'), may hold values from -4 to 4
- owners: int32 [1792, 4], P('cols'), may hold values from 0 to 63, all different within a row; in each aligned block of 28 rows (0 to 27, 28 to 55, ...) at most 3 rows name the same one
- ocean_tile: int32 [1792, 4], P('cols'), may hold values from 0 to 6
- centroid_offset: float32 [1792, 4, 128], P('cols'), may hold values from -0.5 to 0.5
- remap_weight: bfloat16 [1792, 4, 128, 128], P('cols'), may hold values from 0 to 1, as said below
- ocean_state: float32 [4, 57344], P(None, 'cols'), may hold values from -4 to 4
Outputs:
- sample_fluxes: float32 [16, 4, 57344], P('fld', None, 'cols')
- ocean_next: float32 [4, 57344], P(None, 'cols')
- atm_surface: float32 [4, 229376], P(None, 'cols')
The draws below stay inside these ranges and needn't reach their ends.
Inputs may be any that keep to these rules, and one draw needn't show every extreme that they name: In each device's aligned block of 28 rows no owner appears more than 3 times, and the 4 owners of a row differ. `remap_weight`: entries are nonnegative.
All inputs are finite; a program needn't handle non-finite values.
Results may differ from the reference program's by a relative error of at most 0.00078.
Values may be sent and summed in bfloat16 or wider, within the bound.
A program may use at most 32 MiB of HBM per device.

```python
import math
import jax
import jax.numpy as jnp
import numpy as np
from jax import lax

NF = 8
TILE = 128
TOP = 4
ATILES = 28
OT_DEV = 7
MOST = 3
SAMPLES = 16
ATM_TILES = 1792
ATM_CELLS = 229376
OCN_CELLS = 57344
N_COLS = 64


def draw_atm_state(key, part):
    key = jax.random.fold_in(key, 5)
    key_body, key_size, key_sign = jax.random.split(key, 3)
    extent = (SAMPLES, NF, ATM_CELLS)
    interior = jnp.clip(jax.random.normal(key_body, extent, jnp.float32), -4.0, 4.0)
    block_length = ATILES * TILE
    position = jnp.arange(ATM_CELLS) % block_length
    at_rim = ((position == 0) | (position == block_length - 1)).astype(jnp.float32)
    rim_size = jax.random.uniform(key_size, extent, jnp.float32, 3.0, 4.0)
    rim_sign = jnp.where(jax.random.bernoulli(key_sign, 0.5, extent), 1.0, -1.0)
    values = interior * (1.0 - at_rim) + at_rim * rim_size * rim_sign
    return values.astype(jnp.bfloat16)


def draw_centroid_offset(key, part):
    key = jax.random.fold_in(key, 7)
    key_body, key_size, key_sign = jax.random.split(key, 3)
    extent = (ATILES * N_COLS, TOP, TILE)
    spread = jax.random.uniform(key_body, extent, jnp.float32, -0.5, 0.5)
    tile_place = (jnp.arange(ATILES * N_COLS) % ATILES)[:, None, None]
    cell_place = jnp.arange(TILE)[None, None, :]
    at_rim = ((tile_place == 0) & (cell_place == 0) | (tile_place == ATILES - 1) & (cell_place == TILE - 1)).astype(jnp.float32)
    rim_size = jax.random.uniform(key_size, extent, jnp.float32, 0.35, 0.5)
    rim_sign = jnp.where(jax.random.bernoulli(key_sign, 0.5, extent), 1.0, -1.0)
    return spread * (1.0 - at_rim) + at_rim * rim_size * rim_sign


def draw_remap_weight(key, part):
    key = jax.random.fold_in(key, 11)
    first, second = jax.random.split(key, 2)
    key_rim = jax.random.fold_in(key, 13)
    diagonal = jnp.exp(jax.random.uniform(first, (ATILES * N_COLS, TOP, TILE), jnp.float32, math.log(0.2), math.log(0.6)))
    beside = jax.random.uniform(second, (ATILES * N_COLS, TOP, TILE, TILE), jnp.float32, 0.0, 0.005)
    tile_place = (jnp.arange(ATILES * N_COLS) % ATILES)[:, None, None]
    cell_place = jnp.arange(TILE)[None, None, :]
    at_rim = ((tile_place == 0) & (cell_place == 0) | (tile_place == ATILES - 1) & (cell_place == TILE - 1)).astype(jnp.float32)
    rim_diagonal = jax.random.uniform(key_rim, (ATILES * N_COLS, TOP, TILE), jnp.float32, 0.8, 0.95)
    diagonal = diagonal * (1.0 - at_rim) + at_rim * rim_diagonal
    identity = (jnp.arange(TILE)[:, None] == jnp.arange(TILE)[None, :]).astype(jnp.float32)
    return (beside + identity * diagonal[..., None]).astype(jnp.bfloat16)


def touch_ends(entries, own_key, smallest, largest):
    index_at = [jax.random.randint(jax.random.fold_in(own_key, axis), (), 0, length) for axis, length in enumerate(entries.shape)]
    longest = entries.shape.index(max(entries.shape))
    neighbour = index_at[:longest] + [(index_at[longest] + 1) % entries.shape[longest]] + index_at[longest + 1:]
    return entries.at[tuple(index_at)].set(smallest).at[tuple(neighbour)].set(largest)


def shard_levels(rng, shape, pieces, smallest, high):
    gain, own = 1.0, jax.random.fold_in(rng, 6)
    for dim, blocks in pieces:
        draws = jnp.exp(jax.random.uniform(jax.random.fold_in(own, dim), (blocks,), jnp.float32, smallest / len(pieces), high / len(pieces)))
        gain = gain * jnp.repeat(draws, shape[dim] // blocks).reshape([-1 if axis == dim else 1 for axis in range(len(shape))])
    return gain


def deal_out(key, own, number, rows, amount, top, bound, skew):
    ranking = jax.random.permutation(key, amount)
    crowded, common = load_shares(amount, rows * top, bound, skew, True), load_shares(amount, rows * top, bound, skew, False)
    places = jnp.arange(amount)

    def named(tallies, offset_by):
        used = int((tallies > 0).sum())
        fixed = max(1, used // 4)
        passed = fixed + (places - fixed + offset_by * (used - fixed)) % max(1, amount - fixed)
        return jnp.zeros((amount,), jnp.int32).at[ranking[jnp.where(places < fixed, places, passed)]].set(jnp.asarray(tallies, jnp.int32))

    tallies = jnp.where(number % 4 == 0, named(crowded, number // 4), named(common, number - number // 4 - 1))
    mixed = jax.random.permutation(jax.random.fold_in(own, 3), amount)
    source_of, sink = mixed[0:amount // 2 * 2:2], mixed[1:amount // 2 * 2:2]
    room = jnp.minimum(tallies[source_of] - 1, bound - tallies[sink]) // 2
    room = jnp.where((source_of == ranking[0]) | (sink == ranking[0]) | (tallies[sink] == 0), 0, jnp.maximum(room, 0))
    passed = jax.random.randint(jax.random.fold_in(own, 4), (amount // 2,), 0, 1 << 20) % (room + 1)
    tallies = tallies.at[source_of].add(-passed).at[sink].add(passed)
    labels = jnp.searchsorted(jnp.cumsum(tallies), jnp.arange(rows * top), side="right").astype(jnp.int32)
    grid = labels.reshape(top, rows).T
    grid = grid[jax.random.permutation(jax.random.fold_in(own, 1), rows)]
    offset_by = jax.random.randint(jax.random.fold_in(own, 2), (rows, 1), 0, top)
    return jnp.take_along_axis(grid, (jnp.arange(top)[None, :] + offset_by) % top, axis=1)


def load_shares(count, total, limit, skew, full):
    portions = [(1 << 20) // math.isqrt(standing ** skew) + 1 for standing in range(1, count + 1)]
    largest = limit if full else min(limit, max(-(-total // count), total * portions[0] // sum(portions)))
    least = 1 if total - largest >= count - 1 else 0
    given, rest = [largest] + [least] * (count - 1), total - largest - least * (count - 1)
    while rest > 0:
        candidates = [i for i in range(1, count) if given[i] < largest] or [i for i in range(1, count) if given[i] < limit]
        whole, left = sum([portions[i] for i in candidates]), rest
        for i in candidates:
            more = min(limit - given[i], max(1, left * portions[i] // whole), rest)
            given[i] = given[i] + more
            rest = rest - more
    return np.array(given)


def normal_values(key, shape, scale, bound, cuts=(), kind=jnp.bfloat16):
    level = shard_levels(key, shape, cuts, -0.22, 0.18) if cuts else 1.0
    entries = jax.random.normal(key, shape, jnp.float32) * scale * level
    return jnp.minimum(jnp.maximum(entries, -bound), bound).astype(kind)


def setup_inputs(seed: int = 0) -> dict:
    streams_of = jax.random.split(jax.random.key(seed), 7)
    atm_state = draw_atm_state(jax.random.fold_in(streams_of[6], 71), 0)
    owners_keys = jax.random.split(jax.random.fold_in(streams_of[1], 1), ATM_TILES // ATILES)
    owners_turns = jax.random.permutation(jax.random.fold_in(streams_of[1], 3), ATM_TILES // ATILES)
    owners = jax.vmap(lambda own, number: deal_out(jax.random.fold_in(streams_of[1], 2), own, number, ATILES, N_COLS, TOP, MOST, 2))(owners_keys, owners_turns).reshape((ATM_TILES, TOP))
    ocean_tile = touch_ends(jax.random.randint(streams_of[2], (ATM_TILES, TOP), 0, OT_DEV), jax.random.fold_in(streams_of[2], 1), 0, OT_DEV - 1).astype(jnp.int32)
    centroid_offset = draw_centroid_offset(jax.random.fold_in(streams_of[6], 71), 0)
    remap_weight = draw_remap_weight(jax.random.fold_in(streams_of[6], 71), 0)
    ocean_state = normal_values(streams_of[5], (4, OCN_CELLS), 1.0, 4.0, ((1, 64),), jnp.float32)
    return dict(atm_state=atm_state, owners=owners, ocean_tile=ocean_tile, centroid_offset=centroid_offset, remap_weight=remap_weight, ocean_state=ocean_state)


def surface_fluxes(forcing, ocean_now, insolation):
    slip_u = forcing[0] - ocean_now[1]
    slip_v = forcing[1] - ocean_now[2]
    wind_speed = jnp.sqrt(slip_u * slip_u + slip_v * slip_v + 0.25)
    saturation = 0.9 * jnp.exp(0.07 * ocean_now[0] - 0.1 * forcing[4])
    sensible = 0.4 * wind_speed * (ocean_now[0] - forcing[2])
    latent = 0.4 * wind_speed * (saturation - forcing[3])
    net_heat = insolation * jax.nn.softplus(forcing[5]) + 0.3 * forcing[6] - 0.1 * ocean_now[0] - sensible - latent
    freshwater = jax.nn.softplus(forcing[7]) - latent
    return jnp.stack([0.5 * wind_speed * slip_u, 0.5 * wind_speed * slip_v, net_heat, freshwater])

def reference(atm_state, owners, ocean_tile, centroid_offset, remap_weight, ocean_state):
    tile_count = ATILES * N_COLS
    ocean_tiles = OT_DEV * N_COLS
    wide_weights = remap_weight.astype(jnp.float32)
    target = (owners * OT_DEV + ocean_tile).reshape(-1).astype(jnp.int32)
    intersection_area = lax.optimization_barrier(jnp.sum(wide_weights, axis=3)).reshape(-1, TILE)
    coverage = jax.ops.segment_sum(intersection_area, target, num_segments=ocean_tiles)
    divisor = jnp.maximum(coverage, 1.0)

    def one_sample(packed):
        block, position = packed
        values = block.astype(jnp.float32)
        slope = 0.5 * (jnp.roll(values, -1, axis=1) - jnp.roll(values, 1, axis=1))
        value_tiles = values.reshape(NF, tile_count, TILE).transpose(1, 0, 2)
        slope_tiles = slope.reshape(NF, tile_count, TILE).transpose(1, 0, 2)
        rebuilt = (value_tiles[:, None] + centroid_offset[:, :, None, :] * slope_tiles[:, None]).astype(jnp.bfloat16)
        partials = jnp.einsum('tkfa,tkoa->tkfo', rebuilt.astype(jnp.float32), wide_weights)
        summed = jax.ops.segment_sum(partials.reshape(-1, NF, TILE), target, num_segments=ocean_tiles)
        forcing = (summed / divisor[:, None, :]).transpose(1, 0, 2).reshape(NF, OCN_CELLS)
        insolation = 0.5 + 1.5 * position.astype(jnp.float32) / (SAMPLES - 1)
        return surface_fluxes(forcing, ocean_state, insolation)
    sample_fluxes = lax.map(one_sample, (atm_state, jnp.arange(SAMPLES, dtype=jnp.int32)))
    mean_flux = lax.optimization_barrier(jnp.sum(sample_fluxes, axis=0)) / SAMPLES
    ocean_next = ocean_state + 0.5 * jnp.stack([mean_flux[2], mean_flux[0], mean_flux[1], -mean_flux[3]])
    states = ocean_next.reshape(4, ocean_tiles, TILE)
    entry_state = jnp.take(states, target, axis=1).transpose(1, 0, 2).reshape(tile_count, TOP, 4, TILE)
    remapped = jnp.einsum('tkso,tkoa->tksa', entry_state, wide_weights, precision=lax.Precision.HIGHEST)
    remapped = lax.optimization_barrier(jnp.sum(remapped, axis=1))
    column_area = lax.optimization_barrier(jnp.sum(lax.optimization_barrier(jnp.sum(wide_weights, axis=2)), axis=1))
    atm_surface = (remapped / column_area[:, None, :]).transpose(1, 0, 2).reshape(4, ATM_CELLS)
    return (sample_fluxes, ocean_next, atm_surface)
```

```python
import functools
import math

import jax
import jax.numpy as jnp
from jax import lax
from jax.experimental import pallas as pl
from jax.experimental.pallas import tpu as pltpu
from jax.sharding import PartitionSpec as P

TILE = 128
FIELDS = 8
MOST = 3
PAD = 32
MESH = pl.DeviceIdType.MESH
F32 = jnp.float32
BF16 = jnp.bfloat16


def split(x):
    high = x.astype(BF16)
    return high, (x - high.astype(F32)).astype(BF16)


def mixed(matrix, x):
    high, low = split(x)
    return jnp.dot(matrix, jnp.concatenate([high, low], axis=0), preferred_element_type=F32)


def kernel(
    ring, samples, tiles, reach, otiles, quarter,
    atm, owners, otile, cent, w_hbm, ocean,
    flux_out, ocean_out, atm_out,
    w, val, part, pick, pick_t, spread, oc, back,
    send1, recv1, send2, recv2, send3, recv3, send4, recv4, send5, recv5, send6, recv6,
    w_sem, halo_send, halo_recv, local_sem, ssem, rsem, osend, orecv,
):
    cols = ring * ring
    slots = MOST * ring
    rows = ring * slots
    entries = reach * PAD
    col = lax.axis_index("cols")
    fld = lax.axis_index("fld")
    x, z = col // ring, col % ring
    core = fld % 2
    first = (1 - core) * x + core * z
    second = (1 - core) * z + core * x

    def on_first(p):
        return ((1 - core) * (p * ring + second) + core * (second * ring + p), fld)

    def on_second(p):
        return ((1 - core) * (first * ring + p) + core * (p * ring + first), fld)

    def on_fld(p):
        return (col, p)

    left, right = (col + cols - 1) % cols, (col + 1) % cols

    chunk = 4 if tiles % 4 == 0 else 1
    chunks = tiles // chunk

    def weights(c):
        at = pl.ds(c * chunk, chunk)
        return pltpu.make_async_copy(w_hbm.at[at], w.at[at], w_sem.at[c])

    def start_weights(c, carry):
        weights(c).start()
        return carry

    lax.fori_loop(0, chunks, start_weights, 0)

    barrier = pltpu.get_barrier_semaphore()

    def greet(device):
        pl.semaphore_signal(barrier, inc=1, device_id=device, device_id_type=MESH)

    def greet_ring(d, carry):
        greet(on_first((first + d) % ring))
        greet(on_second((second + d) % ring))
        return carry

    def greet_fld(d, carry):
        greet(on_fld((fld + d) % samples))
        return carry

    greet((left, fld))
    greet((right, fld))
    lax.fori_loop(1, ring, greet_ring, 0)
    lax.fori_loop(1, samples, greet_fld, 0)

    def exchange(stage, count, me, device, source, target):
        def copy(d, to):
            return pltpu.make_async_remote_copy(
                src_ref=source((me + d) % count),
                dst_ref=target.at[to],
                send_sem=ssem.at[stage, d],
                recv_sem=rsem.at[stage, d],
                device_id=device((me + d) % count),
                device_id_type=MESH,
            )

        def send():
            def one(d, carry):
                copy(d, me).start()
                return carry

            lax.fori_loop(1, count, one, 0)

        def arrive():
            def one(d, carry):
                copy(d, (me + count - d) % count).wait_recv()
                return carry

            lax.fori_loop(1, count, one, 0)

        def leave():
            def one(d, carry):
                copy(d, me).wait_send()
                return carry

            lax.fori_loop(1, count, one, 0)

        return send, arrive, leave

    for t in range(tiles):
        val[t + 1] = atm[0, :, t * TILE : (t + 1) * TILE].astype(F32)
    for r in range(4):
        oc[r] = jnp.zeros((8, TILE), F32)
        for t in range(otiles):
            oc[r, t : t + 1, :] = ocean[r : r + 1, t * TILE : (t + 1) * TILE]
    part[...] = jnp.zeros_like(part)

    pl.semaphore_wait(barrier, 2 + 2 * (ring - 1) + samples - 1)
    to_right = pltpu.make_async_remote_copy(
        src_ref=val.at[tiles], dst_ref=val.at[0], send_sem=halo_send.at[0], recv_sem=halo_recv.at[0],
        device_id=(right, fld), device_id_type=MESH,
    )
    to_left = pltpu.make_async_remote_copy(
        src_ref=val.at[1], dst_ref=val.at[tiles + 1], send_sem=halo_send.at[1], recv_sem=halo_recv.at[1],
        device_id=(left, fld), device_id_type=MESH,
    )
    to_right.start()
    to_left.start()

    def down(ref, fill):
        table = jnp.concatenate([ref[...], jnp.full((PAD - tiles, reach), fill, jnp.int32)], axis=0)
        columns = [jnp.broadcast_to(table[:, k : k + 1], (PAD, entries)) for k in range(reach)]
        return jnp.concatenate(columns, axis=0).astype(F32)

    owner_down = down(owners, cols)
    owner_across = owner_down.T
    tile_across = down(otile, 0).T.astype(jnp.int32)
    at_row = lax.broadcasted_iota(jnp.int32, (entries, entries), 0)
    at_lane = lax.broadcasted_iota(jnp.int32, (entries, entries), 1)
    same = owner_down == owner_across
    rank_down = jnp.sum((same & (at_lane < at_row)).astype(F32), axis=1, keepdims=True).astype(jnp.int32)
    rank_across = jnp.sum((same & (at_row < at_lane)).astype(F32), axis=0, keepdims=True).astype(jnp.int32)

    def slot(owner, rank):
        owner = owner.astype(jnp.int32)
        high = owner // ring
        low = owner - high * ring
        group = (1 - core) * high + core * low
        place = (1 - core) * low + core * high
        return jnp.where(owner < cols, group * slots + rank * ring + place, -1)

    slot_across = slot(owner_across[:1], rank_across)
    slot_down = slot(owner_down[:, :1], rank_down)
    pick_f = (lax.broadcasted_iota(jnp.int32, (rows, entries), 0) == slot_across).astype(F32)
    pick[:, :entries] = pick_f.astype(BF16)
    pick[:, entries:] = pick_f.astype(BF16)
    pick_b = (lax.broadcasted_iota(jnp.int32, (entries, rows), 1) == slot_down).astype(F32).astype(BF16)
    pick_t[...] = pick_b
    named = jnp.sum(pick_f * (tile_across[:1] + 1).astype(F32), axis=1, keepdims=True)
    named = jnp.broadcast_to(named - 1.0, (rows, TILE))
    for g in range(ring):
        send1[g, (FIELDS + 1) * slots :] = named[g * slots : (g + 1) * slots]

    lane = lax.broadcasted_iota(jnp.int32, (FIELDS, TILE), 1)
    ones = jnp.ones((FIELDS, TILE), F32)

    def tile_sums(t):
        before, here, after = val[t], val[t + 1], val[t + 2]
        low = jnp.where(lane == 0, pltpu.roll(before, 1, 1), pltpu.roll(here, 1, 1))
        high = jnp.where(lane == TILE - 1, pltpu.roll(after, TILE - 1, 1), pltpu.roll(here, TILE - 1, 1))
        slope = 0.5 * (high - low)
        for k in range(reach):
            rebuilt = here + cent[t, k : k + 1, :] * slope
            operand = jnp.concatenate([rebuilt, ones], axis=0).astype(BF16)
            sums = lax.dot_general(
                operand, w[t, k], (((1,), (1,)), ((), ())), preferred_element_type=F32
            )
            part[pl.ds(k * PAD + t, FIELDS, stride=entries), :] = sums[:FIELDS]
            part[pl.ds(FIELDS * entries + k * PAD + t, 1), :] = sums[FIELDS : FIELDS + 1]

    def chunk_sums(c):
        weights(c).wait()
        for q in range(chunk):
            tile_sums(c * chunk + q)

    def inner(c, carry):
        chunk_sums(c)
        return carry

    lax.fori_loop(1, chunks - 1, inner, 0)
    to_right.wait_recv()
    to_left.wait_recv()

    def outer(c, carry):
        chunk_sums(c * (chunks - 1))
        return carry

    lax.fori_loop(0, 2, outer, 0)

    send, arrive, leave1 = exchange(0, ring, first, on_first, lambda p: send1.at[p], recv1)
    for f in range(FIELDS + 1):
        slotted = mixed(pick[...], part[f * entries : (f + 1) * entries])
        for g in range(ring):
            send1[g, f * slots : (f + 1) * slots] = slotted[g * slots : (g + 1) * slots]
    send()
    own = pltpu.make_async_copy(send1.at[first], recv1.at[first], local_sem.at[0])
    own.start()
    arrive()
    own.wait()

    row = lax.broadcasted_iota(jnp.int32, (rows, TILE), 0)
    target = recv1[:, (FIELDS + 1) * slots :].reshape(rows, TILE).astype(jnp.int32)
    member = (target >= 0) & (target + 8 * (row % ring) == lax.broadcasted_iota(jnp.int32, (rows, TILE), 1))
    member = member.astype(F32)
    gather = member.T[: 8 * ring].astype(BF16)
    spread[...] = member.astype(BF16)
    gather = jnp.concatenate([gather, gather], axis=1)
    send, arrive, leave2 = exchange(1, ring, second, on_second, lambda p: send2.at[p], recv2)
    for f in range(FIELDS + 1):
        dense = mixed(gather, recv1[:, f * slots : (f + 1) * slots].reshape(rows, TILE))
        send2[:, f] = dense.reshape(ring, 8, TILE)
    send()
    own = pltpu.make_async_copy(send2.at[second], recv2.at[second], local_sem.at[1])
    own.start()
    arrive()
    own.wait()

    total = recv2[0]
    for p in range(1, ring):
        total = total + recv2[p]
    forcing = total[:FIELDS] / jnp.maximum(total[FIELDS], 1.0)[None]

    sst, uo, vo = oc[0], oc[1], oc[2]
    slip_u = forcing[0] - uo
    slip_v = forcing[1] - vo
    wind_speed = jnp.sqrt(slip_u * slip_u + slip_v * slip_v + 0.25)
    saturation = 0.9 * jnp.exp(0.07 * sst - 0.1 * forcing[4])
    sensible = 0.4 * wind_speed * (sst - forcing[2])
    latent = 0.4 * wind_speed * (saturation - forcing[3])

    def softplus(v):
        return jnp.maximum(v, 0.0) + jnp.log1p(jnp.exp(-jnp.abs(v)))

    insolation = 0.5 + 1.5 * fld.astype(F32) / (samples - 1)
    net_heat = insolation * softplus(forcing[5]) + 0.3 * forcing[6] - 0.1 * sst - sensible - latent
    freshwater = softplus(forcing[7]) - latent
    stress_u = 0.5 * wind_speed * slip_u
    stress_v = 0.5 * wind_speed * slip_v
    send3[0] = net_heat
    send3[1] = stress_u
    send3[2] = stress_v
    send3[3] = -freshwater

    my_row = fld % 4
    send, arrive, leave3 = exchange(2, samples, fld, on_fld, lambda p: send3.at[p % 4], recv3)
    send()
    own = pltpu.make_async_copy(send3.at[my_row], recv3.at[fld], local_sem.at[2])
    own.start()
    for i, flux in enumerate((stress_u, stress_v, net_heat, freshwater)):
        flux_out[i] = flux
    arrive()
    own.wait()
    flux_sum = recv3[0]
    for p in range(1, samples):
        flux_sum = flux_sum + recv3[p]
    send4[...] = oc[my_row] + (0.5 / samples) * flux_sum

    send, arrive, leave4 = exchange(3, ring, second, on_second, lambda p: send4, recv4)
    send()
    mates = []
    for d in range(1, 4):
        mates.append(
            [
                pltpu.make_async_remote_copy(
                    src_ref=send4, dst_ref=ocean_row, send_sem=osend.at[d], recv_sem=orecv.at[d],
                    device_id=(col, (fld // 4) * 4 + (my_row + d) % 4), device_id_type=MESH,
                )
                for ocean_row in (back.at[my_row], back.at[(my_row + 4 - d) % 4])
            ]
        )
        mates[-1][0].start()
    recv4[second] = send4[...]
    back[my_row] = send4[...]
    arrive()

    states = recv4[...].reshape(ring * 8, TILE)
    scatter = spread[:, : ring * 8]
    slotted = mixed(jnp.concatenate([scatter, scatter], axis=1), states)
    for p in range(ring):
        send5[p] = slotted[p * slots : (p + 1) * slots]
    send, arrive, leave5 = exchange(4, ring, first, on_first, lambda p: send5.at[p], recv5)
    send()
    own = pltpu.make_async_copy(send5.at[first], recv5.at[first], local_sem.at[3])
    own.start()
    arrive()
    own.wait()
    pick_b = pick_t[...]
    part[:entries] = mixed(jnp.concatenate([pick_b, pick_b], axis=1), recv5[...].reshape(rows, TILE))

    begin = (fld // 4) * quarter
    row16 = lax.broadcasted_iota(jnp.int32, (16, TILE), 0)

    def remap(q, carry):
        t = begin + q
        state = part[pl.ds(t, reach, stride=PAD), :]
        high, low = split(state)
        high, low = high.astype(F32), low.astype(F32)
        sums = jnp.zeros((16, TILE), F32)
        for k in range(reach):
            operand = jnp.where(row16 == 0, high[k : k + 1], jnp.where(row16 == 1, low[k : k + 1], 1.0))
            sums = sums + jnp.dot(operand.astype(BF16), w[t, k], preferred_element_type=F32)
        send6[pl.ds(q, 1), :] = (sums[0:1] + sums[1:2]) / sums[2:3]
        return carry

    send6[...] = jnp.zeros_like(send6)
    lax.fori_loop(0, quarter, remap, 0)
    send, arrive, leave6 = exchange(5, samples, fld, on_fld, lambda p: send6, recv6)
    send()
    recv6[fld] = send6[...]
    for d in range(1, 4):
        mates[d - 1][1].wait_recv()
    ocean_out[...] = back[...]
    arrive()
    atm_out[...] = recv6[...]

    to_right.wait_send()
    to_left.wait_send()
    leave1()
    leave2()
    leave3()
    leave4()
    leave5()
    leave6()
    for d in range(1, 4):
        mates[d - 1][0].wait_send()


def shards(atm_state, owners, ocean_tile, centroid_offset, remap_weight, ocean_state):
    ring = math.isqrt(lax.axis_size("cols"))
    samples = lax.axis_size("fld")
    cells = atm_state.shape[2]
    tiles = cells // TILE
    reach = owners.shape[1]
    ocells = ocean_state.shape[1]
    otiles = ocells // TILE
    slots = MOST * ring
    rows = ring * slots
    entries = reach * PAD
    groups = samples // 4
    quarter = -(-tiles // groups)
    sent = (FIELDS + 2) * slots
    most = max(ring, samples)
    vmem = pl.BlockSpec(memory_space=pltpu.VMEM)
    fluxes, ocean, back = pl.pallas_call(
        functools.partial(kernel, ring, samples, tiles, reach, otiles, quarter),
        out_shape=(
            jax.ShapeDtypeStruct((4, 8, TILE), F32),
            jax.ShapeDtypeStruct((4, 8, TILE), F32),
            jax.ShapeDtypeStruct((samples, 8, TILE), F32),
        ),
        in_specs=[vmem, vmem, vmem, vmem, pl.BlockSpec(memory_space=pl.ANY), vmem],
        out_specs=(vmem, vmem, vmem),
        scratch_shapes=[
            pltpu.VMEM((tiles, reach, TILE, TILE), BF16),
            pltpu.VMEM((tiles + 2, FIELDS, TILE), F32),
            pltpu.VMEM(((FIELDS + 1) * entries, TILE), F32),
            pltpu.VMEM((rows, 2 * entries), BF16),
            pltpu.VMEM((entries, rows), BF16),
            pltpu.VMEM((rows, TILE), BF16),
            pltpu.VMEM((4, 8, TILE), F32),
            pltpu.VMEM((4, 8, TILE), F32),
            pltpu.VMEM((ring, sent, TILE), F32),
            pltpu.VMEM((ring, sent, TILE), F32),
            pltpu.VMEM((ring, FIELDS + 1, 8, TILE), F32),
            pltpu.VMEM((ring, FIELDS + 1, 8, TILE), F32),
            pltpu.VMEM((4, 8, TILE), F32),
            pltpu.VMEM((samples, 8, TILE), F32),
            pltpu.VMEM((8, TILE), F32),
            pltpu.VMEM((ring, 8, TILE), F32),
            pltpu.VMEM((ring, slots, TILE), F32),
            pltpu.VMEM((ring, slots, TILE), F32),
            pltpu.VMEM((8, TILE), F32),
            pltpu.VMEM((samples, 8, TILE), F32),
            pltpu.SemaphoreType.DMA((tiles,)),
            pltpu.SemaphoreType.DMA((2,)),
            pltpu.SemaphoreType.DMA((2,)),
            pltpu.SemaphoreType.DMA((4,)),
            pltpu.SemaphoreType.DMA((6, most)),
            pltpu.SemaphoreType.DMA((6, most)),
            pltpu.SemaphoreType.DMA((4,)),
            pltpu.SemaphoreType.DMA((4,)),
        ],
        compiler_params=pltpu.CompilerParams(
            collective_id=0, has_side_effects=True, vmem_limit_bytes=32 * 1024 * 1024
        ),
        name="coupling",
    )(atm_state, owners, ocean_tile, centroid_offset, remap_weight, ocean_state)
    sample_fluxes = fluxes[:, :otiles].reshape(1, 4, ocells)
    ocean_next = ocean[:, :otiles].reshape(4, ocells)
    atm_surface = back.reshape(groups, 4, 8, TILE)[:, :, :quarter].transpose(1, 0, 2, 3)
    return sample_fluxes, ocean_next, atm_surface.reshape(4, groups * quarter * TILE)[:, :cells]


def solution(mesh):
    return jax.shard_map(
        shards,
        mesh=mesh,
        in_specs=(
            P("fld", None, "cols"),
            P("cols", None),
            P("cols", None),
            P("cols", None, None),
            P("cols", None, None, None),
            P(None, "cols"),
        ),
        out_specs=(P("fld", None, "cols"), P(None, "cols"), P(None, "cols")),
        check_vma=False,
    )
```

```python
import functools
import math

import jax
import jax.numpy as jnp
from jax import lax
from jax.experimental import pallas as pl
from jax.experimental.pallas import tpu as pltpu
from jax.sharding import PartitionSpec as P

TILE = 128
FIELDS = 8
MOST = 3
PAD = 32
LEVELS = 5400.0
LEAST = 1e-30
MESH = pl.DeviceIdType.MESH
F32 = jnp.float32
BF16 = jnp.bfloat16
I32 = jnp.int32
I16 = jnp.int16


def split(x):
    high = x.astype(BF16)
    return high, (x - high.astype(F32)).astype(BF16)


def mixed(matrix, x):
    high, low = split(x)
    return jnp.dot(matrix, jnp.concatenate([high, low], axis=0), preferred_element_type=F32)


def twice(matrix):
    return jnp.concatenate([matrix, matrix], axis=1)


def kernel(
    ring, samples, tiles, reach, otiles,
    atm_hbm, owners_hbm, otile_hbm, cent_hbm, w_hbm, ocean_hbm,
    flux_out, ocean_out, atm_out,
    atm, owners, otile, cent, w, ocean,
    val, part, pick, pick_t, spread, oc, table, col_inverse, lhs,
    send0, recv0, send1a, recv1a, send1, recv1, send2a, recv2a, send2, recv2,
    send3, recv3, send3y, recv3y, send4, recv4, send5, recv5,
    in_sem, w_sem, halo_send, halo_recv, ssem, rsem, psend, precv,
):
    cols = ring * ring
    chips = samples // 2
    slots = MOST * ring
    rows = ring * slots
    entries = reach * PAD
    col = lax.axis_index("cols")
    fld = lax.axis_index("fld")
    x, z = col // ring, col % ring
    chip, core = fld // 2, fld % 2
    first = (1 - core) * x + core * z
    second = (1 - core) * z + core * x

    def on_first(p):
        return ((1 - core) * (p * ring + second) + core * (second * ring + p), fld)

    def on_second(p):
        return ((1 - core) * (first * ring + p) + core * (p * ring + first), fld)

    def on_chip(p):
        return (col, p * 2 + core)

    sibling = (col, chip * 2 + 1 - core)
    left, right = (col + cols - 1) % cols, (col + 1) % cols

    barrier = pltpu.get_barrier_semaphore()

    def greet(device):
        pl.semaphore_signal(barrier, inc=1, device_id=device, device_id_type=MESH)

    def greet_ring(d, carry):
        greet(on_first((first + d) % ring))
        greet(on_second((second + d) % ring))
        return carry

    def greet_chip(d, carry):
        greet(on_chip((chip + d) % chips))
        return carry

    greet((left, fld))
    greet((right, fld))
    greet(sibling)
    lax.fori_loop(1, ring, greet_ring, 0)
    lax.fori_loop(1, chips, greet_chip, 0)

    small = [
        pltpu.make_async_copy(source, target, in_sem.at[i])
        for i, (source, target) in enumerate(
            ((atm_hbm, atm), (owners_hbm, owners), (otile_hbm, otile), (cent_hbm, cent), (ocean_hbm, ocean))
        )
    ]
    for copy in small:
        copy.start()
    chunk = 4 if tiles % 4 == 0 else 1
    chunks = tiles // chunk

    def weights(c):
        at = pl.ds(c * chunk, chunk)
        return pltpu.make_async_copy(w_hbm.at[at], w.at[at], w_sem.at[c])

    def start_weights(c, carry):
        weights(c).start()
        return carry

    lax.fori_loop(0, chunks, start_weights, 0)

    def exchange(stage, count, me, device, source, target):
        def copy(d, to):
            return pltpu.make_async_remote_copy(
                src_ref=source((me + d) % count),
                dst_ref=target.at[to],
                send_sem=ssem.at[stage, d],
                recv_sem=rsem.at[stage, d],
                device_id=device((me + d) % count),
                device_id_type=MESH,
            )

        def send():
            for d in sorted(range(1, count), key=lambda d: -min(d, count - d)):
                copy(d, me).start()

        def arrive():
            def one(d, carry):
                copy(d, (me + count - d) % count).wait_recv()
                return carry

            lax.fori_loop(1, count, one, 0)

        def leave():
            def one(d, carry):
                copy(d, me).wait_send()
                return carry

            lax.fori_loop(1, count, one, 0)

        return send, arrive, leave

    def to_sibling(i, source, target):
        return pltpu.make_async_remote_copy(
            src_ref=source, dst_ref=target, send_sem=psend.at[i], recv_sem=precv.at[i],
            device_id=sibling, device_id_type=MESH,
        )

    part[...] = jnp.zeros_like(part)
    col_inverse[...] = jnp.ones_like(col_inverse)
    small[0].wait()
    for t in range(tiles):
        val[t + 1] = atm[0, :, t * TILE : (t + 1) * TILE].astype(F32)
    to_right = pltpu.make_async_remote_copy(
        src_ref=val.at[tiles], dst_ref=val.at[0], send_sem=halo_send.at[0], recv_sem=halo_recv.at[0],
        device_id=(right, fld), device_id_type=MESH,
    )
    to_left = pltpu.make_async_remote_copy(
        src_ref=val.at[1], dst_ref=val.at[tiles + 1], send_sem=halo_send.at[1], recv_sem=halo_recv.at[1],
        device_id=(left, fld), device_id_type=MESH,
    )
    pl.semaphore_wait(barrier, 3 + 2 * (ring - 1) + chips - 1)
    to_right.start()
    to_left.start()

    small[1].wait()
    small[2].wait()
    lane = lax.broadcasted_iota(I32, (FIELDS, TILE), 1)

    def across(ref, fill):
        table[...] = jnp.full((8, TILE), fill, F32)
        table[:reach, :tiles] = ref[...].astype(F32)
        line = jnp.broadcast_to(table[0:1], (8, TILE))
        for k in range(1, reach):
            shifted = pltpu.roll(jnp.broadcast_to(table[k : k + 1], (8, TILE)), k * PAD, 1)
            line = jnp.where(lane >= k * PAD, shifted, line)
        return line[:1]

    owner_across = across(owners, float(cols))
    tile_across = across(otile, 0.0)
    owner_down = jnp.broadcast_to(owner_across, (entries, entries)).T
    at_row = lax.broadcasted_iota(I32, (entries, entries), 0)
    at_lane = lax.broadcasted_iota(I32, (entries, entries), 1)
    same = owner_down == owner_across
    rank_down = jnp.sum((same & (at_lane < at_row)).astype(F32), axis=1, keepdims=True).astype(I32)
    rank_across = jnp.sum((same & (at_row < at_lane)).astype(F32), axis=0, keepdims=True).astype(I32)

    def slot(owner, rank):
        owner = owner.astype(I32)
        high = owner // ring
        low = owner - high * ring
        group = (1 - core) * high + core * low
        place = (1 - core) * low + core * high
        return jnp.where(owner < cols, group * slots + rank * ring + place, -1)

    slot_across = slot(owner_across, rank_across)
    slot_down = slot(owner_down[:, :1], rank_down)
    pick_f = (lax.broadcasted_iota(I32, (rows, entries), 0) == slot_across).astype(F32)
    pick[...] = twice(pick_f.astype(BF16))
    pick_b = (lax.broadcasted_iota(I32, (entries, rows), 1) == slot_down).astype(F32).astype(BF16)
    pick_t[...] = twice(pick_b)
    named = jnp.sum(pick_f * (tile_across + 1.0), axis=1, keepdims=True)
    named = jnp.broadcast_to(named - 1.0, (rows, TILE))
    for g in range(ring):
        send0[g] = named[g * slots : (g + 1) * slots]
    send, arrive0, leave0 = exchange(0, ring, first, on_first, lambda p: send0.at[p], recv0)
    send()
    recv0[first] = send0[first]

    small[4].wait()
    for r in range(4):
        oc[r] = jnp.zeros((8, TILE), F32)
        for t in range(otiles):
            oc[r, t : t + 1, :] = ocean[r : r + 1, t * TILE : (t + 1) * TILE]

    ones = jnp.ones((FIELDS, TILE), F32)
    small[3].wait()

    def tile_sums(t):
        before, here, after = val[t], val[t + 1], val[t + 2]
        low = jnp.where(lane == 0, pltpu.roll(before, 1, 1), pltpu.roll(here, 1, 1))
        high = jnp.where(lane == TILE - 1, pltpu.roll(after, TILE - 1, 1), pltpu.roll(here, TILE - 1, 1))
        slope = 0.5 * (high - low)
        for k in range(reach):
            rebuilt = here + cent[t, k : k + 1, :] * slope
            operand = jnp.concatenate([rebuilt, ones], axis=0).astype(BF16)
            sums = lax.dot_general(
                operand, w[t, k], (((1,), (1,)), ((), ())), preferred_element_type=F32
            )
            area = sums[FIELDS : FIELDS + 1]
            code = jnp.round(sums[:FIELDS] * (LEVELS / jnp.maximum(area, LEAST)))
            part[pl.ds(k * PAD + t, FIELDS, stride=entries), :] = code
            part[pl.ds(FIELDS * entries + k * PAD + t, 1), :] = area

    def chunk_sums(c):
        weights(c).wait()
        for q in range(chunk):
            tile_sums(c * chunk + q)

    def inner(c, carry):
        chunk_sums(c)
        return carry

    lax.fori_loop(1, chunks - 1, inner, 0)
    to_right.wait_recv()
    to_left.wait_recv()

    def outer(c, carry):
        chunk_sums(c * (chunks - 1))
        return carry

    lax.fori_loop(0, 2, outer, 0)

    send, arrive1a, leave1a = exchange(1, ring, first, on_first, lambda p: send1a.at[p], recv1a)
    slotted = mixed(pick[...], part[FIELDS * entries :])
    for g in range(ring):
        send1a[g] = slotted[g * slots : (g + 1) * slots]
    send()
    send, arrive1, leave1 = exchange(2, ring, first, on_first, lambda p: send1.at[p], recv1)
    for f in range(0, FIELDS, 2):
        one = mixed(pick[...], part[f * entries : (f + 1) * entries])
        two = mixed(pick[...], part[(f + 1) * entries : (f + 2) * entries])
        for g in range(ring):
            at = slice(g * slots, (g + 1) * slots)
            pair = jnp.concatenate([one[at], two[at]], axis=0)
            send1[g, f * slots : (f + 2) * slots] = pair.astype(I32).astype(I16)
    send()
    recv1a[first] = send1a[first]
    recv1[first] = send1[first]

    arrive0()
    row = lax.broadcasted_iota(I32, (rows, TILE), 0)
    target = recv0[...].reshape(rows, TILE).astype(I32)
    member = (target >= 0) & (target + 8 * (row % ring) == lax.broadcasted_iota(I32, (rows, TILE), 1))
    member = member.astype(F32)
    gather = twice(member.T[: 8 * ring].astype(BF16))
    spread[...] = twice(member[:, : 8 * ring].astype(BF16))
    all_ones = jnp.ones((16, reach * TILE), BF16)

    def column_area(c, carry):
        for q in range(chunk):
            t = c * chunk + q
            area = jnp.dot(all_ones, w[t].reshape(reach * TILE, TILE), preferred_element_type=F32)
            col_inverse[pl.ds(t, 1), :] = 1.0 / area[:1]
        return carry

    lax.fori_loop(0, chunks, column_area, 0)

    send, arrive2a, leave2a = exchange(3, ring, second, on_second, lambda p: send2a.at[p], recv2a)
    arrive1a()
    areas = recv1a[...].reshape(rows, TILE)
    dense_area = mixed(gather, areas)
    send2a[...] = dense_area.reshape(ring, 8, TILE)
    send()
    per_area = 1.0 / jnp.maximum(dense_area, LEAST)
    send, arrive2, leave2 = exchange(4, ring, second, on_second, lambda p: send2.at[p], recv2)
    arrive1()
    for f in range(0, FIELDS, 2):
        pair = recv1[:, f * slots : (f + 2) * slots].astype(I32).astype(F32)
        one = mixed(gather, pair[:, :slots].reshape(rows, TILE) * areas) * per_area
        two = mixed(gather, pair[:, slots:].reshape(rows, TILE) * areas) * per_area
        both = jnp.concatenate([one.reshape(ring, 8, TILE), two.reshape(ring, 8, TILE)], axis=1)
        send2[:, f * 8 : (f + 2) * 8] = jnp.round(both).astype(I32).astype(I16)
    send()
    recv2a[second] = send2a[second]
    recv2[second] = send2[second]
    arrive2a()
    arrive2()

    coverage = jnp.zeros((8, TILE), F32)
    total = jnp.zeros((FIELDS, 8, TILE), F32)
    for p in range(ring):
        area = recv2a[p]
        coverage = coverage + area
        total = total + recv2[p].astype(I32).astype(F32).reshape(FIELDS, 8, TILE) * area[None]
    forcing = total * (1.0 / (LEVELS * jnp.maximum(coverage, 1.0)))[None]

    sst, uo, vo = oc[0], oc[1], oc[2]
    slip_u = forcing[0] - uo
    slip_v = forcing[1] - vo
    wind_speed = jnp.sqrt(slip_u * slip_u + slip_v * slip_v + 0.25)
    saturation = 0.9 * jnp.exp(0.07 * sst - 0.1 * forcing[4])
    sensible = 0.4 * wind_speed * (sst - forcing[2])
    latent = 0.4 * wind_speed * (saturation - forcing[3])

    def softplus(v):
        return jnp.maximum(v, 0.0) + jnp.log1p(jnp.exp(-jnp.abs(v)))

    insolation = 0.5 + 1.5 * fld.astype(F32) / (samples - 1)
    net_heat = insolation * softplus(forcing[5]) + 0.3 * forcing[6] - 0.1 * sst - sensible - latent
    freshwater = softplus(forcing[7]) - latent
    stress_u = 0.5 * wind_speed * slip_u
    stress_v = 0.5 * wind_speed * slip_v
    send3[0] = net_heat
    send3[1] = stress_u
    send3[2] = stress_v
    send3[3] = -freshwater

    mine, other = pl.ds(2 * core, 2), pl.ds(2 - 2 * core, 2)
    pair_copy = to_sibling(0, send3.at[other], recv3)
    pair_copy.start()
    for i, flux in enumerate((stress_u, stress_v, net_heat, freshwater)):
        flux_out[i] = flux
    pair_copy.wait_recv()
    send3y[...] = send3[mine] + recv3[...]
    send, arrive, leave3 = exchange(5, chips, chip, on_chip, lambda p: send3y, recv3y)
    send()
    recv3y[chip] = send3y[...]
    arrive()
    flux_sum = recv3y[0]
    for p in range(1, chips):
        flux_sum = flux_sum + recv3y[p]
    state = oc[mine] + (0.5 / samples) * flux_sum
    send4[...] = state

    send, arrive, leave4 = exchange(6, ring, second, on_second, lambda p: send4, recv4)
    send()
    recv4[second] = state
    ocean_out[mine] = state
    ocean_copy = to_sibling(1, ocean_out.at[mine], ocean_out.at[mine])
    ocean_copy.start()
    arrive()

    states = [recv4[:, r].reshape(ring * 8, TILE) for r in range(2)]
    slotted = mixed(spread[...], jnp.concatenate(states, axis=1))
    for p in range(ring):
        for r in range(2):
            send5[p, r] = slotted[p * slots : (p + 1) * slots, r * TILE : (r + 1) * TILE]
    send, arrive, leave5 = exchange(7, ring, first, on_first, lambda p: send5.at[p], recv5)
    send()
    recv5[first] = send5[first]
    arrive()

    states = [recv5[:, r].reshape(rows, TILE) for r in range(2)]
    entry = mixed(pick_t[...], jnp.concatenate(states, axis=1))
    high, low = split(entry)
    high, low = high.astype(F32), low.astype(F32)
    for k in range(reach):
        for j in range(PAD // 8):
            at = slice(k * PAD + j * 8, k * PAD + j * 8 + 8)
            block = [high[at, :TILE], low[at, :TILE], high[at, TILE:], low[at, TILE:]]
            lhs[j, :, k * TILE : (k + 1) * TILE] = jnp.concatenate(block, axis=0).astype(BF16)

    row8 = lax.broadcasted_iota(I32, (8, TILE), 0)

    def results(j):
        at = pl.ds(j * 8, 8)
        return to_sibling(2 + j, atm_out.at[mine, at], atm_out.at[mine, at])

    def remap(j, count):
        operand = lhs[j]
        one = two = jnp.zeros((8, TILE), F32)
        for q in range(count):
            sums = jnp.dot(operand, w[j * 8 + q].reshape(reach * TILE, TILE), preferred_element_type=F32)
            one = jnp.where(row8 == q, sums[0:8] + sums[8:16], one)
            two = jnp.where(row8 == q, sums[16:24] + sums[24:32], two)
        at = pl.ds(j * 8, 8)
        inverse = col_inverse[at]
        atm_out[2 * core, at] = one * inverse
        atm_out[2 * core + 1, at] = two * inverse
        results(j).start()

    def full_remap(j, carry):
        remap(j, 8)
        return carry

    whole, rest = tiles // 8, tiles % 8
    lax.fori_loop(0, whole, full_remap, 0)
    if rest:
        remap(whole, rest)
    blocks = whole + (rest > 0)

    def finish(j, carry):
        at = pl.ds(j * 8, 8)
        to_sibling(2 + j, atm_out.at[mine, at], atm_out.at[other, at]).wait_recv()
        results(j).wait_send()
        return carry

    lax.fori_loop(0, blocks, finish, 0)
    to_sibling(1, ocean_out.at[mine], ocean_out.at[other]).wait_recv()
    ocean_copy.wait_send()
    pair_copy.wait_send()
    to_right.wait_send()
    to_left.wait_send()
    for leave in (leave0, leave1a, leave1, leave2a, leave2, leave3, leave4, leave5):
        leave()


def shards(atm_state, owners, ocean_tile, centroid_offset, remap_weight, ocean_state):
    ring = math.isqrt(lax.axis_size("cols"))
    samples = lax.axis_size("fld")
    cells = atm_state.shape[2]
    tiles = cells // TILE
    reach = owners.shape[1]
    ocells = ocean_state.shape[1]
    otiles = ocells // TILE
    chips = samples // 2
    slots = MOST * ring
    rows = ring * slots
    entries = reach * PAD
    most = max(ring, chips)
    hbm = pl.BlockSpec(memory_space=pltpu.HBM)
    vmem = pl.BlockSpec(memory_space=pltpu.VMEM)
    fluxes, ocean, back = pl.pallas_call(
        functools.partial(kernel, ring, samples, tiles, reach, otiles),
        out_shape=(
            jax.ShapeDtypeStruct((4, 8, TILE), F32),
            jax.ShapeDtypeStruct((4, 8, TILE), F32),
            jax.ShapeDtypeStruct((4, PAD, TILE), F32),
        ),
        in_specs=[hbm] * 6,
        out_specs=(vmem, vmem, vmem),
        scratch_shapes=[
            pltpu.VMEM(atm_state.shape, BF16),
            pltpu.VMEM((reach, tiles), I32),
            pltpu.VMEM((reach, tiles), I32),
            pltpu.VMEM((tiles, reach, TILE), F32),
            pltpu.VMEM((tiles, reach, TILE, TILE), BF16),
            pltpu.VMEM((4, ocells), F32),
            pltpu.VMEM((tiles + 2, FIELDS, TILE), F32),
            pltpu.VMEM(((FIELDS + 1) * entries, TILE), F32),
            pltpu.VMEM((rows, 2 * entries), BF16),
            pltpu.VMEM((entries, 2 * rows), BF16),
            pltpu.VMEM((rows, 16 * ring), BF16),
            pltpu.VMEM((4, 8, TILE), F32),
            pltpu.VMEM((8, TILE), F32),
            pltpu.VMEM((PAD, TILE), F32),
            pltpu.VMEM((PAD // 8, 32, reach * TILE), BF16),
            pltpu.VMEM((ring, slots, TILE), F32),
            pltpu.VMEM((ring, slots, TILE), F32),
            pltpu.VMEM((ring, slots, TILE), F32),
            pltpu.VMEM((ring, slots, TILE), F32),
            pltpu.VMEM((ring, FIELDS * slots, TILE), I16),
            pltpu.VMEM((ring, FIELDS * slots, TILE), I16),
            pltpu.VMEM((ring, 8, TILE), F32),
            pltpu.VMEM((ring, 8, TILE), F32),
            pltpu.VMEM((ring, FIELDS * 8, TILE), I16),
            pltpu.VMEM((ring, FIELDS * 8, TILE), I16),
            pltpu.VMEM((4, 8, TILE), F32),
            pltpu.VMEM((2, 8, TILE), F32),
            pltpu.VMEM((2, 8, TILE), F32),
            pltpu.VMEM((chips, 2, 8, TILE), F32),
            pltpu.VMEM((2, 8, TILE), F32),
            pltpu.VMEM((ring, 2, 8, TILE), F32),
            pltpu.VMEM((ring, 2, slots, TILE), F32),
            pltpu.VMEM((ring, 2, slots, TILE), F32),
            pltpu.SemaphoreType.DMA((5,)),
            pltpu.SemaphoreType.DMA((tiles,)),
            pltpu.SemaphoreType.DMA((2,)),
            pltpu.SemaphoreType.DMA((2,)),
            pltpu.SemaphoreType.DMA((8, most)),
            pltpu.SemaphoreType.DMA((8, most)),
            pltpu.SemaphoreType.DMA((2 + PAD // 8,)),
            pltpu.SemaphoreType.DMA((2 + PAD // 8,)),
        ],
        compiler_params=pltpu.CompilerParams(
            collective_id=0, has_side_effects=True, vmem_limit_bytes=60 * 1024 * 1024
        ),
        name="coupling",
    )(atm_state, owners.T, ocean_tile.T, centroid_offset, remap_weight, ocean_state)
    sample_fluxes = fluxes[:, :otiles].reshape(1, 4, ocells)
    ocean_next = ocean[:, :otiles].reshape(4, ocells)
    return sample_fluxes, ocean_next, back[:, :tiles].reshape(4, cells)


def solution(mesh):
    return jax.shard_map(
        shards,
        mesh=mesh,
        in_specs=(
            P("fld", None, "cols"),
            P("cols", None),
            P("cols", None),
            P("cols", None, None),
            P("cols", None, None, None),
            P(None, "cols"),
        ),
        out_specs=(P("fld", None, "cols"), P(None, "cols"), P(None, "cols")),
        check_vma=False,
    )
```

```python
import functools
import math

import jax
import jax.numpy as jnp
from jax import lax
from jax.experimental import pallas as pl
from jax.experimental.pallas import tpu as pltpu
from jax.sharding import PartitionSpec as P

TILE = 128
FIELDS = 8
MOST = 3
PAD = 32
LEVELS = 5400.0
LEAST = 1e-30
MESH = pl.DeviceIdType.MESH
F32 = jnp.float32
BF16 = jnp.bfloat16
I32 = jnp.int32
I16 = jnp.int16


def split(x):
    high = x.astype(BF16)
    return high, (x - high.astype(F32)).astype(BF16)


def mixed(matrix, x):
    high, low = split(x)
    return jnp.dot(matrix, jnp.concatenate([high, low], axis=0), preferred_element_type=F32)


def twice(matrix):
    return jnp.concatenate([matrix, matrix], axis=1)


def kernel(
    ring, samples, tiles, reach, otiles,
    atm_hbm, owners_hbm, otile_hbm, cent_hbm, w_hbm, ocean_hbm,
    flux_hbm, ocean_next_hbm, back_hbm,
    flux_out, ocean_out, atm_out,
    rows_next, rows_back, atm, owners, otile, cent, w, ocean,
    val, part, pick, pick_t, spread, oc, table, col_inverse, lhs,
    send0, recv0, send1a, recv1a, send1, recv1, send2a, recv2a, send2, recv2,
    send3, recv3, send3y, recv3y, send4, recv4, send5, recv5,
    in_sem, out_sem, w_sem, halo_send, halo_recv, ssem, rsem, psend, precv,
):
    cols = ring * ring
    chips = samples // 2
    slots = MOST * ring
    rows = ring * slots
    entries = reach * PAD
    col = lax.axis_index("cols")
    fld = lax.axis_index("fld")
    x, z = col // ring, col % ring
    chip, core = fld // 2, fld % 2
    first = (1 - core) * x + core * z
    second = (1 - core) * z + core * x

    def on_first(p):
        return ((1 - core) * (p * ring + second) + core * (second * ring + p), fld)

    def on_second(p):
        return ((1 - core) * (first * ring + p) + core * (p * ring + first), fld)

    def on_chip(p):
        return (col, p * 2 + core)

    sibling = (col, chip * 2 + 1 - core)
    left, right = (col + cols - 1) % cols, (col + 1) % cols

    barrier = pltpu.get_barrier_semaphore()

    def greet(device):
        pl.semaphore_signal(barrier, inc=1, device_id=device, device_id_type=MESH)

    def far_first(count):
        return sorted(range(1, count), key=lambda d: -min(d, count - d))

    for d in far_first(ring):
        greet(on_first((first + d) % ring))
        greet(on_second((second + d) % ring))
    for d in far_first(chips):
        greet(on_chip((chip + d) % chips))
    greet((left, fld))
    greet((right, fld))
    greet(sibling)

    small = [
        pltpu.make_async_copy(source, target, in_sem.at[i])
        for i, (source, target) in enumerate(
            ((atm_hbm, atm), (owners_hbm, owners), (otile_hbm, otile), (cent_hbm, cent), (ocean_hbm, ocean))
        )
    ]
    for copy in small:
        copy.start()
    groups, rest = (tiles - 2) // 4, (tiles - 2) % 4
    spans = [(1 + 4 * c, 4) for c in range(groups)] + [(1 + 4 * groups, rest + 1), (0, 1)]

    def weights(c):
        at = pl.ds(*spans[c]) if isinstance(c, int) else pl.ds(1 + 4 * c, 4)
        return pltpu.make_async_copy(w_hbm.at[at], w.at[at], w_sem.at[c])

    for c in range(groups + 2):
        weights(c).start()

    def exchange(stage, count, me, device, source, target):
        def send():
            for d in far_first(count):
                pltpu.make_async_remote_copy(
                    src_ref=source((me + d) % count),
                    dst_ref=target.at[me],
                    send_sem=ssem.at[stage],
                    recv_sem=rsem.at[stage],
                    device_id=device((me + d) % count),
                    device_id_type=MESH,
                ).start()

        others = target.at[pl.ds(0, count - 1)]
        everything = pltpu.make_async_remote_copy(
            src_ref=others, dst_ref=others, send_sem=ssem.at[stage], recv_sem=rsem.at[stage],
            device_id=device((me + 1) % count), device_id_type=MESH,
        )
        return send, everything.wait_recv, everything.wait_send

    def to_sibling(i, source, target):
        return pltpu.make_async_remote_copy(
            src_ref=source, dst_ref=target, send_sem=psend.at[i], recv_sem=precv.at[i],
            device_id=sibling, device_id_type=MESH,
        )

    part[...] = jnp.zeros_like(part)
    col_inverse[...] = jnp.ones_like(col_inverse)
    small[0].wait()
    for t in range(tiles):
        val[t + 1] = atm[0, :, t * TILE : (t + 1) * TILE].astype(F32)
    to_right = pltpu.make_async_remote_copy(
        src_ref=val.at[tiles], dst_ref=val.at[0], send_sem=halo_send.at[0], recv_sem=halo_recv.at[0],
        device_id=(right, fld), device_id_type=MESH,
    )
    to_left = pltpu.make_async_remote_copy(
        src_ref=val.at[1], dst_ref=val.at[tiles + 1], send_sem=halo_send.at[1], recv_sem=halo_recv.at[1],
        device_id=(left, fld), device_id_type=MESH,
    )
    small[1].wait()
    small[2].wait()
    lane = lax.broadcasted_iota(I32, (FIELDS, TILE), 1)

    def across(ref, fill):
        table[...] = jnp.full((8, TILE), fill, F32)
        table[:reach, :tiles] = ref[...].astype(F32)
        line = jnp.broadcast_to(table[0:1], (8, TILE))
        for k in range(1, reach):
            shifted = pltpu.roll(jnp.broadcast_to(table[k : k + 1], (8, TILE)), k * PAD, 1)
            line = jnp.where(lane >= k * PAD, shifted, line)
        return line[:1]

    owner_across = across(owners, float(cols))
    tile_across = across(otile, 0.0)
    owner_down = jnp.broadcast_to(owner_across, (entries, entries)).T
    at_row = lax.broadcasted_iota(I32, (entries, entries), 0)
    at_lane = lax.broadcasted_iota(I32, (entries, entries), 1)
    same = owner_down == owner_across
    rank_down = jnp.sum((same & (at_lane < at_row)).astype(F32), axis=1, keepdims=True).astype(I32)
    rank_across = jnp.sum((same & (at_row < at_lane)).astype(F32), axis=0, keepdims=True).astype(I32)

    def slot(owner, rank):
        owner = owner.astype(I32)
        high = owner // ring
        low = owner - high * ring
        group = (1 - core) * high + core * low
        place = (1 - core) * low + core * high
        return jnp.where(owner < cols, group * slots + rank * ring + place, -1)

    slot_across = slot(owner_across, rank_across)
    slot_down = slot(owner_down[:, :1], rank_down)
    pick_f = (lax.broadcasted_iota(I32, (rows, entries), 0) == slot_across).astype(F32)
    pick[...] = twice(pick_f.astype(BF16))
    pick_b = (lax.broadcasted_iota(I32, (entries, rows), 1) == slot_down).astype(F32).astype(BF16)
    pick_t[...] = twice(pick_b)
    named = jnp.sum(pick_f * (tile_across + 1.0), axis=1, keepdims=True)
    named = jnp.broadcast_to(named - 1.0, (rows, TILE))
    for g in range(ring):
        send0[g] = named[g * slots : (g + 1) * slots]
    send_named, arrive0, leave0 = exchange(0, ring, first, on_first, lambda p: send0.at[p], recv0)

    small[4].wait()
    for r in range(4):
        oc[r] = jnp.zeros((8, TILE), F32)
        for t in range(otiles):
            oc[r, t : t + 1, :] = ocean[r : r + 1, t * TILE : (t + 1) * TILE]

    ones = jnp.ones((FIELDS, TILE), F32)
    small[3].wait()

    zeros = jnp.zeros((16, TILE), F32)

    def tile_sums(t):
        before, here, after = val[t], val[t + 1], val[t + 2]
        low = jnp.where(lane == 0, pltpu.roll(before, 1, 1), pltpu.roll(here, 1, 1))
        high = jnp.where(lane == TILE - 1, pltpu.roll(after, TILE - 1, 1), pltpu.roll(here, TILE - 1, 1))
        slope = 0.5 * (high - low)
        operand, operator = [], []
        for k in range(reach):
            rebuilt = jnp.concatenate([here + cent[t, k : k + 1, :] * slope, ones], axis=0)
            operand.append(jnp.concatenate([zeros, rebuilt] if k % 2 else [rebuilt, zeros], axis=1))
        for k in range(0, reach, 2):
            operator.append(jnp.concatenate([w[t, k], w[t, k + 1]], axis=1))
        product = lax.dot_general(
            jnp.concatenate(operand, axis=0).astype(BF16), jnp.concatenate(operator, axis=0),
            (((1,), (1,)), ((), ())), preferred_element_type=F32,
        )
        for k in range(reach):
            sums = product[16 * k : 16 * k + 16, k // 2 * TILE : (k // 2 + 1) * TILE]
            area = sums[FIELDS : FIELDS + 1]
            code = jnp.round(sums[:FIELDS] * (LEVELS / jnp.maximum(area, LEAST)))
            part[pl.ds(k * PAD + t, FIELDS, stride=entries), :] = code
            part[pl.ds(FIELDS * entries + k * PAD + t, 1), :] = area

    def group_sums(c, carry):
        weights(c).wait()
        for q in range(4):
            tile_sums(1 + 4 * c + q)
        return carry

    early = min(groups, 3)
    lax.fori_loop(0, early, group_sums, 0)
    pl.semaphore_wait(barrier, 3 + 2 * (ring - 1) + chips - 1)
    to_right.start()
    to_left.start()
    send_named()
    recv0[first] = send0[first]
    lax.fori_loop(early, groups, group_sums, 0)
    weights(groups).wait()
    for q in range(rest):
        tile_sums(1 + 4 * groups + q)
    weights(groups + 1).wait()
    to_right.wait_recv()
    to_left.wait_recv()
    tile_sums(0)
    tile_sums(tiles - 1)

    send, arrive1a, leave1a = exchange(1, ring, first, on_first, lambda p: send1a.at[p], recv1a)
    slotted = mixed(pick[...], part[FIELDS * entries :])
    for g in range(ring):
        send1a[g] = slotted[g * slots : (g + 1) * slots]
    send()
    send, arrive1, leave1 = exchange(2, ring, first, on_first, lambda p: send1.at[p], recv1)
    for f in range(0, FIELDS, 2):
        one = mixed(pick[...], part[f * entries : (f + 1) * entries])
        two = mixed(pick[...], part[(f + 1) * entries : (f + 2) * entries])
        for g in range(ring):
            at = slice(g * slots, (g + 1) * slots)
            pair = jnp.concatenate([one[at], two[at]], axis=0)
            send1[g, f * slots : (f + 2) * slots] = pair.astype(I32).astype(I16)
    send()
    recv1a[first] = send1a[first]
    recv1[first] = send1[first]

    arrive0()
    row = lax.broadcasted_iota(I32, (rows, TILE), 0)
    target = recv0[...].reshape(rows, TILE).astype(I32)
    member = (target >= 0) & (target + 8 * (row % ring) == lax.broadcasted_iota(I32, (rows, TILE), 1))
    member = member.astype(F32)
    gather = twice(member.T[: 8 * ring].astype(BF16))
    spread[...] = twice(member[:, : 8 * ring].astype(BF16))

    def column_area(c, carry):
        for q in range(chunk):
            t = c * chunk + q
            area = jnp.sum(w[t].reshape(reach * TILE, TILE).astype(F32), axis=0, keepdims=True)
            col_inverse[pl.ds(t, 1), :] = 1.0 / area
        return carry

    chunk = 4 if tiles % 4 == 0 else 1
    lax.fori_loop(0, tiles // chunk, column_area, 0)

    send, arrive2a, leave2a = exchange(3, ring, second, on_second, lambda p: send2a.at[p], recv2a)
    arrive1a()
    areas = recv1a[...].reshape(rows, TILE)
    dense_area = mixed(gather, areas)
    send2a[...] = dense_area.reshape(ring, 8, TILE)
    send()
    per_area = 1.0 / jnp.maximum(dense_area, LEAST)
    send, arrive2, leave2 = exchange(4, ring, second, on_second, lambda p: send2.at[p], recv2)
    arrive1()
    for f in range(0, FIELDS, 2):
        pair = recv1[:, f * slots : (f + 2) * slots].astype(I32).astype(F32)
        one = mixed(gather, pair[:, :slots].reshape(rows, TILE) * areas) * per_area
        two = mixed(gather, pair[:, slots:].reshape(rows, TILE) * areas) * per_area
        both = jnp.concatenate([one.reshape(ring, 8, TILE), two.reshape(ring, 8, TILE)], axis=1)
        send2[:, f * 8 : (f + 2) * 8] = jnp.round(both).astype(I32).astype(I16)
    send()
    recv2a[second] = send2a[second]
    recv2[second] = send2[second]
    arrive2a()
    arrive2()

    coverage = jnp.zeros((8, TILE), F32)
    total = jnp.zeros((FIELDS, 8, TILE), F32)
    for p in range(ring):
        area = recv2a[p]
        coverage = coverage + area
        total = total + recv2[p].astype(I32).astype(F32).reshape(FIELDS, 8, TILE) * area[None]
    forcing = total * (1.0 / (LEVELS * jnp.maximum(coverage, 1.0)))[None]

    sst, uo, vo = oc[0], oc[1], oc[2]
    slip_u = forcing[0] - uo
    slip_v = forcing[1] - vo
    wind_speed = jnp.sqrt(slip_u * slip_u + slip_v * slip_v + 0.25)
    saturation = 0.9 * jnp.exp(0.07 * sst - 0.1 * forcing[4])
    sensible = 0.4 * wind_speed * (sst - forcing[2])
    latent = 0.4 * wind_speed * (saturation - forcing[3])

    def softplus(v):
        return jnp.maximum(v, 0.0) + jnp.log1p(jnp.exp(-jnp.abs(v)))

    insolation = 0.5 + 1.5 * fld.astype(F32) / (samples - 1)
    net_heat = insolation * softplus(forcing[5]) + 0.3 * forcing[6] - 0.1 * sst - sensible - latent
    freshwater = softplus(forcing[7]) - latent
    stress_u = 0.5 * wind_speed * slip_u
    stress_v = 0.5 * wind_speed * slip_v
    send3[0] = net_heat
    send3[1] = stress_u
    send3[2] = stress_v
    send3[3] = -freshwater

    mine, other = pl.ds(2 * core, 2), pl.ds(2 - 2 * core, 2)
    pair_copy = to_sibling(0, send3.at[other], recv3)
    pair_copy.start()
    pair_copy.wait_recv()
    send3y[...] = send3[mine] + recv3[...]
    send, arrive, leave3 = exchange(5, chips, chip, on_chip, lambda p: send3y, recv3y)
    send()
    recv3y[chip] = send3y[...]
    for i, flux in enumerate((stress_u, stress_v, net_heat, freshwater)):
        for t in range(otiles):
            flux_out[0, i : i + 1, t * TILE : (t + 1) * TILE] = flux[t : t + 1]
    flux_copy = pltpu.make_async_copy(flux_out, flux_hbm, out_sem.at[0])
    flux_copy.start()
    for leave in (leave0, leave1a, leave1, leave2a, leave2, to_right.wait_send, to_left.wait_send):
        leave()
    pair_copy.wait_send()
    arrive()
    flux_sum = recv3y[0]
    for p in range(1, chips):
        flux_sum = flux_sum + recv3y[p]
    state = oc[mine] + (0.5 / samples) * flux_sum
    send4[...] = state

    send, arrive, leave4 = exchange(6, ring, second, on_second, lambda p: send4, recv4)
    send()
    recv4[second] = state
    rows_next[mine] = state
    ocean_copy = to_sibling(1, rows_next.at[mine], rows_next.at[mine])
    ocean_copy.start()
    leave3()
    arrive()

    states = [recv4[:, r].reshape(ring * 8, TILE) for r in range(2)]
    slotted = mixed(spread[...], jnp.concatenate(states, axis=1))
    for p in range(ring):
        for r in range(2):
            send5[p, r] = slotted[p * slots : (p + 1) * slots, r * TILE : (r + 1) * TILE]
    send, arrive, leave5 = exchange(7, ring, first, on_first, lambda p: send5.at[p], recv5)
    send()
    recv5[first] = send5[first]
    to_sibling(1, rows_next.at[mine], rows_next.at[other]).wait_recv()
    for r in range(4):
        for t in range(otiles):
            ocean_out[r : r + 1, t * TILE : (t + 1) * TILE] = rows_next[r, t : t + 1]
    next_copy = pltpu.make_async_copy(ocean_out, ocean_next_hbm, out_sem.at[1])
    next_copy.start()
    ocean_copy.wait_send()
    leave4()
    flux_copy.wait()
    arrive()

    states = [recv5[:, r].reshape(rows, TILE) for r in range(2)]
    entry = mixed(pick_t[...], jnp.concatenate(states, axis=1))
    high, low = split(entry)
    high, low = high.astype(F32), low.astype(F32)
    for k in range(reach):
        for j in range(PAD // 8):
            at = slice(k * PAD + j * 8, k * PAD + j * 8 + 8)
            block = [high[at, :TILE], low[at, :TILE], high[at, TILE:], low[at, TILE:]]
            lhs[j, :, k * TILE : (k + 1) * TILE] = jnp.concatenate(block, axis=0).astype(BF16)

    row8 = lax.broadcasted_iota(I32, (8, TILE), 0)

    def results(j):
        at = pl.ds(j * 8, 8)
        return to_sibling(2 + j, rows_back.at[mine, at], rows_back.at[mine, at])

    def remap(j, count):
        operand = lhs[j]
        one = two = jnp.zeros((8, TILE), F32)
        for q in range(count):
            sums = jnp.dot(operand, w[j * 8 + q].reshape(reach * TILE, TILE), preferred_element_type=F32)
            one = jnp.where(row8 == q, sums[0:8] + sums[8:16], one)
            two = jnp.where(row8 == q, sums[16:24] + sums[24:32], two)
        at = pl.ds(j * 8, 8)
        inverse = col_inverse[at]
        rows_back[2 * core, at] = one * inverse
        rows_back[2 * core + 1, at] = two * inverse
        results(j).start()

    def full_remap(j, carry):
        remap(j, 8)
        return carry

    whole, last = tiles // 8, tiles % 8
    lax.fori_loop(0, whole, full_remap, 0)
    if last:
        remap(whole, last)
    leave5()
    next_copy.wait()
    for j in range(whole + (last > 0)):
        at = pl.ds(j * 8, 8)
        to_sibling(2 + j, rows_back.at[mine, at], rows_back.at[other, at]).wait_recv()
        for r in range(4):
            for t in range(8 * j, min(8 * j + 8, tiles)):
                atm_out[r : r + 1, t * TILE : (t + 1) * TILE] = rows_back[r, t : t + 1]
    back_copy = pltpu.make_async_copy(atm_out, back_hbm, out_sem.at[2])
    back_copy.start()
    for j in range(whole + (last > 0)):
        results(j).wait_send()
    back_copy.wait()


def write_out(*refs):
    sources, targets, sems = refs[:3], refs[3:6], refs[6]
    copies = [pltpu.make_async_copy(s, t, sems.at[i]) for i, (s, t) in enumerate(zip(sources, targets))]
    for copy in copies:
        copy.start()
    for copy in copies:
        copy.wait()


def shards(atm_state, owners, ocean_tile, centroid_offset, remap_weight, ocean_state):
    ring = math.isqrt(lax.axis_size("cols"))
    samples = lax.axis_size("fld")
    cells = atm_state.shape[2]
    tiles = cells // TILE
    reach = owners.shape[1]
    ocells = ocean_state.shape[1]
    otiles = ocells // TILE
    chips = samples // 2
    slots = MOST * ring
    rows = ring * slots
    entries = reach * PAD
    hbm = pl.BlockSpec(memory_space=pltpu.HBM)
    out_shape = (
        jax.ShapeDtypeStruct((1, 4, ocells), F32),
        jax.ShapeDtypeStruct((4, ocells), F32),
        jax.ShapeDtypeStruct((4, cells), F32),
    )
    results = pl.pallas_call(
        functools.partial(kernel, ring, samples, tiles, reach, otiles),
        out_shape=out_shape,
        in_specs=[hbm] * 6,
        out_specs=(hbm, hbm, hbm),
        scratch_shapes=[
            pltpu.VMEM((1, 4, ocells), F32),
            pltpu.VMEM((4, ocells), F32),
            pltpu.VMEM((4, cells), F32),
            pltpu.VMEM((4, 8, TILE), F32),
            pltpu.VMEM((4, PAD, TILE), F32),
            pltpu.VMEM(atm_state.shape, BF16),
            pltpu.VMEM((reach, tiles), I32),
            pltpu.VMEM((reach, tiles), I32),
            pltpu.VMEM((tiles, reach, TILE), F32),
            pltpu.VMEM((tiles, reach, TILE, TILE), BF16),
            pltpu.VMEM((4, ocells), F32),
            pltpu.VMEM((tiles + 2, FIELDS, TILE), F32),
            pltpu.VMEM(((FIELDS + 1) * entries, TILE), F32),
            pltpu.VMEM((rows, 2 * entries), BF16),
            pltpu.VMEM((entries, 2 * rows), BF16),
            pltpu.VMEM((rows, 16 * ring), BF16),
            pltpu.VMEM((4, 8, TILE), F32),
            pltpu.VMEM((8, TILE), F32),
            pltpu.VMEM((PAD, TILE), F32),
            pltpu.VMEM((PAD // 8, 32, reach * TILE), BF16),
            pltpu.VMEM((ring, slots, TILE), F32),
            pltpu.VMEM((ring, slots, TILE), F32),
            pltpu.VMEM((ring, slots, TILE), F32),
            pltpu.VMEM((ring, slots, TILE), F32),
            pltpu.VMEM((ring, FIELDS * slots, TILE), I16),
            pltpu.VMEM((ring, FIELDS * slots, TILE), I16),
            pltpu.VMEM((ring, 8, TILE), F32),
            pltpu.VMEM((ring, 8, TILE), F32),
            pltpu.VMEM((ring, FIELDS * 8, TILE), I16),
            pltpu.VMEM((ring, FIELDS * 8, TILE), I16),
            pltpu.VMEM((4, 8, TILE), F32),
            pltpu.VMEM((2, 8, TILE), F32),
            pltpu.VMEM((2, 8, TILE), F32),
            pltpu.VMEM((chips, 2, 8, TILE), F32),
            pltpu.VMEM((2, 8, TILE), F32),
            pltpu.VMEM((ring, 2, 8, TILE), F32),
            pltpu.VMEM((ring, 2, slots, TILE), F32),
            pltpu.VMEM((ring, 2, slots, TILE), F32),
            pltpu.SemaphoreType.DMA((5,)),
            pltpu.SemaphoreType.DMA((3,)),
            pltpu.SemaphoreType.DMA((tiles,)),
            pltpu.SemaphoreType.DMA((2,)),
            pltpu.SemaphoreType.DMA((2,)),
            pltpu.SemaphoreType.DMA((8,)),
            pltpu.SemaphoreType.DMA((8,)),
            pltpu.SemaphoreType.DMA((2 + PAD // 8,)),
            pltpu.SemaphoreType.DMA((2 + PAD // 8,)),
        ],
        compiler_params=pltpu.CompilerParams(
            collective_id=0, has_side_effects=True, vmem_limit_bytes=60 * 1024 * 1024
        ),
        name="coupling",
    )(atm_state, owners.T, ocean_tile.T, centroid_offset, remap_weight, ocean_state)
    return pl.pallas_call(
        write_out,
        out_shape=out_shape,
        in_specs=[hbm] * 3,
        out_specs=(hbm, hbm, hbm),
        scratch_shapes=[pltpu.SemaphoreType.DMA((3,))],
        compiler_params=pltpu.CompilerParams(vmem_limit_bytes=60 * 1024 * 1024),
        name="write_out",
    )(*results)


def solution(mesh):
    return jax.shard_map(
        shards,
        mesh=mesh,
        in_specs=(
            P("fld", None, "cols"),
            P("cols", None),
            P("cols", None),
            P("cols", None, None),
            P("cols", None, None, None),
            P(None, "cols"),
        ),
        out_specs=(P("fld", None, "cols"), P(None, "cols"), P(None, "cols")),
        check_vma=False,
    )
```

```python
import functools
import math

import jax
import jax.numpy as jnp
from jax import lax
from jax.experimental import pallas as pl
from jax.experimental.pallas import tpu as pltpu
from jax.sharding import PartitionSpec as P

TILE = 128
FIELDS = 8
MOST = 3
PAD = 32
LEVELS = 5400.0
LEAST = 1e-30
PAIRS = (4, 6, 0, 2)
MESH = pl.DeviceIdType.MESH
F32 = jnp.float32
BF16 = jnp.bfloat16
I32 = jnp.int32
I16 = jnp.int16


def split(x):
    high = x.astype(BF16)
    return high, (x - high.astype(F32)).astype(BF16)


def mixed(matrix, x):
    high, low = split(x)
    return jnp.dot(matrix, jnp.concatenate([high, low], axis=0), preferred_element_type=F32)


def twice(matrix):
    return jnp.concatenate([matrix, matrix], axis=1)


def kernel(
    ring, samples, tiles, reach, otiles,
    atm_hbm, owners_hbm, otile_hbm, cent_hbm, w_hbm, ocean_hbm,
    flux_out, ocean_out, atm_out,
    rows_next, rows_back, atm, owners, otile, cent, w, ocean,
    val, part, pick, pick_t, spread, oc, table, col_inverse, lhs,
    send0, recv0, send1a, recv1a, send1, recv1, send2a, recv2a, send2, recv2,
    send3, recv3, send3y, recv3y, send4, recv4, send5, recv5,
    in_sem, w_sem, halo_send, halo_recv, ssem, rsem, psend, precv,
):
    cols = ring * ring
    chips = samples // 2
    slots = MOST * ring
    rows = ring * slots
    entries = reach * PAD
    col = lax.axis_index("cols")
    fld = lax.axis_index("fld")
    x, z = col // ring, col % ring
    chip, core = fld // 2, fld % 2
    first = (1 - core) * x + core * z
    second = (1 - core) * z + core * x

    def on_first(p):
        return ((1 - core) * (p * ring + second) + core * (second * ring + p), fld)

    def on_second(p):
        return ((1 - core) * (first * ring + p) + core * (p * ring + first), fld)

    def on_chip(p):
        return (col, p * 2 + core)

    sibling = (col, chip * 2 + 1 - core)
    left, right = (col + cols - 1) % cols, (col + 1) % cols

    barrier = pltpu.get_barrier_semaphore()

    def greet(device):
        pl.semaphore_signal(barrier, inc=1, device_id=device, device_id_type=MESH)

    def far_first(count):
        return sorted(range(1, count), key=lambda d: -min(d, count - d))

    for d in far_first(ring):
        greet(on_first((first + d) % ring))
        greet(on_second((second + d) % ring))
    for d in far_first(chips):
        greet(on_chip((chip + d) % chips))
    greet((left, fld))
    greet((right, fld))
    greet(sibling)

    small = [
        pltpu.make_async_copy(source, target, in_sem.at[i])
        for i, (source, target) in enumerate(
            ((atm_hbm, atm), (owners_hbm, owners), (otile_hbm, otile), (cent_hbm, cent), (ocean_hbm, ocean))
        )
    ]
    for copy in small:
        copy.start()
    groups, rest = (tiles - 2) // 4, (tiles - 2) % 4
    spans = [(1 + 4 * c, 4) for c in range(groups)] + [(1 + 4 * groups, rest + 1), (0, 1)]

    def weights(c):
        at = pl.ds(*spans[c]) if isinstance(c, int) else pl.ds(1 + 4 * c, 4)
        return pltpu.make_async_copy(w_hbm.at[at], w.at[at], w_sem.at[c])

    for c in range(groups + 2):
        weights(c).start()

    def exchange(stage, count, me, device, source, target):
        def send():
            for d in far_first(count):
                pltpu.make_async_remote_copy(
                    src_ref=source((me + d) % count),
                    dst_ref=target.at[me],
                    send_sem=ssem.at[stage],
                    recv_sem=rsem.at[stage],
                    device_id=device((me + d) % count),
                    device_id_type=MESH,
                ).start()

        others = target.at[pl.ds(0, count - 1)]
        everything = pltpu.make_async_remote_copy(
            src_ref=others, dst_ref=others, send_sem=ssem.at[stage], recv_sem=rsem.at[stage],
            device_id=device((me + 1) % count), device_id_type=MESH,
        )
        return send, everything.wait_recv, everything.wait_send

    def to_sibling(i, source, target):
        return pltpu.make_async_remote_copy(
            src_ref=source, dst_ref=target, send_sem=psend.at[i], recv_sem=precv.at[i],
            device_id=sibling, device_id_type=MESH,
        )

    part[...] = jnp.zeros_like(part)
    col_inverse[...] = jnp.ones_like(col_inverse)
    small[0].wait()
    for t in range(tiles):
        val[t + 1] = atm[0, :, t * TILE : (t + 1) * TILE].astype(F32)
    to_right = pltpu.make_async_remote_copy(
        src_ref=val.at[tiles], dst_ref=val.at[0], send_sem=halo_send.at[0], recv_sem=halo_recv.at[0],
        device_id=(right, fld), device_id_type=MESH,
    )
    to_left = pltpu.make_async_remote_copy(
        src_ref=val.at[1], dst_ref=val.at[tiles + 1], send_sem=halo_send.at[1], recv_sem=halo_recv.at[1],
        device_id=(left, fld), device_id_type=MESH,
    )
    small[1].wait()
    small[2].wait()
    lane = lax.broadcasted_iota(I32, (FIELDS, TILE), 1)

    def across(ref, fill):
        table[...] = jnp.full((8, TILE), fill, F32)
        table[:reach, :tiles] = ref[...].astype(F32)
        line = jnp.broadcast_to(table[0:1], (8, TILE))
        for k in range(1, reach):
            shifted = pltpu.roll(jnp.broadcast_to(table[k : k + 1], (8, TILE)), k * PAD, 1)
            line = jnp.where(lane >= k * PAD, shifted, line)
        return line[:1]

    owner_across = across(owners, float(cols))
    tile_across = across(otile, 0.0)
    owner_down = jnp.broadcast_to(owner_across, (entries, entries)).T
    at_row = lax.broadcasted_iota(I32, (entries, entries), 0)
    at_lane = lax.broadcasted_iota(I32, (entries, entries), 1)
    same = owner_down == owner_across
    rank_down = jnp.sum((same & (at_lane < at_row)).astype(F32), axis=1, keepdims=True).astype(I32)
    rank_across = jnp.sum((same & (at_row < at_lane)).astype(F32), axis=0, keepdims=True).astype(I32)

    def slot(owner, rank):
        owner = owner.astype(I32)
        high = owner // ring
        low = owner - high * ring
        group = (1 - core) * high + core * low
        place = (1 - core) * low + core * high
        return jnp.where(owner < cols, group * slots + rank * ring + place, -1)

    slot_across = slot(owner_across, rank_across)
    slot_down = slot(owner_down[:, :1], rank_down)
    pick_f = (lax.broadcasted_iota(I32, (rows, entries), 0) == slot_across).astype(F32)
    pick[...] = twice(pick_f.astype(BF16))
    pick_b = (lax.broadcasted_iota(I32, (entries, rows), 1) == slot_down).astype(F32).astype(BF16)
    pick_t[...] = twice(pick_b)
    named = jnp.sum(pick_f * (tile_across + 1.0), axis=1, keepdims=True)
    named = jnp.broadcast_to(named - 1.0, (rows, TILE))
    for g in range(ring):
        send0[g] = named[g * slots : (g + 1) * slots]
    send_named, arrive0, leave0 = exchange(0, ring, first, on_first, lambda p: send0.at[p], recv0)

    small[4].wait()
    for r in range(4):
        oc[r] = jnp.zeros((8, TILE), F32)
        for t in range(otiles):
            oc[r, t : t + 1, :] = ocean[r : r + 1, t * TILE : (t + 1) * TILE]

    ones = jnp.ones((FIELDS, TILE), F32)
    small[3].wait()

    zeros = jnp.zeros((16, TILE), F32)

    def tile_sums(t):
        before, here, after = val[t], val[t + 1], val[t + 2]
        low = jnp.where(lane == 0, pltpu.roll(before, 1, 1), pltpu.roll(here, 1, 1))
        high = jnp.where(lane == TILE - 1, pltpu.roll(after, TILE - 1, 1), pltpu.roll(here, TILE - 1, 1))
        slope = 0.5 * (high - low)
        operand, operator = [], []
        for k in range(reach):
            rebuilt = jnp.concatenate([here + cent[t, k : k + 1, :] * slope, ones], axis=0)
            operand.append(jnp.concatenate([zeros, rebuilt] if k % 2 else [rebuilt, zeros], axis=1))
        for k in range(0, reach, 2):
            operator.append(jnp.concatenate([w[t, k], w[t, k + 1]], axis=1))
        product = lax.dot_general(
            jnp.concatenate(operand, axis=0).astype(BF16), jnp.concatenate(operator, axis=0),
            (((1,), (1,)), ((), ())), preferred_element_type=F32,
        )
        for k in range(reach):
            sums = product[16 * k : 16 * k + 16, k // 2 * TILE : (k // 2 + 1) * TILE]
            area = sums[FIELDS : FIELDS + 1]
            code = jnp.round(sums[:FIELDS] * (LEVELS / jnp.maximum(area, LEAST)))
            part[pl.ds(k * PAD + t, FIELDS, stride=entries), :] = code
            part[pl.ds(FIELDS * entries + k * PAD + t, 1), :] = area

    def group_sums(c, carry):
        weights(c).wait()
        for q in range(4):
            tile_sums(1 + 4 * c + q)
        return carry

    early = min(groups, 3)
    lax.fori_loop(0, early, group_sums, 0)
    pl.semaphore_wait(barrier, 3 + 2 * (ring - 1) + chips - 1)
    to_right.start()
    to_left.start()
    send_named()
    recv0[first] = send0[first]
    lax.fori_loop(early, groups, group_sums, 0)
    weights(groups).wait()
    for q in range(rest):
        tile_sums(1 + 4 * groups + q)
    weights(groups + 1).wait()
    to_right.wait_recv()
    to_left.wait_recv()
    tile_sums(0)
    tile_sums(tiles - 1)

    send, arrive1a, leave1a = exchange(1, ring, first, on_first, lambda p: send1a.at[p], recv1a)
    slotted = mixed(pick[...], part[FIELDS * entries :])
    for g in range(ring):
        send1a[g] = slotted[g * slots : (g + 1) * slots]
    send()
    recv1a[first] = send1a[first]
    sent1 = []
    for m, f in enumerate(PAIRS):
        one = mixed(pick[...], part[f * entries : (f + 1) * entries])
        two = mixed(pick[...], part[(f + 1) * entries : (f + 2) * entries])
        for g in range(ring):
            at = slice(g * slots, (g + 1) * slots)
            pair = jnp.concatenate([one[at], two[at]], axis=0)
            send1[m, g] = pair.astype(I32).astype(I16)
        send, *ends = exchange(2 + m, ring, first, on_first, lambda p: send1.at[m, p], recv1.at[m])
        send()
        sent1.append(ends)
        recv1[m, first] = send1[m, first]

    arrive0()
    row = lax.broadcasted_iota(I32, (rows, TILE), 0)
    target = recv0[...].reshape(rows, TILE).astype(I32)
    member = (target >= 0) & (target + 8 * (row % ring) == lax.broadcasted_iota(I32, (rows, TILE), 1))
    member = member.astype(F32)
    gather = twice(member.T[: 8 * ring].astype(BF16))
    spread[...] = twice(member[:, : 8 * ring].astype(BF16))

    def column_area(c, carry):
        for q in range(chunk):
            t = c * chunk + q
            area = jnp.sum(w[t].reshape(reach * TILE, TILE).astype(F32), axis=0, keepdims=True)
            col_inverse[pl.ds(t, 1), :] = 1.0 / area
        return carry

    chunk = 4 if tiles % 4 == 0 else 1
    lax.fori_loop(0, tiles // chunk, column_area, 0)

    send, arrive2a, leave2a = exchange(6, ring, second, on_second, lambda p: send2a.at[p], recv2a)
    arrive1a()
    areas = recv1a[...].reshape(rows, TILE)
    dense_area = mixed(gather, areas)
    send2a[...] = dense_area.reshape(ring, 8, TILE)
    send()
    recv2a[second] = send2a[second]
    per_area = 1.0 / jnp.maximum(dense_area, LEAST)
    sent2 = []
    for m in range(len(PAIRS)):
        arrive, _ = sent1[m]
        arrive()
        pair = recv1[m].astype(I32).astype(F32)
        one = mixed(gather, pair[:, :slots].reshape(rows, TILE) * areas) * per_area
        two = mixed(gather, pair[:, slots:].reshape(rows, TILE) * areas) * per_area
        both = jnp.concatenate([one.reshape(ring, 8, TILE), two.reshape(ring, 8, TILE)], axis=1)
        send2[m] = jnp.round(both).astype(I32).astype(I16)
        send, *ends = exchange(7 + m, ring, second, on_second, lambda p: send2.at[m, p], recv2.at[m])
        send()
        sent2.append(ends)
        recv2[m, second] = send2[m, second]

    arrive2a()
    coverage = jnp.zeros((8, TILE), F32)
    for p in range(ring):
        coverage = coverage + recv2a[p]
    per_coverage = 1.0 / (LEVELS * jnp.maximum(coverage, 1.0))
    forcing = [None] * FIELDS
    for m, f in enumerate(PAIRS):
        arrive, _ = sent2[m]
        arrive()
        one = two = jnp.zeros((8, TILE), F32)
        for p in range(ring):
            pair = recv2[m, p].astype(I32).astype(F32)
            one = one + pair[:8] * recv2a[p]
            two = two + pair[8:] * recv2a[p]
        forcing[f] = one * per_coverage
        forcing[f + 1] = two * per_coverage

    sst, uo, vo = oc[0], oc[1], oc[2]
    slip_u = forcing[0] - uo
    slip_v = forcing[1] - vo
    wind_speed = jnp.sqrt(slip_u * slip_u + slip_v * slip_v + 0.25)
    saturation = 0.9 * jnp.exp(0.07 * sst - 0.1 * forcing[4])
    sensible = 0.4 * wind_speed * (sst - forcing[2])
    latent = 0.4 * wind_speed * (saturation - forcing[3])

    def softplus(v):
        return jnp.maximum(v, 0.0) + jnp.log1p(jnp.exp(-jnp.abs(v)))

    insolation = 0.5 + 1.5 * fld.astype(F32) / (samples - 1)
    net_heat = insolation * softplus(forcing[5]) + 0.3 * forcing[6] - 0.1 * sst - sensible - latent
    freshwater = softplus(forcing[7]) - latent
    stress_u = 0.5 * wind_speed * slip_u
    stress_v = 0.5 * wind_speed * slip_v
    send3[0] = net_heat
    send3[1] = stress_u
    send3[2] = stress_v
    send3[3] = -freshwater

    mine, other = pl.ds(2 * core, 2), pl.ds(2 - 2 * core, 2)
    pair_copy = to_sibling(0, send3.at[other], recv3)
    pair_copy.start()
    pair_copy.wait_recv()
    send3y[...] = send3[mine] + recv3[...]
    send, arrive, leave3 = exchange(11, chips, chip, on_chip, lambda p: send3y, recv3y)
    send()
    recv3y[chip] = send3y[...]
    for i, flux in enumerate((stress_u, stress_v, net_heat, freshwater)):
        for t in range(otiles):
            flux_out[0, i : i + 1, t * TILE : (t + 1) * TILE] = flux[t : t + 1]
    for leave in (leave0, leave1a, leave2a, to_right.wait_send, to_left.wait_send):
        leave()
    for _, leave in sent1 + sent2:
        leave()
    pair_copy.wait_send()
    arrive()
    flux_sum = recv3y[0]
    for p in range(1, chips):
        flux_sum = flux_sum + recv3y[p]
    state = oc[mine] + (0.5 / samples) * flux_sum
    send4[...] = state

    send, arrive, leave4 = exchange(12, ring, second, on_second, lambda p: send4, recv4)
    send()
    recv4[second] = state
    rows_next[mine] = state
    ocean_copy = to_sibling(1, rows_next.at[mine], rows_next.at[mine])
    ocean_copy.start()
    leave3()
    arrive()

    states = [recv4[:, r].reshape(ring * 8, TILE) for r in range(2)]
    slotted = mixed(spread[...], jnp.concatenate(states, axis=1))
    for p in range(ring):
        for r in range(2):
            send5[p, r] = slotted[p * slots : (p + 1) * slots, r * TILE : (r + 1) * TILE]
    send, arrive, leave5 = exchange(13, ring, first, on_first, lambda p: send5.at[p], recv5)
    send()
    recv5[first] = send5[first]
    to_sibling(1, rows_next.at[mine], rows_next.at[other]).wait_recv()
    for r in range(4):
        for t in range(otiles):
            ocean_out[r : r + 1, t * TILE : (t + 1) * TILE] = rows_next[r, t : t + 1]
    ocean_copy.wait_send()
    leave4()
    arrive()

    states = [recv5[:, r].reshape(rows, TILE) for r in range(2)]
    entry = mixed(pick_t[...], jnp.concatenate(states, axis=1))
    high, low = split(entry)
    high, low = high.astype(F32), low.astype(F32)
    for k in range(reach):
        for j in range(PAD // 8):
            at = slice(k * PAD + j * 8, k * PAD + j * 8 + 8)
            block = [high[at, :TILE], low[at, :TILE], high[at, TILE:], low[at, TILE:]]
            lhs[j, :, k * TILE : (k + 1) * TILE] = jnp.concatenate(block, axis=0).astype(BF16)

    row8 = lax.broadcasted_iota(I32, (8, TILE), 0)

    def results(j):
        at = pl.ds(j * 8, 8)
        return to_sibling(2 + j, rows_back.at[mine, at], rows_back.at[mine, at])

    def remap(j, count):
        operand = lhs[j]
        one = two = jnp.zeros((8, TILE), F32)
        for q in range(count):
            sums = jnp.dot(operand, w[j * 8 + q].reshape(reach * TILE, TILE), preferred_element_type=F32)
            one = jnp.where(row8 == q, sums[0:8] + sums[8:16], one)
            two = jnp.where(row8 == q, sums[16:24] + sums[24:32], two)
        at = pl.ds(j * 8, 8)
        inverse = col_inverse[at]
        rows_back[2 * core, at] = one * inverse
        rows_back[2 * core + 1, at] = two * inverse
        results(j).start()

    def full_remap(j, carry):
        remap(j, 8)
        return carry

    whole, last = tiles // 8, tiles % 8
    lax.fori_loop(0, whole, full_remap, 0)
    if last:
        remap(whole, last)
    leave5()
    for j in range(whole + (last > 0)):
        at = pl.ds(j * 8, 8)
        to_sibling(2 + j, rows_back.at[mine, at], rows_back.at[other, at]).wait_recv()
        for r in range(4):
            for t in range(8 * j, min(8 * j + 8, tiles)):
                atm_out[r : r + 1, t * TILE : (t + 1) * TILE] = rows_back[r, t : t + 1]
    for j in range(whole + (last > 0)):
        results(j).wait_send()


def shards(atm_state, owners, ocean_tile, centroid_offset, remap_weight, ocean_state):
    ring = math.isqrt(lax.axis_size("cols"))
    samples = lax.axis_size("fld")
    cells = atm_state.shape[2]
    tiles = cells // TILE
    reach = owners.shape[1]
    ocells = ocean_state.shape[1]
    otiles = ocells // TILE
    chips = samples // 2
    slots = MOST * ring
    rows = ring * slots
    entries = reach * PAD
    hbm = pl.BlockSpec(memory_space=pltpu.HBM)
    vmem = pl.BlockSpec(memory_space=pltpu.VMEM)
    out_shape = (
        jax.ShapeDtypeStruct((1, 4, ocells), F32),
        jax.ShapeDtypeStruct((4, ocells), F32),
        jax.ShapeDtypeStruct((4, cells), F32),
    )
    results = pl.pallas_call(
        functools.partial(kernel, ring, samples, tiles, reach, otiles),
        out_shape=tuple(pltpu.VMEM(s.shape, s.dtype) for s in out_shape),
        in_specs=[hbm] * 6,
        out_specs=(vmem, vmem, vmem),
        scratch_shapes=[
            pltpu.VMEM((4, 8, TILE), F32),
            pltpu.VMEM((4, PAD, TILE), F32),
            pltpu.VMEM(atm_state.shape, BF16),
            pltpu.VMEM((reach, tiles), I32),
            pltpu.VMEM((reach, tiles), I32),
            pltpu.VMEM((tiles, reach, TILE), F32),
            pltpu.VMEM((tiles, reach, TILE, TILE), BF16),
            pltpu.VMEM((4, ocells), F32),
            pltpu.VMEM((tiles + 2, FIELDS, TILE), F32),
            pltpu.VMEM(((FIELDS + 1) * entries, TILE), F32),
            pltpu.VMEM((rows, 2 * entries), BF16),
            pltpu.VMEM((entries, 2 * rows), BF16),
            pltpu.VMEM((rows, 16 * ring), BF16),
            pltpu.VMEM((4, 8, TILE), F32),
            pltpu.VMEM((8, TILE), F32),
            pltpu.VMEM((PAD, TILE), F32),
            pltpu.VMEM((PAD // 8, 32, reach * TILE), BF16),
            pltpu.VMEM((ring, slots, TILE), F32),
            pltpu.VMEM((ring, slots, TILE), F32),
            pltpu.VMEM((ring, slots, TILE), F32),
            pltpu.VMEM((ring, slots, TILE), F32),
            pltpu.VMEM((len(PAIRS), ring, 2 * slots, TILE), I16),
            pltpu.VMEM((len(PAIRS), ring, 2 * slots, TILE), I16),
            pltpu.VMEM((ring, 8, TILE), F32),
            pltpu.VMEM((ring, 8, TILE), F32),
            pltpu.VMEM((len(PAIRS), ring, 16, TILE), I16),
            pltpu.VMEM((len(PAIRS), ring, 16, TILE), I16),
            pltpu.VMEM((4, 8, TILE), F32),
            pltpu.VMEM((2, 8, TILE), F32),
            pltpu.VMEM((2, 8, TILE), F32),
            pltpu.VMEM((chips, 2, 8, TILE), F32),
            pltpu.VMEM((2, 8, TILE), F32),
            pltpu.VMEM((ring, 2, 8, TILE), F32),
            pltpu.VMEM((ring, 2, slots, TILE), F32),
            pltpu.VMEM((ring, 2, slots, TILE), F32),
            pltpu.SemaphoreType.DMA((5,)),
            pltpu.SemaphoreType.DMA((tiles,)),
            pltpu.SemaphoreType.DMA((2,)),
            pltpu.SemaphoreType.DMA((2,)),
            pltpu.SemaphoreType.DMA((14,)),
            pltpu.SemaphoreType.DMA((14,)),
            pltpu.SemaphoreType.DMA((2 + PAD // 8,)),
            pltpu.SemaphoreType.DMA((2 + PAD // 8,)),
        ],
        compiler_params=pltpu.CompilerParams(
            collective_id=0, has_side_effects=True, vmem_limit_bytes=60 * 1024 * 1024
        ),
        name="coupling",
    )(atm_state, owners.T, ocean_tile.T, centroid_offset, remap_weight, ocean_state)
    return results


def solution(mesh):
    return jax.shard_map(
        shards,
        mesh=mesh,
        in_specs=(
            P("fld", None, "cols"),
            P("cols", None),
            P("cols", None),
            P("cols", None, None),
            P("cols", None, None, None),
            P(None, "cols"),
        ),
        out_specs=(P("fld", None, "cols"), P(None, "cols"), P(None, "cols")),
        check_vma=False,
    )
```

```python
import functools
import math

import jax
import jax.numpy as jnp
from jax import lax
from jax.experimental import pallas as pl
from jax.experimental.pallas import tpu as pltpu
from jax.sharding import PartitionSpec as P

TILE = 128
FIELDS = 8
MOST = 3
PAD = 32
LEVELS = 5400.0
LEAST = 1e-30
MESH = pl.DeviceIdType.MESH
F32 = jnp.float32
BF16 = jnp.bfloat16
I32 = jnp.int32
I16 = jnp.int16


def split(x):
    high = x.astype(BF16)
    return high, (x - high.astype(F32)).astype(BF16)


def mixed(matrix, x):
    high, low = split(x)
    return jnp.dot(matrix, jnp.concatenate([high, low], axis=0), preferred_element_type=F32)


def twice(matrix):
    return jnp.concatenate([matrix, matrix], axis=1)


def kernel(
    ring, samples, tiles, reach, otiles,
    atm_hbm, owners_hbm, otile_hbm, cent_hbm, w_hbm, ocean_hbm,
    flux_out, ocean_out, atm_out,
    rows_next, rows_back, atm, owners, otile, cent, w, ocean,
    val, part, pick, pick_t, spread, oc, table, col_inverse, lhs,
    send0, recv0, ends_sent, ends_got, send1a, recv1a, send1, recv1, send2a, recv2a, send2, recv2,
    send3, recv3, send3y, recv3y, send4, recv4, send5, recv5,
    in_sem, w_sem, halo_send, halo_recv, ssem, rsem, psend, precv,
):
    cols = ring * ring
    chips = samples // 2
    slots = MOST * ring
    rows = ring * slots
    entries = reach * PAD
    ends = 2 * reach
    col = lax.axis_index("cols")
    fld = lax.axis_index("fld")
    x, z = col // ring, col % ring
    chip, core = fld // 2, fld % 2
    first = (1 - core) * x + core * z
    second = (1 - core) * z + core * x

    def on_first(p):
        return ((1 - core) * (p * ring + second) + core * (second * ring + p), fld)

    def on_second(p):
        return ((1 - core) * (first * ring + p) + core * (p * ring + first), fld)

    def on_chip(p):
        return (col, p * 2 + core)

    sibling = (col, chip * 2 + 1 - core)
    left, right = (col + cols - 1) % cols, (col + 1) % cols

    barrier = pltpu.get_barrier_semaphore()

    def greet(device):
        pl.semaphore_signal(barrier, inc=1, device_id=device, device_id_type=MESH)

    def far_first(count):
        return sorted(range(1, count), key=lambda d: -min(d, count - d))

    for d in far_first(ring):
        greet(on_first((first + d) % ring))
        greet(on_second((second + d) % ring))
    for d in far_first(chips):
        greet(on_chip((chip + d) % chips))
    greet((left, fld))
    greet((right, fld))
    greet(sibling)

    small = [
        pltpu.make_async_copy(source, target, in_sem.at[i])
        for i, (source, target) in enumerate(
            ((atm_hbm, atm), (owners_hbm, owners), (otile_hbm, otile), (cent_hbm, cent), (ocean_hbm, ocean))
        )
    ]
    for copy in small:
        copy.start()
    groups, rest = (tiles - 2) // 4, (tiles - 2) % 4
    spans = [(1 + 4 * c, 4) for c in range(groups)] + [(1 + 4 * groups, rest + 1), (0, 1)]

    def weights(c):
        at = pl.ds(*spans[c]) if isinstance(c, int) else pl.ds(1 + 4 * c, 4)
        return pltpu.make_async_copy(w_hbm.at[at], w.at[at], w_sem.at[c])

    for c in (groups + 1, groups, *range(groups)):
        weights(c).start()

    def exchange(stage, count, me, device, source, target):
        def send():
            for d in far_first(count):
                pltpu.make_async_remote_copy(
                    src_ref=source((me + d) % count),
                    dst_ref=target.at[me],
                    send_sem=ssem.at[stage],
                    recv_sem=rsem.at[stage],
                    device_id=device((me + d) % count),
                    device_id_type=MESH,
                ).start()

        others = target.at[pl.ds(0, count - 1)]
        everything = pltpu.make_async_remote_copy(
            src_ref=others, dst_ref=others, send_sem=ssem.at[stage], recv_sem=rsem.at[stage],
            device_id=device((me + 1) % count), device_id_type=MESH,
        )
        return send, everything.wait_recv, everything.wait_send

    def to_sibling(i, source, target):
        return pltpu.make_async_remote_copy(
            src_ref=source, dst_ref=target, send_sem=psend.at[i], recv_sem=precv.at[i],
            device_id=sibling, device_id_type=MESH,
        )

    part[...] = jnp.zeros_like(part)
    col_inverse[...] = jnp.ones_like(col_inverse)
    small[0].wait()
    for t in range(tiles):
        val[t + 1] = atm[0, :, t * TILE : (t + 1) * TILE].astype(F32)
    to_right = pltpu.make_async_remote_copy(
        src_ref=val.at[tiles], dst_ref=val.at[0], send_sem=halo_send.at[0], recv_sem=halo_recv.at[0],
        device_id=(right, fld), device_id_type=MESH,
    )
    to_left = pltpu.make_async_remote_copy(
        src_ref=val.at[1], dst_ref=val.at[tiles + 1], send_sem=halo_send.at[1], recv_sem=halo_recv.at[1],
        device_id=(left, fld), device_id_type=MESH,
    )
    small[1].wait()
    small[2].wait()
    lane = lax.broadcasted_iota(I32, (FIELDS, TILE), 1)

    def across(ref, fill):
        table[...] = jnp.full((8, TILE), fill, F32)
        table[:reach, :tiles] = ref[...].astype(F32)
        line = jnp.broadcast_to(table[0:1], (8, TILE))
        for k in range(1, reach):
            shifted = pltpu.roll(jnp.broadcast_to(table[k : k + 1], (8, TILE)), k * PAD, 1)
            line = jnp.where(lane >= k * PAD, shifted, line)
        return line[:1]

    owner_across = across(owners, float(cols))
    tile_across = across(otile, 0.0)
    owner_down = jnp.broadcast_to(owner_across, (entries, entries)).T
    at_row = lax.broadcasted_iota(I32, (entries, entries), 0)
    at_lane = lax.broadcasted_iota(I32, (entries, entries), 1)
    same = owner_down == owner_across
    rank_down = jnp.sum((same & (at_lane < at_row)).astype(F32), axis=1, keepdims=True).astype(I32)
    rank_across = jnp.sum((same & (at_row < at_lane)).astype(F32), axis=0, keepdims=True).astype(I32)

    def slot(owner, rank):
        owner = owner.astype(I32)
        high = owner // ring
        low = owner - high * ring
        group = (1 - core) * high + core * low
        place = (1 - core) * low + core * high
        return jnp.where(owner < cols, group * slots + rank * ring + place, -1)

    tile_down = jnp.broadcast_to(tile_across, (entries, entries)).T

    def end_rows(x):
        at = [k * PAD for k in range(reach)] + [k * PAD + tiles - 1 for k in range(reach)]
        return jnp.concatenate([x[i : i + 1] for i in at], axis=0)

    end_owner = end_rows(owner_down).astype(I32)
    end_high = end_owner // ring
    end_low = end_owner - end_high * ring
    end_group = (1 - core) * end_high + core * end_low
    end_row = ((1 - core) * end_low + core * end_high) * 8 + end_rows(tile_down).astype(I32)

    slot_across = slot(owner_across, rank_across)
    slot_down = slot(owner_down[:, :1], rank_down)
    pick_f = (lax.broadcasted_iota(I32, (rows, entries), 0) == slot_across).astype(F32)
    pick[...] = twice(pick_f.astype(BF16))
    pick_b = (lax.broadcasted_iota(I32, (entries, rows), 1) == slot_down).astype(F32).astype(BF16)
    pick_t[...] = twice(pick_b)
    named = jnp.sum(pick_f * (tile_across + 1.0), axis=1, keepdims=True)
    named = jnp.broadcast_to(named - 1.0, (rows, TILE))
    for g in range(ring):
        send0[g, :slots] = named[g * slots : (g + 1) * slots]
        send0[g, slots : slots + ends] = jnp.where(end_group == g, end_row, -1).astype(F32)
    send_named, arrive0, leave0 = exchange(0, ring, first, on_first, lambda p: send0.at[p], recv0)

    small[4].wait()
    for r in range(4):
        oc[r] = jnp.zeros((8, TILE), F32)
        for t in range(otiles):
            oc[r, t : t + 1, :] = ocean[r : r + 1, t * TILE : (t + 1) * TILE]

    small[3].wait()
    zeros = jnp.zeros((16, TILE), F32)
    row8 = lax.broadcasted_iota(I32, (8, TILE), 0)
    last_lane = TILE - 1
    extra = jnp.where(row8 == 0, 1.0, 0.0)
    extra = jnp.where((row8 == 1) & (lane == 0) | (row8 == 2) & (lane == last_lane), 1.0, extra)

    def rebuild(t, before, here, after):
        low = jnp.where(lane == 0, pltpu.roll(before, 1, 1), pltpu.roll(here, 1, 1))
        high = jnp.where(lane == last_lane, pltpu.roll(after, last_lane, 1), pltpu.roll(here, last_lane, 1))
        slope = 0.5 * (high - low)
        return [here + cent[t, k : k + 1, :] * slope for k in range(reach)]

    def tile_sums(t, rebuilt):
        operand, operator = [], []
        for k in range(reach):
            block = jnp.concatenate([rebuilt[k], extra], axis=0)
            operand.append(jnp.concatenate([zeros, block] if k % 2 else [block, zeros], axis=1))
        for k in range(0, reach, 2):
            operator.append(jnp.concatenate([w[t, k], w[t, k + 1]], axis=1))
        product = lax.dot_general(
            jnp.concatenate(operand, axis=0).astype(BF16), jnp.concatenate(operator, axis=0),
            (((1,), (1,)), ((), ())), preferred_element_type=F32,
        )
        for k in range(reach):
            sums = product[16 * k : 16 * k + 16, k // 2 * TILE : (k // 2 + 1) * TILE]
            area = sums[FIELDS : FIELDS + 1]
            code = jnp.round(sums[:FIELDS] * (LEVELS / jnp.maximum(area, LEAST)))
            part[pl.ds(k * PAD + t, FIELDS, stride=entries), :] = code
            part[pl.ds(FIELDS * entries + k * PAD + t, 1), :] = area
        return [product[16 * k : 16 * k + 16, k // 2 * TILE : (k // 2 + 1) * TILE] for k in range(reach)]

    def inner_sums(t):
        return tile_sums(t, rebuild(t, val[t], val[t + 1], val[t + 2]))

    def group_sums(c, carry):
        weights(c).wait()
        for q in range(4):
            inner_sums(1 + 4 * c + q)
        return carry

    weights(groups + 1).wait()
    here = val[1]
    cut = [jnp.where(lane == 0, 0.0, x) for x in rebuild(0, here, here, val[2])]
    low_weights = [x[FIELDS + 1 : FIELDS + 2] for x in tile_sums(0, cut)]
    weights(groups).wait()
    here = val[tiles]
    cut = [jnp.where(lane == last_lane, 0.0, x) for x in rebuild(tiles - 1, val[tiles - 1], here, here)]
    high_weights = [x[FIELDS + 2 : FIELDS + 3] for x in tile_sums(tiles - 1, cut)]
    end_weights = jnp.concatenate(low_weights + high_weights, axis=0)
    for g in range(ring):
        send0[g, slots + ends :] = end_weights
    for q in range(rest):
        inner_sums(1 + 4 * groups + q)

    early = min(groups, 3)
    lax.fori_loop(0, early, group_sums, 0)
    pl.semaphore_wait(barrier, 3 + 2 * (ring - 1) + chips - 1)
    send_named()
    to_right.start()
    to_left.start()
    recv0[first] = send0[first]
    lax.fori_loop(early, groups, group_sums, 0)

    send, arrive1a, leave1a = exchange(1, ring, first, on_first, lambda p: send1a.at[p], recv1a)
    slotted = mixed(pick[...], part[FIELDS * entries :])
    for g in range(ring):
        send1a[g] = slotted[g * slots : (g + 1) * slots]
    send()
    sent1 = []
    for m in range(2):
        codes = []
        for f in range(4 * m, 4 * m + 4):
            codes.append(mixed(pick[...], part[f * entries : (f + 1) * entries]))
        for g in range(ring):
            block = jnp.concatenate([x[g * slots : (g + 1) * slots] for x in codes], axis=0)
            send1[m, g] = block.astype(I32).astype(I16)
        send, *done = exchange(2 + m, ring, first, on_first, lambda p: send1.at[m, p], recv1.at[m])
        send()
        sent1.append(done)
    recv1a[first] = send1a[first]
    for m in range(2):
        recv1[m, first] = send1[m, first]

    to_right.wait_recv()
    to_left.wait_recv()
    end_values = jnp.zeros((8, TILE), F32)
    low = rebuild(0, val[0], val[1], val[2])
    high = rebuild(tiles - 1, val[tiles - 1], val[tiles], val[tiles + 1])
    for k in range(reach):
        moved = pltpu.roll(low[k], k, 1) if k else low[k]
        end_values = jnp.where(lane == k, moved, end_values)
        end_values = jnp.where(lane == reach + k, pltpu.roll(high[k], reach + 1 + k, 1), end_values)
    end_values = end_values.astype(BF16).astype(F32)
    ends_sent[...] = jnp.concatenate([end_values, jnp.zeros((TILE - 8, TILE), F32)], axis=0).T[:ends]
    send, arrive_ends, leave_ends = exchange(4, ring, first, on_first, lambda p: ends_sent, ends_got)
    send()
    ends_got[first] = ends_sent[...]

    arrive0()
    row = lax.broadcasted_iota(I32, (rows, TILE), 0)
    lane_of = lax.broadcasted_iota(I32, (rows, TILE), 1)
    target = recv0[:, :slots].reshape(rows, TILE).astype(I32)
    member = ((target >= 0) & (target + 8 * (row % ring) == lane_of)).astype(F32)
    spread[...] = twice(member[:, : 8 * ring].astype(BF16))
    target = recv0[:, slots : slots + ends].reshape(ring * ends, TILE).astype(I32)
    member_ends = (target == lax.broadcasted_iota(I32, (ring * ends, TILE), 1)).astype(F32)
    gather = twice(jnp.concatenate([member, member_ends], axis=0).T[: 8 * ring].astype(BF16))
    end_weights = recv0[:, slots + ends :].reshape(ring * ends, TILE) * LEVELS

    def column_area(c, carry):
        for q in range(chunk):
            t = c * chunk + q
            area = jnp.sum(w[t].reshape(reach * TILE, TILE).astype(F32), axis=0, keepdims=True)
            col_inverse[pl.ds(t, 1), :] = 1.0 / area
        return carry

    chunk = 4 if tiles % 4 == 0 else 1
    lax.fori_loop(0, tiles // chunk, column_area, 0)

    send, arrive2a, leave2a = exchange(5, ring, second, on_second, lambda p: send2a.at[p], recv2a)
    arrive1a()
    areas = recv1a[...].reshape(rows, TILE)
    dense_area = mixed(gather, jnp.concatenate([areas, jnp.zeros((ring * ends, TILE), F32)], axis=0))
    send2a[...] = dense_area.reshape(ring, 8, TILE)
    send()
    recv2a[second] = send2a[second]
    per_area = 1.0 / jnp.maximum(dense_area, LEAST)
    send, arrive2, leave2 = exchange(6, ring, second, on_second, lambda p: send2.at[p], recv2)
    arrive_ends()
    end_values = ends_got[...].reshape(ring * ends, TILE)
    for m in range(2):
        arrive, _ = sent1[m]
        arrive()
        block = recv1[m].astype(I32).astype(F32)
        means = []
        for i in range(4):
            f = 4 * m + i
            sums = block[:, i * slots : (i + 1) * slots].reshape(rows, TILE) * areas
            sums = jnp.concatenate([sums, end_values[:, f : f + 1] * end_weights], axis=0)
            means.append((mixed(gather, sums) * per_area).reshape(ring, 8, TILE))
        block = jnp.concatenate(means, axis=1)
        send2[:, 32 * m : 32 * m + 32] = jnp.round(block).astype(I32).astype(I16)
    send()
    recv2[second] = send2[second]
    arrive2a()
    arrive2()

    coverage = jnp.zeros((8, TILE), F32)
    total = jnp.zeros((FIELDS, 8, TILE), F32)
    for p in range(ring):
        area = recv2a[p]
        coverage = coverage + area
        total = total + recv2[p].astype(I32).astype(F32).reshape(FIELDS, 8, TILE) * area[None]
    forcing = total * (1.0 / (LEVELS * jnp.maximum(coverage, 1.0)))[None]

    sst, uo, vo = oc[0], oc[1], oc[2]
    slip_u = forcing[0] - uo
    slip_v = forcing[1] - vo
    wind_speed = jnp.sqrt(slip_u * slip_u + slip_v * slip_v + 0.25)
    saturation = 0.9 * jnp.exp(0.07 * sst - 0.1 * forcing[4])
    sensible = 0.4 * wind_speed * (sst - forcing[2])
    latent = 0.4 * wind_speed * (saturation - forcing[3])

    def softplus(v):
        return jnp.maximum(v, 0.0) + jnp.log1p(jnp.exp(-jnp.abs(v)))

    insolation = 0.5 + 1.5 * fld.astype(F32) / (samples - 1)
    net_heat = insolation * softplus(forcing[5]) + 0.3 * forcing[6] - 0.1 * sst - sensible - latent
    freshwater = softplus(forcing[7]) - latent
    stress_u = 0.5 * wind_speed * slip_u
    stress_v = 0.5 * wind_speed * slip_v
    send3[0] = net_heat
    send3[1] = stress_u
    send3[2] = stress_v
    send3[3] = -freshwater

    mine, other = pl.ds(2 * core, 2), pl.ds(2 - 2 * core, 2)
    pair_copy = to_sibling(0, send3.at[other], recv3)
    pair_copy.start()
    pair_copy.wait_recv()
    send3y[...] = send3[mine] + recv3[...]
    send, arrive, leave3 = exchange(7, chips, chip, on_chip, lambda p: send3y, recv3y)
    send()
    recv3y[chip] = send3y[...]
    for i, flux in enumerate((stress_u, stress_v, net_heat, freshwater)):
        for t in range(otiles):
            flux_out[0, i : i + 1, t * TILE : (t + 1) * TILE] = flux[t : t + 1]
    for leave in (leave0, leave1a, leave_ends, leave2a, leave2, to_right.wait_send, to_left.wait_send):
        leave()
    for _, leave in sent1:
        leave()
    pair_copy.wait_send()
    arrive()
    flux_sum = recv3y[0]
    for p in range(1, chips):
        flux_sum = flux_sum + recv3y[p]
    state = oc[mine] + (0.5 / samples) * flux_sum
    send4[...] = state

    send, arrive, leave4 = exchange(8, ring, second, on_second, lambda p: send4, recv4)
    send()
    recv4[second] = state
    rows_next[mine] = state
    ocean_copy = to_sibling(1, rows_next.at[mine], rows_next.at[mine])
    ocean_copy.start()
    leave3()
    arrive()

    states = [recv4[:, r].reshape(ring * 8, TILE) for r in range(2)]
    slotted = mixed(spread[...], jnp.concatenate(states, axis=1))
    for p in range(ring):
        for r in range(2):
            send5[p, r] = slotted[p * slots : (p + 1) * slots, r * TILE : (r + 1) * TILE]
    send, arrive, leave5 = exchange(9, ring, first, on_first, lambda p: send5.at[p], recv5)
    send()
    recv5[first] = send5[first]
    to_sibling(1, rows_next.at[mine], rows_next.at[other]).wait_recv()
    for r in range(4):
        for t in range(otiles):
            ocean_out[r : r + 1, t * TILE : (t + 1) * TILE] = rows_next[r, t : t + 1]
    ocean_copy.wait_send()
    leave4()
    arrive()

    states = [recv5[:, r].reshape(rows, TILE) for r in range(2)]
    entry = mixed(pick_t[...], jnp.concatenate(states, axis=1))
    high, low = split(entry)
    high, low = high.astype(F32), low.astype(F32)
    for k in range(reach):
        for j in range(PAD // 8):
            at = slice(k * PAD + j * 8, k * PAD + j * 8 + 8)
            block = [high[at, :TILE], low[at, :TILE], high[at, TILE:], low[at, TILE:]]
            lhs[j, :, k * TILE : (k + 1) * TILE] = jnp.concatenate(block, axis=0).astype(BF16)


    def results(j):
        at = pl.ds(j * 8, 8)
        return to_sibling(2 + j, rows_back.at[mine, at], rows_back.at[mine, at])

    def remap(j, count):
        operand = lhs[j]
        one = two = jnp.zeros((8, TILE), F32)
        for q in range(count):
            sums = jnp.dot(operand, w[j * 8 + q].reshape(reach * TILE, TILE), preferred_element_type=F32)
            one = jnp.where(row8 == q, sums[0:8] + sums[8:16], one)
            two = jnp.where(row8 == q, sums[16:24] + sums[24:32], two)
        at = pl.ds(j * 8, 8)
        inverse = col_inverse[at]
        rows_back[2 * core, at] = one * inverse
        rows_back[2 * core + 1, at] = two * inverse
        results(j).start()

    def full_remap(j, carry):
        remap(j, 8)
        return carry

    whole, last = tiles // 8, tiles % 8
    lax.fori_loop(0, whole, full_remap, 0)
    if last:
        remap(whole, last)
    leave5()
    for j in range(whole + (last > 0)):
        at = pl.ds(j * 8, 8)
        to_sibling(2 + j, rows_back.at[mine, at], rows_back.at[other, at]).wait_recv()
        for r in range(4):
            for t in range(8 * j, min(8 * j + 8, tiles)):
                atm_out[r : r + 1, t * TILE : (t + 1) * TILE] = rows_back[r, t : t + 1]
    for j in range(whole + (last > 0)):
        results(j).wait_send()


def shards(atm_state, owners, ocean_tile, centroid_offset, remap_weight, ocean_state):
    ring = math.isqrt(lax.axis_size("cols"))
    samples = lax.axis_size("fld")
    cells = atm_state.shape[2]
    tiles = cells // TILE
    reach = owners.shape[1]
    ocells = ocean_state.shape[1]
    otiles = ocells // TILE
    chips = samples // 2
    slots = MOST * ring
    rows = ring * slots
    entries = reach * PAD
    hbm = pl.BlockSpec(memory_space=pltpu.HBM)
    vmem = pl.BlockSpec(memory_space=pltpu.VMEM)
    out_shape = (
        jax.ShapeDtypeStruct((1, 4, ocells), F32),
        jax.ShapeDtypeStruct((4, ocells), F32),
        jax.ShapeDtypeStruct((4, cells), F32),
    )
    results = pl.pallas_call(
        functools.partial(kernel, ring, samples, tiles, reach, otiles),
        out_shape=tuple(pltpu.VMEM(s.shape, s.dtype) for s in out_shape),
        in_specs=[hbm] * 6,
        out_specs=(vmem, vmem, vmem),
        scratch_shapes=[
            pltpu.VMEM((4, 8, TILE), F32),
            pltpu.VMEM((4, PAD, TILE), F32),
            pltpu.VMEM(atm_state.shape, BF16),
            pltpu.VMEM((reach, tiles), I32),
            pltpu.VMEM((reach, tiles), I32),
            pltpu.VMEM((tiles, reach, TILE), F32),
            pltpu.VMEM((tiles, reach, TILE, TILE), BF16),
            pltpu.VMEM((4, ocells), F32),
            pltpu.VMEM((tiles + 2, FIELDS, TILE), F32),
            pltpu.VMEM(((FIELDS + 1) * entries, TILE), F32),
            pltpu.VMEM((rows, 2 * entries), BF16),
            pltpu.VMEM((entries, 2 * rows), BF16),
            pltpu.VMEM((rows, 16 * ring), BF16),
            pltpu.VMEM((4, 8, TILE), F32),
            pltpu.VMEM((8, TILE), F32),
            pltpu.VMEM((PAD, TILE), F32),
            pltpu.VMEM((PAD // 8, 32, reach * TILE), BF16),
            pltpu.VMEM((ring, slots + 4 * reach, TILE), F32),
            pltpu.VMEM((ring, slots + 4 * reach, TILE), F32),
            pltpu.VMEM((2 * reach, TILE), F32),
            pltpu.VMEM((ring, 2 * reach, TILE), F32),
            pltpu.VMEM((ring, slots, TILE), F32),
            pltpu.VMEM((ring, slots, TILE), F32),
            pltpu.VMEM((2, ring, 4 * slots, TILE), I16),
            pltpu.VMEM((2, ring, 4 * slots, TILE), I16),
            pltpu.VMEM((ring, 8, TILE), F32),
            pltpu.VMEM((ring, 8, TILE), F32),
            pltpu.VMEM((ring, FIELDS * 8, TILE), I16),
            pltpu.VMEM((ring, FIELDS * 8, TILE), I16),
            pltpu.VMEM((4, 8, TILE), F32),
            pltpu.VMEM((2, 8, TILE), F32),
            pltpu.VMEM((2, 8, TILE), F32),
            pltpu.VMEM((chips, 2, 8, TILE), F32),
            pltpu.VMEM((2, 8, TILE), F32),
            pltpu.VMEM((ring, 2, 8, TILE), F32),
            pltpu.VMEM((ring, 2, slots, TILE), F32),
            pltpu.VMEM((ring, 2, slots, TILE), F32),
            pltpu.SemaphoreType.DMA((5,)),
            pltpu.SemaphoreType.DMA((tiles,)),
            pltpu.SemaphoreType.DMA((2,)),
            pltpu.SemaphoreType.DMA((2,)),
            pltpu.SemaphoreType.DMA((10,)),
            pltpu.SemaphoreType.DMA((10,)),
            pltpu.SemaphoreType.DMA((2 + PAD // 8,)),
            pltpu.SemaphoreType.DMA((2 + PAD // 8,)),
        ],
        compiler_params=pltpu.CompilerParams(
            collective_id=0, has_side_effects=True, vmem_limit_bytes=60 * 1024 * 1024
        ),
        name="coupling",
    )(atm_state, owners.T, ocean_tile.T, centroid_offset, remap_weight, ocean_state)
    return results


def solution(mesh):
    return jax.shard_map(
        shards,
        mesh=mesh,
        in_specs=(
            P("fld", None, "cols"),
            P("cols", None),
            P("cols", None),
            P("cols", None, None),
            P("cols", None, None, None),
            P(None, "cols"),
        ),
        out_specs=(P("fld", None, "cols"), P(None, "cols"), P(None, "cols")),
        check_vma=False,
    )
```

```python
import functools
import math

import jax
import jax.numpy as jnp
from jax import lax
from jax.experimental import pallas as pl
from jax.experimental.pallas import tpu as pltpu
from jax.sharding import PartitionSpec as P

TILE = 128
FIELDS = 8
MOST = 3
PAD = 32
LEVELS = 5400.0
LEAST = 1e-30
MESH = pl.DeviceIdType.MESH
F32 = jnp.float32
BF16 = jnp.bfloat16
I32 = jnp.int32
I16 = jnp.int16


def split(x):
    high = x.astype(BF16)
    return high, (x - high.astype(F32)).astype(BF16)


def mixed(matrix, x):
    high, low = split(x)
    return jnp.dot(matrix, jnp.concatenate([high, low], axis=0), preferred_element_type=F32)


def twice(matrix):
    return jnp.concatenate([matrix, matrix], axis=1)


def kernel(
    ring, samples, tiles, reach, otiles,
    atm_hbm, owners_hbm, otile_hbm, cent_hbm, w_hbm, ocean_hbm,
    out,
    rows_next, rows_back, atm, owners, otile, cent, w, ocean,
    val, part, pick, pick_t, spread, oc, table, col_inverse, lhs,
    send0, recv0, ends_sent, ends_got, send1a, recv1a, send1, recv1, send2a, recv2a, send2, recv2,
    send3, recv3, send3y, recv3y, send4, recv4, send5, recv5,
    in_sem, w_sem, halo_send, halo_recv, ssem, rsem, psend, precv,
):
    cols = ring * ring
    chips = samples // 2
    slots = MOST * ring
    rows = ring * slots
    entries = reach * PAD
    ends = 2 * reach
    col = lax.axis_index("cols")
    fld = lax.axis_index("fld")
    x, z = col // ring, col % ring
    chip, core = fld // 2, fld % 2
    first = (1 - core) * x + core * z
    second = (1 - core) * z + core * x

    def on_first(p):
        return ((1 - core) * (p * ring + second) + core * (second * ring + p), fld)

    def on_second(p):
        return ((1 - core) * (first * ring + p) + core * (p * ring + first), fld)

    def on_chip(p):
        return (col, p * 2 + core)

    sibling = (col, chip * 2 + 1 - core)
    left, right = (col + cols - 1) % cols, (col + 1) % cols

    barrier = pltpu.get_barrier_semaphore()

    def greet(device):
        pl.semaphore_signal(barrier, inc=1, device_id=device, device_id_type=MESH)

    def far_first(count):
        return sorted(range(1, count), key=lambda d: -min(d, count - d))

    for d in far_first(ring):
        greet(on_first((first + d) % ring))
        greet(on_second((second + d) % ring))
    for d in far_first(chips):
        greet(on_chip((chip + d) % chips))
    greet((left, fld))
    greet((right, fld))
    greet(sibling)

    small = [
        pltpu.make_async_copy(source, target, in_sem.at[i])
        for i, (source, target) in enumerate(
            ((atm_hbm, atm), (owners_hbm, owners), (otile_hbm, otile), (cent_hbm, cent), (ocean_hbm, ocean))
        )
    ]
    for copy in small:
        copy.start()
    groups, rest = (tiles - 2) // 4, (tiles - 2) % 4
    spans = [(1 + 4 * c, 4) for c in range(groups)] + [(1 + 4 * groups, rest + 1), (0, 1)]

    def weights(c):
        at = pl.ds(*spans[c]) if isinstance(c, int) else pl.ds(1 + 4 * c, 4)
        return pltpu.make_async_copy(w_hbm.at[at], w.at[at], w_sem.at[c])

    for c in (groups + 1, groups, *range(groups)):
        weights(c).start()

    def exchange(stage, count, me, device, source, target):
        def send():
            for d in far_first(count):
                pltpu.make_async_remote_copy(
                    src_ref=source((me + d) % count),
                    dst_ref=target.at[me],
                    send_sem=ssem.at[stage],
                    recv_sem=rsem.at[stage],
                    device_id=device((me + d) % count),
                    device_id_type=MESH,
                ).start()

        others = target.at[pl.ds(0, count - 1)]
        everything = pltpu.make_async_remote_copy(
            src_ref=others, dst_ref=others, send_sem=ssem.at[stage], recv_sem=rsem.at[stage],
            device_id=device((me + 1) % count), device_id_type=MESH,
        )
        return send, everything.wait_recv, everything.wait_send

    def to_sibling(i, source, target):
        return pltpu.make_async_remote_copy(
            src_ref=source, dst_ref=target, send_sem=psend.at[i], recv_sem=precv.at[i],
            device_id=sibling, device_id_type=MESH,
        )

    part[...] = jnp.zeros_like(part)
    col_inverse[...] = jnp.ones_like(col_inverse)
    small[0].wait()
    for t in range(tiles):
        val[t + 1] = atm[0, :, t * TILE : (t + 1) * TILE].astype(F32)
    to_right = pltpu.make_async_remote_copy(
        src_ref=val.at[tiles], dst_ref=val.at[0], send_sem=halo_send.at[0], recv_sem=halo_recv.at[0],
        device_id=(right, fld), device_id_type=MESH,
    )
    to_left = pltpu.make_async_remote_copy(
        src_ref=val.at[1], dst_ref=val.at[tiles + 1], send_sem=halo_send.at[1], recv_sem=halo_recv.at[1],
        device_id=(left, fld), device_id_type=MESH,
    )
    small[1].wait()
    small[2].wait()
    lane = lax.broadcasted_iota(I32, (FIELDS, TILE), 1)

    def across(ref, fill):
        table[...] = jnp.full((8, TILE), fill, F32)
        table[:reach, :tiles] = ref[...].astype(F32)
        line = jnp.broadcast_to(table[0:1], (8, TILE))
        for k in range(1, reach):
            shifted = pltpu.roll(jnp.broadcast_to(table[k : k + 1], (8, TILE)), k * PAD, 1)
            line = jnp.where(lane >= k * PAD, shifted, line)
        return line[:1]

    owner_across = across(owners, float(cols))
    tile_across = across(otile, 0.0)
    owner_down = jnp.broadcast_to(owner_across, (entries, entries)).T
    at_row = lax.broadcasted_iota(I32, (entries, entries), 0)
    at_lane = lax.broadcasted_iota(I32, (entries, entries), 1)
    same = owner_down == owner_across
    rank_down = jnp.sum((same & (at_lane < at_row)).astype(F32), axis=1, keepdims=True).astype(I32)
    rank_across = jnp.sum((same & (at_row < at_lane)).astype(F32), axis=0, keepdims=True).astype(I32)

    def slot(owner, rank):
        owner = owner.astype(I32)
        high = owner // ring
        low = owner - high * ring
        group = (1 - core) * high + core * low
        place = (1 - core) * low + core * high
        return jnp.where(owner < cols, group * slots + rank * ring + place, -1)

    def place_of(owner):
        owner = owner.astype(I32)
        high = owner // ring
        low = owner - high * ring
        return (1 - core) * high + core * low, (1 - core) * low + core * high

    group_across, place_across = place_of(owner_across)
    group_down, place_down = place_of(owner_down)
    slot_across = jnp.where(owner_across < cols, group_across * slots + rank_across * ring + place_across, -1)
    seat_down = rank_down * ring + place_down
    slot_down = jnp.where(owner_down < cols, group_down * slots + seat_down, -1)[:, :1]
    pick_f = (lax.broadcasted_iota(I32, (rows, entries), 0) == slot_across).astype(F32)
    pick[...] = twice(pick_f.astype(BF16))
    pick_b = (lax.broadcasted_iota(I32, (entries, rows), 1) == slot_down).astype(F32).astype(BF16)
    pick_t[...] = twice(pick_b)

    stride = slots + ends
    per_line = TILE // stride
    base = (first % per_line) * stride
    ocean_row = place_across * 8 + tile_across.astype(I32) + 1
    group_row = lax.broadcasted_iota(I32, (8, entries), 0) == group_across
    marked = jnp.where(group_row & (owner_across < cols), ocean_row, 0).astype(F32).astype(BF16)
    tile_at, k_at = at_row % PAD, at_row // PAD
    seated = (at_lane == base + seat_down) & (owner_down < cols)
    seated = seated | (tile_at == 0) & (at_lane == base + slots + k_at)
    seated = seated | (tile_at == tiles - 1) & (at_lane == base + slots + reach + k_at)
    named = jnp.dot(marked, seated.astype(F32).astype(BF16), preferred_element_type=F32)
    line_of = lax.broadcasted_iota(I32, (8, TILE), 0) == first // per_line
    for g in range(ring):
        send0[g, :8] = jnp.where(line_of, named[g : g + 1], 0.0)
    send_named, arrive0, leave0 = exchange(0, ring, first, on_first, lambda p: send0.at[p], recv0)

    small[4].wait()
    for r in range(4):
        oc[r] = jnp.zeros((8, TILE), F32)
        for t in range(otiles):
            oc[r, t : t + 1, :] = ocean[r : r + 1, t * TILE : (t + 1) * TILE]

    small[3].wait()
    zeros = jnp.zeros((16, TILE), F32)
    row8 = lax.broadcasted_iota(I32, (8, TILE), 0)
    last_lane = TILE - 1
    extra = jnp.where(row8 == 0, 1.0, 0.0)
    extra = jnp.where((row8 == 1) & (lane == 0) | (row8 == 2) & (lane == last_lane), 1.0, extra)

    def rebuild(t, before, here, after):
        low = jnp.where(lane == 0, pltpu.roll(before, 1, 1), pltpu.roll(here, 1, 1))
        high = jnp.where(lane == last_lane, pltpu.roll(after, last_lane, 1), pltpu.roll(here, last_lane, 1))
        slope = 0.5 * (high - low)
        return [here + cent[t, k : k + 1, :] * slope for k in range(reach)]

    def tile_sums(t, rebuilt):
        operand, operator = [], []
        for k in range(reach):
            block = jnp.concatenate([rebuilt[k], extra], axis=0)
            operand.append(jnp.concatenate([zeros, block] if k % 2 else [block, zeros], axis=1))
        for k in range(0, reach, 2):
            operator.append(jnp.concatenate([w[t, k], w[t, k + 1]], axis=1))
        product = lax.dot_general(
            jnp.concatenate(operand, axis=0).astype(BF16), jnp.concatenate(operator, axis=0),
            (((1,), (1,)), ((), ())), preferred_element_type=F32,
        )
        for k in range(reach):
            sums = product[16 * k : 16 * k + 16, k // 2 * TILE : (k // 2 + 1) * TILE]
            area = sums[FIELDS : FIELDS + 1]
            code = jnp.round(sums[:FIELDS] * (LEVELS / jnp.maximum(area, LEAST)))
            part[pl.ds(k * PAD + t, FIELDS, stride=entries), :] = code
            part[pl.ds(FIELDS * entries + k * PAD + t, 1), :] = area
        return [product[16 * k : 16 * k + 16, k // 2 * TILE : (k // 2 + 1) * TILE] for k in range(reach)]

    def inner_sums(t):
        return tile_sums(t, rebuild(t, val[t], val[t + 1], val[t + 2]))

    def group_sums(c, carry):
        weights(c).wait()
        for q in range(4):
            inner_sums(1 + 4 * c + q)
        return carry

    weights(groups + 1).wait()
    here = val[1]
    cut = [jnp.where(lane == 0, 0.0, x) for x in rebuild(0, here, here, val[2])]
    low_weights = [x[FIELDS + 1 : FIELDS + 2] for x in tile_sums(0, cut)]
    weights(groups).wait()
    here = val[tiles]
    cut = [jnp.where(lane == last_lane, 0.0, x) for x in rebuild(tiles - 1, val[tiles - 1], here, here)]
    high_weights = [x[FIELDS + 2 : FIELDS + 3] for x in tile_sums(tiles - 1, cut)]
    end_weights = jnp.concatenate(low_weights + high_weights, axis=0)
    for g in range(ring):
        send0[g, 8:] = end_weights
    for q in range(rest):
        inner_sums(1 + 4 * groups + q)

    early = min(groups, 5)
    lax.fori_loop(0, early, group_sums, 0)
    pl.semaphore_wait(barrier, 3 + 2 * (ring - 1) + chips - 1)
    send_named()
    to_right.start()
    to_left.start()
    recv0[first] = send0[first]
    lax.fori_loop(early, groups, group_sums, 0)

    send, arrive1a, leave1a = exchange(1, ring, first, on_first, lambda p: send1a.at[p], recv1a)
    slotted = mixed(pick[...], part[FIELDS * entries :])
    for g in range(ring):
        send1a[g] = slotted[g * slots : (g + 1) * slots]
    send()
    sent1 = []
    for m in range(2):
        codes = [part[f * entries : (f + 1) * entries] for f in range(4 * m, 4 * m + 4)]
        codes = mixed(pick[...], jnp.concatenate(codes, axis=1))
        codes = [codes[:, i * TILE : (i + 1) * TILE] for i in range(4)]
        for g in range(ring):
            block = jnp.concatenate([x[g * slots : (g + 1) * slots] for x in codes], axis=0)
            send1[m, g] = block.astype(I32).astype(I16)
        send, *done = exchange(2 + m, ring, first, on_first, lambda p: send1.at[m, p], recv1.at[m])
        send()
        sent1.append(done)
    recv1a[first] = send1a[first]
    for m in range(2):
        recv1[m, first] = send1[m, first]

    to_right.wait_recv()
    to_left.wait_recv()
    end_values = jnp.zeros((8, TILE), F32)
    low = rebuild(0, val[0], val[1], val[2])
    high = rebuild(tiles - 1, val[tiles - 1], val[tiles], val[tiles + 1])
    for k in range(reach):
        moved = pltpu.roll(low[k], k, 1) if k else low[k]
        end_values = jnp.where(lane == k, moved, end_values)
        end_values = jnp.where(lane == reach + k, pltpu.roll(high[k], reach + 1 + k, 1), end_values)
    end_values = end_values.astype(BF16).astype(F32)
    ends_sent[...] = jnp.concatenate([end_values, jnp.zeros((TILE - 8, TILE), F32)], axis=0).T[:ends]
    send, arrive_ends, leave_ends = exchange(4, ring, first, on_first, lambda p: ends_sent, ends_got)
    send()
    ends_got[first] = ends_sent[...]

    arrive0()
    lines = jnp.zeros((8, TILE), F32)
    for p in range(ring):
        lines = lines + recv0[p, :8]
    want = (lax.broadcasted_iota(I32, (TILE, TILE), 0) + 1).astype(F32)
    member = [(want == lines[i : i + 1]).astype(F32) for i in range(-(-ring // per_line))]
    gather = jnp.concatenate(member, axis=1)[: 8 * ring, : ring * stride]
    gather = twice(gather.astype(BF16))
    back_rows = jnp.concatenate([x.T for x in member], axis=0)[: ring * stride, : 8 * ring]
    spread[...] = twice(back_rows.astype(BF16))
    end_weights = recv0[:, 8:] * LEVELS

    def stacked(of_slots, of_ends):
        return jnp.concatenate([of_slots, of_ends], axis=1).reshape(ring * stride, TILE)

    def column_area(c, carry):
        for q in range(chunk):
            t = c * chunk + q
            area = jnp.sum(w[t].reshape(reach * TILE, TILE).astype(F32), axis=0, keepdims=True)
            col_inverse[pl.ds(t, 1), :] = 1.0 / area
        return carry

    chunk = 4 if tiles % 4 == 0 else 1
    lax.fori_loop(0, tiles // chunk, column_area, 0)

    send, arrive2a, leave2a = exchange(5, ring, second, on_second, lambda p: send2a.at[p], recv2a)
    arrive1a()
    areas = recv1a[...]
    dense_area = mixed(gather, stacked(areas, jnp.zeros((ring, ends, TILE), F32)))
    send2a[...] = dense_area.reshape(ring, 8, TILE)
    send()
    recv2a[second] = send2a[second]
    per_area = 1.0 / jnp.maximum(dense_area, LEAST)
    send, arrive2, leave2 = exchange(6, ring, second, on_second, lambda p: send2.at[p], recv2)
    arrive_ends()
    end_values = ends_got[...]
    for m in range(2):
        arrive, _ = sent1[m]
        arrive()
        block = recv1[m].astype(I32).astype(F32)
        means = []
        for i in range(4):
            f = 4 * m + i
            sums = block[:, i * slots : (i + 1) * slots] * areas
            sums = stacked(sums, end_values[:, :, f : f + 1] * end_weights)
            means.append((mixed(gather, sums) * per_area).reshape(ring, 8, TILE))
        block = jnp.concatenate(means, axis=1)
        send2[:, 32 * m : 32 * m + 32] = jnp.round(block).astype(I32).astype(I16)
    send()
    recv2[second] = send2[second]
    arrive2a()
    arrive2()

    coverage = jnp.zeros((8, TILE), F32)
    total = jnp.zeros((FIELDS, 8, TILE), F32)
    for p in range(ring):
        area = recv2a[p]
        coverage = coverage + area
        total = total + recv2[p].astype(I32).astype(F32).reshape(FIELDS, 8, TILE) * area[None]
    forcing = total * (1.0 / (LEVELS * jnp.maximum(coverage, 1.0)))[None]

    sst, uo, vo = oc[0], oc[1], oc[2]
    slip_u = forcing[0] - uo
    slip_v = forcing[1] - vo
    wind_speed = jnp.sqrt(slip_u * slip_u + slip_v * slip_v + 0.25)
    saturation = 0.9 * jnp.exp(0.07 * sst - 0.1 * forcing[4])
    sensible = 0.4 * wind_speed * (sst - forcing[2])
    latent = 0.4 * wind_speed * (saturation - forcing[3])

    def softplus(v):
        return jnp.maximum(v, 0.0) + jnp.log1p(jnp.exp(-jnp.abs(v)))

    insolation = 0.5 + 1.5 * fld.astype(F32) / (samples - 1)
    net_heat = insolation * softplus(forcing[5]) + 0.3 * forcing[6] - 0.1 * sst - sensible - latent
    freshwater = softplus(forcing[7]) - latent
    stress_u = 0.5 * wind_speed * slip_u
    stress_v = 0.5 * wind_speed * slip_v
    send3[0] = net_heat
    send3[1] = stress_u
    send3[2] = stress_v
    send3[3] = -freshwater

    mine, other = pl.ds(2 * core, 2), pl.ds(2 - 2 * core, 2)
    pair_copy = to_sibling(0, send3.at[other], recv3)
    pair_copy.start()
    pair_copy.wait_recv()
    send3y[...] = send3[mine] + recv3[...]
    send, arrive, leave3 = exchange(7, chips, chip, on_chip, lambda p: send3y, recv3y)
    send()
    recv3y[chip] = send3y[...]
    for i, flux in enumerate((stress_u, stress_v, net_heat, freshwater)):
        for t in range(otiles):
            out[i : i + 1, t * TILE : (t + 1) * TILE] = flux[t : t + 1]
    for leave in (leave0, leave1a, leave_ends, leave2a, leave2, to_right.wait_send, to_left.wait_send):
        leave()
    for _, leave in sent1:
        leave()
    pair_copy.wait_send()
    arrive()
    flux_sum = recv3y[0]
    for p in range(1, chips):
        flux_sum = flux_sum + recv3y[p]
    state = oc[mine] + (0.5 / samples) * flux_sum
    send4[...] = state

    send, arrive, leave4 = exchange(8, ring, second, on_second, lambda p: send4, recv4)
    send()
    recv4[second] = state
    rows_next[mine] = state
    ocean_copy = to_sibling(1, rows_next.at[mine], rows_next.at[mine])
    ocean_copy.start()
    leave3()
    arrive()

    states = [recv4[:, r].reshape(ring * 8, TILE) for r in range(2)]
    slotted = mixed(spread[...], jnp.concatenate(states, axis=1))
    for p in range(ring):
        for r in range(2):
            send5[p, r] = slotted[p * stride : p * stride + slots, r * TILE : (r + 1) * TILE]
    send, arrive, leave5 = exchange(9, ring, first, on_first, lambda p: send5.at[p], recv5)
    send()
    recv5[first] = send5[first]
    to_sibling(1, rows_next.at[mine], rows_next.at[other]).wait_recv()
    for r in range(4):
        for t in range(otiles):
            out[r : r + 1, (otiles + t) * TILE : (otiles + t + 1) * TILE] = rows_next[r, t : t + 1]
    ocean_copy.wait_send()
    leave4()
    arrive()

    states = [recv5[:, r].reshape(rows, TILE) for r in range(2)]
    entry = mixed(pick_t[...], jnp.concatenate(states, axis=1))
    high, low = split(entry)
    high, low = high.astype(F32), low.astype(F32)
    for k in range(reach):
        for j in range(PAD // 8):
            at = slice(k * PAD + j * 8, k * PAD + j * 8 + 8)
            block = [high[at, :TILE], low[at, :TILE], high[at, TILE:], low[at, TILE:]]
            lhs[j, :, k * TILE : (k + 1) * TILE] = jnp.concatenate(block, axis=0).astype(BF16)


    def results(j):
        at = pl.ds(j * 8, 8)
        return to_sibling(2 + j, rows_back.at[mine, at], rows_back.at[mine, at])

    def remap(j, count):
        operand = lhs[j]
        one = two = jnp.zeros((8, TILE), F32)
        for q in range(count):
            sums = jnp.dot(operand, w[j * 8 + q].reshape(reach * TILE, TILE), preferred_element_type=F32)
            one = jnp.where(row8 == q, sums[0:8] + sums[8:16], one)
            two = jnp.where(row8 == q, sums[16:24] + sums[24:32], two)
        at = pl.ds(j * 8, 8)
        inverse = col_inverse[at]
        rows_back[2 * core, at] = one * inverse
        rows_back[2 * core + 1, at] = two * inverse
        results(j).start()

    def full_remap(j, carry):
        remap(j, 8)
        return carry

    whole, last = tiles // 8, tiles % 8
    lax.fori_loop(0, whole, full_remap, 0)
    if last:
        remap(whole, last)
    leave5()
    for j in range(whole + (last > 0)):
        at = pl.ds(j * 8, 8)
        to_sibling(2 + j, rows_back.at[mine, at], rows_back.at[other, at]).wait_recv()
        for r in range(4):
            for t in range(8 * j, min(8 * j + 8, tiles)):
                out[r : r + 1, (2 * otiles + t) * TILE : (2 * otiles + t + 1) * TILE] = rows_back[r, t : t + 1]
    for j in range(whole + (last > 0)):
        results(j).wait_send()


def shards(atm_state, owners, ocean_tile, centroid_offset, remap_weight, ocean_state):
    ring = math.isqrt(lax.axis_size("cols"))
    samples = lax.axis_size("fld")
    cells = atm_state.shape[2]
    tiles = cells // TILE
    reach = owners.shape[1]
    ocells = ocean_state.shape[1]
    otiles = ocells // TILE
    chips = samples // 2
    slots = MOST * ring
    rows = ring * slots
    entries = reach * PAD
    hbm = pl.BlockSpec(memory_space=pltpu.HBM)
    vmem = pl.BlockSpec(memory_space=pltpu.VMEM)
    results = pl.pallas_call(
        functools.partial(kernel, ring, samples, tiles, reach, otiles),
        out_shape=pltpu.VMEM((4, 2 * ocells + cells), F32),
        in_specs=[hbm] * 6,
        out_specs=vmem,
        scratch_shapes=[
            pltpu.VMEM((4, 8, TILE), F32),
            pltpu.VMEM((4, PAD, TILE), F32),
            pltpu.VMEM(atm_state.shape, BF16),
            pltpu.VMEM((reach, tiles), I32),
            pltpu.VMEM((reach, tiles), I32),
            pltpu.VMEM((tiles, reach, TILE), F32),
            pltpu.VMEM((tiles, reach, TILE, TILE), BF16),
            pltpu.VMEM((4, ocells), F32),
            pltpu.VMEM((tiles + 2, FIELDS, TILE), F32),
            pltpu.VMEM(((FIELDS + 1) * entries, TILE), F32),
            pltpu.VMEM((rows, 2 * entries), BF16),
            pltpu.VMEM((entries, 2 * rows), BF16),
            pltpu.VMEM((ring * (slots + 2 * reach), 16 * ring), BF16),
            pltpu.VMEM((4, 8, TILE), F32),
            pltpu.VMEM((8, TILE), F32),
            pltpu.VMEM((PAD, TILE), F32),
            pltpu.VMEM((PAD // 8, 32, reach * TILE), BF16),
            pltpu.VMEM((ring, 8 + 2 * reach, TILE), F32),
            pltpu.VMEM((ring, 8 + 2 * reach, TILE), F32),
            pltpu.VMEM((2 * reach, TILE), F32),
            pltpu.VMEM((ring, 2 * reach, TILE), F32),
            pltpu.VMEM((ring, slots, TILE), F32),
            pltpu.VMEM((ring, slots, TILE), F32),
            pltpu.VMEM((2, ring, 4 * slots, TILE), I16),
            pltpu.VMEM((2, ring, 4 * slots, TILE), I16),
            pltpu.VMEM((ring, 8, TILE), F32),
            pltpu.VMEM((ring, 8, TILE), F32),
            pltpu.VMEM((ring, FIELDS * 8, TILE), I16),
            pltpu.VMEM((ring, FIELDS * 8, TILE), I16),
            pltpu.VMEM((4, 8, TILE), F32),
            pltpu.VMEM((2, 8, TILE), F32),
            pltpu.VMEM((2, 8, TILE), F32),
            pltpu.VMEM((chips, 2, 8, TILE), F32),
            pltpu.VMEM((2, 8, TILE), F32),
            pltpu.VMEM((ring, 2, 8, TILE), F32),
            pltpu.VMEM((ring, 2, slots, TILE), F32),
            pltpu.VMEM((ring, 2, slots, TILE), F32),
            pltpu.SemaphoreType.DMA((5,)),
            pltpu.SemaphoreType.DMA((tiles,)),
            pltpu.SemaphoreType.DMA((2,)),
            pltpu.SemaphoreType.DMA((2,)),
            pltpu.SemaphoreType.DMA((10,)),
            pltpu.SemaphoreType.DMA((10,)),
            pltpu.SemaphoreType.DMA((2 + PAD // 8,)),
            pltpu.SemaphoreType.DMA((2 + PAD // 8,)),
        ],
        compiler_params=pltpu.CompilerParams(
            collective_id=0, has_side_effects=True, vmem_limit_bytes=60 * 1024 * 1024
        ),
        name="coupling",
    )(atm_state, owners.T, ocean_tile.T, centroid_offset, remap_weight, ocean_state)
    return results[None, :, :ocells], results[:, ocells : 2 * ocells], results[:, 2 * ocells :]


def solution(mesh):
    return jax.shard_map(
        shards,
        mesh=mesh,
        in_specs=(
            P("fld", None, "cols"),
            P("cols", None),
            P("cols", None),
            P("cols", None, None),
            P("cols", None, None, None),
            P(None, "cols"),
        ),
        out_specs=(P("fld", None, "cols"), P(None, "cols"), P(None, "cols")),
        check_vma=False,
    )
```

```python
import functools
import math

import jax
import jax.numpy as jnp
from jax import lax
from jax.experimental import pallas as pl
from jax.experimental.pallas import tpu as pltpu
from jax.sharding import PartitionSpec as P

TILE = 128
FIELDS = 8
MOST = 3
PAD = 32
LEVELS = 5400.0
LEAST = 1e-30
MESH = pl.DeviceIdType.MESH
F32 = jnp.float32
BF16 = jnp.bfloat16
I32 = jnp.int32
I16 = jnp.int16


def split(x):
    high = x.astype(BF16)
    return high, (x - high.astype(F32)).astype(BF16)


def mixed(matrix, x):
    high, low = split(x)
    return jnp.dot(matrix, jnp.concatenate([high, low], axis=0), preferred_element_type=F32)


def twice(matrix):
    return jnp.concatenate([matrix, matrix], axis=1)


def kernel(
    ring, samples, tiles, reach, otiles,
    atm_hbm, owners_hbm, otile_hbm, cent_hbm, w_hbm, ocean_hbm,
    out,
    rows_next, rows_back, atm, owners, otile, cent, w, ocean,
    val, part, pick, pick_t, spread, oc, table, col_inverse, lhs,
    send0, recv0, ends_sent, ends_got, send1a, recv1a, send1, recv1, send2a, recv2a, send2, recv2,
    send3, recv3, send3y, recv3y, send4, recv4, send5, recv5,
    in_sem, w_sem, halo_send, halo_recv, ssem, rsem, psend, precv,
):
    cols = ring * ring
    chips = samples // 2
    slots = MOST * ring
    rows = ring * slots
    entries = reach * PAD
    ends = 2 * reach
    col = lax.axis_index("cols")
    fld = lax.axis_index("fld")
    x, z = col // ring, col % ring
    chip, core = fld // 2, fld % 2
    first = (1 - core) * x + core * z
    second = (1 - core) * z + core * x

    def on_first(p):
        return ((1 - core) * (p * ring + second) + core * (second * ring + p), fld)

    def on_second(p):
        return ((1 - core) * (first * ring + p) + core * (p * ring + first), fld)

    def on_chip(p):
        return (col, p * 2 + core)

    sibling = (col, chip * 2 + 1 - core)
    left, right = (col + cols - 1) % cols, (col + 1) % cols

    barrier = pltpu.get_barrier_semaphore()

    def greet(device):
        pl.semaphore_signal(barrier, inc=1, device_id=device, device_id_type=MESH)

    def far_first(count):
        return sorted(range(1, count), key=lambda d: -min(d, count - d))

    for d in far_first(ring):
        greet(on_first((first + d) % ring))
        greet(on_second((second + d) % ring))
    for d in far_first(chips):
        greet(on_chip((chip + d) % chips))
    greet((left, fld))
    greet((right, fld))
    greet(sibling)

    small = [
        pltpu.make_async_copy(source, target, in_sem.at[i])
        for i, (source, target) in enumerate(
            ((atm_hbm, atm), (owners_hbm, owners), (otile_hbm, otile), (cent_hbm, cent), (ocean_hbm, ocean))
        )
    ]
    for copy in small:
        copy.start()
    groups, rest = (tiles - 2) // 4, (tiles - 2) % 4
    spans = [(1 + 4 * c, 4) for c in range(groups)] + [(1 + 4 * groups, rest + 1), (0, 1)]

    def weights(c):
        at = pl.ds(*spans[c]) if isinstance(c, int) else pl.ds(1 + 4 * c, 4)
        return pltpu.make_async_copy(w_hbm.at[at], w.at[at], w_sem.at[c])

    for c in (groups + 1, groups, *range(groups)):
        weights(c).start()

    def exchange(stage, count, me, device, source, target):
        def send():
            for d in far_first(count):
                pltpu.make_async_remote_copy(
                    src_ref=source((me + d) % count),
                    dst_ref=target.at[me],
                    send_sem=ssem.at[stage],
                    recv_sem=rsem.at[stage],
                    device_id=device((me + d) % count),
                    device_id_type=MESH,
                ).start()

        others = target.at[pl.ds(0, count - 1)]
        everything = pltpu.make_async_remote_copy(
            src_ref=others, dst_ref=others, send_sem=ssem.at[stage], recv_sem=rsem.at[stage],
            device_id=device((me + 1) % count), device_id_type=MESH,
        )
        return send, everything.wait_recv, everything.wait_send

    def to_sibling(i, source, target):
        return pltpu.make_async_remote_copy(
            src_ref=source, dst_ref=target, send_sem=psend.at[i], recv_sem=precv.at[i],
            device_id=sibling, device_id_type=MESH,
        )

    part[...] = jnp.zeros_like(part)
    col_inverse[...] = jnp.ones_like(col_inverse)
    small[0].wait()
    for t in range(tiles):
        val[t + 1] = atm[0, :, t * TILE : (t + 1) * TILE].astype(F32)
    to_right = pltpu.make_async_remote_copy(
        src_ref=val.at[tiles], dst_ref=val.at[0], send_sem=halo_send.at[0], recv_sem=halo_recv.at[0],
        device_id=(right, fld), device_id_type=MESH,
    )
    to_left = pltpu.make_async_remote_copy(
        src_ref=val.at[1], dst_ref=val.at[tiles + 1], send_sem=halo_send.at[1], recv_sem=halo_recv.at[1],
        device_id=(left, fld), device_id_type=MESH,
    )
    small[1].wait()
    small[2].wait()
    lane = lax.broadcasted_iota(I32, (FIELDS, TILE), 1)

    def across(ref, fill):
        table[...] = jnp.full((8, TILE), fill, F32)
        table[:reach, :tiles] = ref[...].astype(F32)
        line = jnp.broadcast_to(table[0:1], (8, TILE))
        for k in range(1, reach):
            shifted = pltpu.roll(jnp.broadcast_to(table[k : k + 1], (8, TILE)), k * PAD, 1)
            line = jnp.where(lane >= k * PAD, shifted, line)
        return line[:1]

    owner_across = across(owners, float(cols))
    tile_across = across(otile, 0.0)
    owner_down = jnp.broadcast_to(owner_across, (entries, entries)).T
    at_row = lax.broadcasted_iota(I32, (entries, entries), 0)
    at_lane = lax.broadcasted_iota(I32, (entries, entries), 1)
    same = owner_down == owner_across
    rank_down = jnp.sum((same & (at_lane < at_row)).astype(F32), axis=1, keepdims=True).astype(I32)
    rank_across = jnp.sum((same & (at_row < at_lane)).astype(F32), axis=0, keepdims=True).astype(I32)

    def slot(owner, rank):
        owner = owner.astype(I32)
        high = owner // ring
        low = owner - high * ring
        group = (1 - core) * high + core * low
        place = (1 - core) * low + core * high
        return jnp.where(owner < cols, group * slots + rank * ring + place, -1)

    def place_of(owner):
        owner = owner.astype(I32)
        high = owner // ring
        low = owner - high * ring
        return (1 - core) * high + core * low, (1 - core) * low + core * high

    group_across, place_across = place_of(owner_across)
    group_down, place_down = place_of(owner_down)
    slot_across = jnp.where(owner_across < cols, group_across * slots + rank_across * ring + place_across, -1)
    seat_down = rank_down * ring + place_down
    slot_down = jnp.where(owner_down < cols, group_down * slots + seat_down, -1)[:, :1]
    pick_f = (lax.broadcasted_iota(I32, (rows, entries), 0) == slot_across).astype(F32)
    pick[...] = twice(pick_f.astype(BF16))
    pick_b = (lax.broadcasted_iota(I32, (entries, rows), 1) == slot_down).astype(F32).astype(BF16)
    pick_t[...] = twice(pick_b)

    stride = slots + ends
    per_line = TILE // stride
    base = (first % per_line) * stride
    ocean_row = place_across * 8 + tile_across.astype(I32) + 1
    group_row = lax.broadcasted_iota(I32, (8, entries), 0) == group_across
    marked = jnp.where(group_row & (owner_across < cols), ocean_row, 0).astype(F32).astype(BF16)
    tile_at, k_at = at_row % PAD, at_row // PAD
    seated = (at_lane == base + seat_down) & (owner_down < cols)
    seated = seated | (tile_at == 0) & (at_lane == base + slots + k_at)
    seated = seated | (tile_at == tiles - 1) & (at_lane == base + slots + reach + k_at)
    named = jnp.dot(marked, seated.astype(F32).astype(BF16), preferred_element_type=F32)
    line_of = lax.broadcasted_iota(I32, (8, TILE), 0) == first // per_line
    for g in range(ring):
        send0[g, :8] = jnp.where(line_of, named[g : g + 1], 0.0)
    send_named, arrive0, leave0 = exchange(0, ring, first, on_first, lambda p: send0.at[p], recv0)

    small[4].wait()
    for r in range(4):
        oc[r] = jnp.zeros((8, TILE), F32)
        for t in range(otiles):
            oc[r, t : t + 1, :] = ocean[r : r + 1, t * TILE : (t + 1) * TILE]

    small[3].wait()
    zeros = jnp.zeros((16, TILE), F32)
    row8 = lax.broadcasted_iota(I32, (8, TILE), 0)
    last_lane = TILE - 1
    extra = jnp.where(row8 == 0, 1.0, 0.0)
    extra = jnp.where((row8 == 1) & (lane == 0) | (row8 == 2) & (lane == last_lane), 1.0, extra)

    def rebuild(t, before, here, after):
        low = jnp.where(lane == 0, pltpu.roll(before, 1, 1), pltpu.roll(here, 1, 1))
        high = jnp.where(lane == last_lane, pltpu.roll(after, last_lane, 1), pltpu.roll(here, last_lane, 1))
        slope = 0.5 * (high - low)
        return [here + cent[t, k : k + 1, :] * slope for k in range(reach)]

    def tile_sums(t, rebuilt):
        operand, operator = [], []
        for k in range(reach):
            block = jnp.concatenate([rebuilt[k], extra], axis=0)
            operand.append(jnp.concatenate([zeros, block] if k % 2 else [block, zeros], axis=1))
        for k in range(0, reach, 2):
            operator.append(jnp.concatenate([w[t, k], w[t, k + 1]], axis=1))
        product = lax.dot_general(
            jnp.concatenate(operand, axis=0).astype(BF16), jnp.concatenate(operator, axis=0),
            (((1,), (1,)), ((), ())), preferred_element_type=F32,
        )
        for k in range(reach):
            sums = product[16 * k : 16 * k + 16, k // 2 * TILE : (k // 2 + 1) * TILE]
            area = sums[FIELDS : FIELDS + 1]
            code = jnp.round(sums[:FIELDS] * (LEVELS / jnp.maximum(area, LEAST)))
            part[pl.ds(k * PAD + t, FIELDS, stride=entries), :] = code
            part[pl.ds(FIELDS * entries + k * PAD + t, 1), :] = area
        return [product[16 * k : 16 * k + 16, k // 2 * TILE : (k // 2 + 1) * TILE] for k in range(reach)]

    def inner_sums(t):
        return tile_sums(t, rebuild(t, val[t], val[t + 1], val[t + 2]))

    def group_sums(c, carry):
        weights(c).wait()
        for q in range(4):
            inner_sums(1 + 4 * c + q)
        return carry

    weights(groups + 1).wait()
    here = val[1]
    cut = [jnp.where(lane == 0, 0.0, x) for x in rebuild(0, here, here, val[2])]
    low_weights = [x[FIELDS + 1 : FIELDS + 2] for x in tile_sums(0, cut)]
    weights(groups).wait()
    here = val[tiles]
    cut = [jnp.where(lane == last_lane, 0.0, x) for x in rebuild(tiles - 1, val[tiles - 1], here, here)]
    high_weights = [x[FIELDS + 2 : FIELDS + 3] for x in tile_sums(tiles - 1, cut)]
    end_weights = jnp.concatenate(low_weights + high_weights, axis=0)
    for g in range(ring):
        send0[g, 8:] = end_weights
    for q in range(rest):
        inner_sums(1 + 4 * groups + q)

    early = min(groups, 5)
    lax.fori_loop(0, early, group_sums, 0)
    pl.semaphore_wait(barrier, 3 + 2 * (ring - 1) + chips - 1)
    send_named()
    to_right.start()
    to_left.start()
    recv0[first] = send0[first]
    lax.fori_loop(early, groups, group_sums, 0)

    send, arrive1a, leave1a = exchange(1, ring, first, on_first, lambda p: send1a.at[p], recv1a)
    slotted = mixed(pick[...], part[FIELDS * entries :])
    for g in range(ring):
        send1a[g] = slotted[g * slots : (g + 1) * slots]
    send()
    sent1 = []
    for m in range(2):
        codes = [part[f * entries : (f + 1) * entries] for f in range(4 * m, 4 * m + 4)]
        codes = mixed(pick[...], jnp.concatenate(codes, axis=1))
        codes = [codes[:, i * TILE : (i + 1) * TILE] for i in range(4)]
        for g in range(ring):
            block = jnp.concatenate([x[g * slots : (g + 1) * slots] for x in codes], axis=0)
            send1[m, g] = block.astype(I32).astype(I16)
        send, *done = exchange(2 + m, ring, first, on_first, lambda p: send1.at[m, p], recv1.at[m])
        send()
        sent1.append(done)
    recv1a[first] = send1a[first]
    for m in range(2):
        recv1[m, first] = send1[m, first]

    to_right.wait_recv()
    to_left.wait_recv()
    end_values = jnp.zeros((8, TILE), F32)
    low = rebuild(0, val[0], val[1], val[2])
    high = rebuild(tiles - 1, val[tiles - 1], val[tiles], val[tiles + 1])
    for k in range(reach):
        moved = pltpu.roll(low[k], k, 1) if k else low[k]
        end_values = jnp.where(lane == k, moved, end_values)
        end_values = jnp.where(lane == reach + k, pltpu.roll(high[k], reach + 1 + k, 1), end_values)
    end_values = end_values.astype(BF16).astype(F32)
    ends_sent[...] = jnp.concatenate([end_values, jnp.zeros((TILE - 8, TILE), F32)], axis=0).T[:ends]
    send, arrive_ends, leave_ends = exchange(4, ring, first, on_first, lambda p: ends_sent, ends_got)
    send()
    ends_got[first] = ends_sent[...]

    arrive0()
    lines = jnp.zeros((8, TILE), F32)
    for p in range(ring):
        lines = lines + recv0[p, :8]
    want = (lax.broadcasted_iota(I32, (TILE, TILE), 0) + 1).astype(F32)
    member = [(want == lines[i : i + 1]).astype(F32) for i in range(-(-ring // per_line))]
    gather = jnp.concatenate(member, axis=1)[: 8 * ring, : ring * stride]
    gather = twice(gather.astype(BF16))
    back_rows = jnp.concatenate([x.T for x in member], axis=0)[: ring * stride, : 8 * ring]
    spread[...] = twice(back_rows.astype(BF16))
    end_weights = recv0[:, 8:] * LEVELS

    def stacked(of_slots, of_ends):
        return jnp.concatenate([of_slots, of_ends], axis=1).reshape(ring * stride, TILE)

    def column_area(c, carry):
        for q in range(chunk):
            t = c * chunk + q
            area = jnp.sum(w[t].reshape(reach * TILE, TILE).astype(F32), axis=0, keepdims=True)
            col_inverse[pl.ds(t, 1), :] = 1.0 / area
        return carry

    chunk = 4 if tiles % 4 == 0 else 1
    lax.fori_loop(0, tiles // chunk, column_area, 0)

    send, arrive2a, leave2a = exchange(5, ring, second, on_second, lambda p: send2a.at[p], recv2a)
    arrive1a()
    areas = recv1a[...]
    dense_area = mixed(gather, stacked(areas, jnp.zeros((ring, ends, TILE), F32)))
    send2a[...] = dense_area.reshape(ring, 8, TILE)
    send()
    recv2a[second] = send2a[second]
    per_area = 1.0 / jnp.maximum(dense_area, LEAST)
    arrive_ends()
    end_values = ends_got[...]
    sent2 = []
    for m in range(2):
        arrive, _ = sent1[m]
        arrive()
        block = recv1[m].astype(I32).astype(F32)
        sums = []
        for i in range(4):
            f = 4 * m + i
            field = block[:, i * slots : (i + 1) * slots] * areas
            sums.append(stacked(field, end_values[:, :, f : f + 1] * end_weights))
        dense = mixed(gather, jnp.concatenate(sums, axis=1))
        means = [(dense[:, i * TILE : (i + 1) * TILE] * per_area).reshape(ring, 8, TILE) for i in range(4)]
        send2[m] = jnp.round(jnp.concatenate(means, axis=1)).astype(I32).astype(I16)
        send, *done = exchange(6 + m, ring, second, on_second, lambda p: send2.at[m, p], recv2.at[m])
        send()
        sent2.append(done)
        recv2[m, second] = send2[m, second]
    arrive2a()

    coverage = jnp.zeros((8, TILE), F32)
    for p in range(ring):
        coverage = coverage + recv2a[p]
    per_coverage = 1.0 / (LEVELS * jnp.maximum(coverage, 1.0))

    def half_forcing(m):
        arrive, _ = sent2[m]
        arrive()
        total = jnp.zeros((4, 8, TILE), F32)
        for p in range(ring):
            total = total + recv2[m, p].astype(I32).astype(F32).reshape(4, 8, TILE) * recv2a[p][None]
        return total * per_coverage[None]

    def softplus(v):
        return jnp.maximum(v, 0.0) + jnp.log1p(jnp.exp(-jnp.abs(v)))

    sst, uo, vo = oc[0], oc[1], oc[2]
    insolation = 0.5 + 1.5 * fld.astype(F32) / (samples - 1)
    wind_u, wind_v, air, vapour = half_forcing(0)
    slip_u = wind_u - uo
    slip_v = wind_v - vo
    wind_speed = jnp.sqrt(slip_u * slip_u + slip_v * slip_v + 0.25)
    sensible = 0.4 * wind_speed * (sst - air)
    stress_u = 0.5 * wind_speed * slip_u
    stress_v = 0.5 * wind_speed * slip_v
    pressure, short, long, rain = half_forcing(1)
    saturation = 0.9 * jnp.exp(0.07 * sst - 0.1 * pressure)
    latent = 0.4 * wind_speed * (saturation - vapour)
    net_heat = insolation * softplus(short) + 0.3 * long - 0.1 * sst - sensible - latent
    freshwater = softplus(rain) - latent
    send3[0] = net_heat
    send3[1] = stress_u
    send3[2] = stress_v
    send3[3] = -freshwater

    mine, other = pl.ds(2 * core, 2), pl.ds(2 - 2 * core, 2)
    pair_copy = to_sibling(0, send3.at[other], recv3)
    pair_copy.start()
    pair_copy.wait_recv()
    send3y[...] = send3[mine] + recv3[...]
    send, arrive, leave3 = exchange(8, chips, chip, on_chip, lambda p: send3y, recv3y)
    send()
    recv3y[chip] = send3y[...]
    for i, flux in enumerate((stress_u, stress_v, net_heat, freshwater)):
        for t in range(otiles):
            out[i : i + 1, t * TILE : (t + 1) * TILE] = flux[t : t + 1]
    for leave in (leave0, leave1a, leave_ends, leave2a, to_right.wait_send, to_left.wait_send):
        leave()
    for _, leave in sent1 + sent2:
        leave()
    pair_copy.wait_send()
    arrive()
    flux_sum = recv3y[0]
    for p in range(1, chips):
        flux_sum = flux_sum + recv3y[p]
    state = oc[mine] + (0.5 / samples) * flux_sum
    send4[...] = state

    send, arrive, leave4 = exchange(9, ring, second, on_second, lambda p: send4, recv4)
    send()
    recv4[second] = state
    rows_next[mine] = state
    ocean_copy = to_sibling(1, rows_next.at[mine], rows_next.at[mine])
    ocean_copy.start()
    leave3()
    arrive()

    states = [recv4[:, r].reshape(ring * 8, TILE) for r in range(2)]
    slotted = mixed(spread[...], jnp.concatenate(states, axis=1))
    for p in range(ring):
        for r in range(2):
            send5[p, r] = slotted[p * stride : p * stride + slots, r * TILE : (r + 1) * TILE]
    send, arrive, leave5 = exchange(10, ring, first, on_first, lambda p: send5.at[p], recv5)
    send()
    recv5[first] = send5[first]
    to_sibling(1, rows_next.at[mine], rows_next.at[other]).wait_recv()
    for r in range(4):
        for t in range(otiles):
            out[r : r + 1, (otiles + t) * TILE : (otiles + t + 1) * TILE] = rows_next[r, t : t + 1]
    ocean_copy.wait_send()
    leave4()
    arrive()

    states = [recv5[:, r].reshape(rows, TILE) for r in range(2)]
    entry = mixed(pick_t[...], jnp.concatenate(states, axis=1))
    high, low = split(entry)
    high, low = high.astype(F32), low.astype(F32)
    for k in range(reach):
        for j in range(PAD // 8):
            at = slice(k * PAD + j * 8, k * PAD + j * 8 + 8)
            block = [high[at, :TILE], low[at, :TILE], high[at, TILE:], low[at, TILE:]]
            lhs[j, :, k * TILE : (k + 1) * TILE] = jnp.concatenate(block, axis=0).astype(BF16)


    def results(j):
        at = pl.ds(j * 8, 8)
        return to_sibling(2 + j, rows_back.at[mine, at], rows_back.at[mine, at])

    def remap(j, count):
        operand = lhs[j]
        one = two = jnp.zeros((8, TILE), F32)
        for q in range(count):
            sums = jnp.dot(operand, w[j * 8 + q].reshape(reach * TILE, TILE), preferred_element_type=F32)
            one = jnp.where(row8 == q, sums[0:8] + sums[8:16], one)
            two = jnp.where(row8 == q, sums[16:24] + sums[24:32], two)
        at = pl.ds(j * 8, 8)
        inverse = col_inverse[at]
        rows_back[2 * core, at] = one * inverse
        rows_back[2 * core + 1, at] = two * inverse
        results(j).start()

    def full_remap(j, carry):
        remap(j, 8)
        return carry

    whole, last = tiles // 8, tiles % 8
    lax.fori_loop(0, whole, full_remap, 0)
    if last:
        remap(whole, last)
    leave5()
    for j in range(whole + (last > 0)):
        at = pl.ds(j * 8, 8)
        to_sibling(2 + j, rows_back.at[mine, at], rows_back.at[other, at]).wait_recv()
        for r in range(4):
            for t in range(8 * j, min(8 * j + 8, tiles)):
                out[r : r + 1, (2 * otiles + t) * TILE : (2 * otiles + t + 1) * TILE] = rows_back[r, t : t + 1]
    for j in range(whole + (last > 0)):
        results(j).wait_send()


def shards(atm_state, owners, ocean_tile, centroid_offset, remap_weight, ocean_state):
    ring = math.isqrt(lax.axis_size("cols"))
    samples = lax.axis_size("fld")
    cells = atm_state.shape[2]
    tiles = cells // TILE
    reach = owners.shape[1]
    ocells = ocean_state.shape[1]
    otiles = ocells // TILE
    chips = samples // 2
    slots = MOST * ring
    rows = ring * slots
    entries = reach * PAD
    hbm = pl.BlockSpec(memory_space=pltpu.HBM)
    vmem = pl.BlockSpec(memory_space=pltpu.VMEM)
    results = pl.pallas_call(
        functools.partial(kernel, ring, samples, tiles, reach, otiles),
        out_shape=pltpu.VMEM((4, 2 * ocells + cells), F32),
        in_specs=[hbm] * 6,
        out_specs=vmem,
        scratch_shapes=[
            pltpu.VMEM((4, 8, TILE), F32),
            pltpu.VMEM((4, PAD, TILE), F32),
            pltpu.VMEM(atm_state.shape, BF16),
            pltpu.VMEM((reach, tiles), I32),
            pltpu.VMEM((reach, tiles), I32),
            pltpu.VMEM((tiles, reach, TILE), F32),
            pltpu.VMEM((tiles, reach, TILE, TILE), BF16),
            pltpu.VMEM((4, ocells), F32),
            pltpu.VMEM((tiles + 2, FIELDS, TILE), F32),
            pltpu.VMEM(((FIELDS + 1) * entries, TILE), F32),
            pltpu.VMEM((rows, 2 * entries), BF16),
            pltpu.VMEM((entries, 2 * rows), BF16),
            pltpu.VMEM((ring * (slots + 2 * reach), 16 * ring), BF16),
            pltpu.VMEM((4, 8, TILE), F32),
            pltpu.VMEM((8, TILE), F32),
            pltpu.VMEM((PAD, TILE), F32),
            pltpu.VMEM((PAD // 8, 32, reach * TILE), BF16),
            pltpu.VMEM((ring, 8 + 2 * reach, TILE), F32),
            pltpu.VMEM((ring, 8 + 2 * reach, TILE), F32),
            pltpu.VMEM((2 * reach, TILE), F32),
            pltpu.VMEM((ring, 2 * reach, TILE), F32),
            pltpu.VMEM((ring, slots, TILE), F32),
            pltpu.VMEM((ring, slots, TILE), F32),
            pltpu.VMEM((2, ring, 4 * slots, TILE), I16),
            pltpu.VMEM((2, ring, 4 * slots, TILE), I16),
            pltpu.VMEM((ring, 8, TILE), F32),
            pltpu.VMEM((ring, 8, TILE), F32),
            pltpu.VMEM((2, ring, 4 * 8, TILE), I16),
            pltpu.VMEM((2, ring, 4 * 8, TILE), I16),
            pltpu.VMEM((4, 8, TILE), F32),
            pltpu.VMEM((2, 8, TILE), F32),
            pltpu.VMEM((2, 8, TILE), F32),
            pltpu.VMEM((chips, 2, 8, TILE), F32),
            pltpu.VMEM((2, 8, TILE), F32),
            pltpu.VMEM((ring, 2, 8, TILE), F32),
            pltpu.VMEM((ring, 2, slots, TILE), F32),
            pltpu.VMEM((ring, 2, slots, TILE), F32),
            pltpu.SemaphoreType.DMA((5,)),
            pltpu.SemaphoreType.DMA((tiles,)),
            pltpu.SemaphoreType.DMA((2,)),
            pltpu.SemaphoreType.DMA((2,)),
            pltpu.SemaphoreType.DMA((11,)),
            pltpu.SemaphoreType.DMA((11,)),
            pltpu.SemaphoreType.DMA((2 + PAD // 8,)),
            pltpu.SemaphoreType.DMA((2 + PAD // 8,)),
        ],
        compiler_params=pltpu.CompilerParams(
            collective_id=0, has_side_effects=True, vmem_limit_bytes=60 * 1024 * 1024
        ),
        name="coupling",
    )(atm_state, owners.T, ocean_tile.T, centroid_offset, remap_weight, ocean_state)
    return results[None, :, :ocells], results[:, ocells : 2 * ocells], results[:, 2 * ocells :]


def solution(mesh):
    return jax.shard_map(
        shards,
        mesh=mesh,
        in_specs=(
            P("fld", None, "cols"),
            P("cols", None),
            P("cols", None),
            P("cols", None, None),
            P("cols", None, None, None),
            P(None, "cols"),
        ),
        out_specs=(P("fld", None, "cols"), P(None, "cols"), P(None, "cols")),
        check_vma=False,
    )
```

```python
import functools
import math

import jax
import jax.numpy as jnp
from jax import lax
from jax.experimental import pallas as pl
from jax.experimental.pallas import tpu as pltpu
from jax.sharding import PartitionSpec as P

TILE = 128
FIELDS = 8
MOST = 3
PAD = 32
LEVELS = 5400.0
LEAST = 1e-30
SMALLEST = 2.0**-24
STEP = 31.0 * math.log(2.0) / 65534.0
MIDDLE = -8.5 * math.log(2.0)
MESH = pl.DeviceIdType.MESH
F32 = jnp.float32
BF16 = jnp.bfloat16
I32 = jnp.int32
I16 = jnp.int16


def split(x):
    high = x.astype(BF16)
    return high, (x - high.astype(F32)).astype(BF16)


def mixed(matrix, x):
    high, low = split(x)
    return jnp.dot(matrix, jnp.concatenate([high, low], axis=0), preferred_element_type=F32)


def twice(matrix):
    return jnp.concatenate([matrix, matrix], axis=1)


def kernel(
    ring, samples, tiles, reach, otiles,
    atm_hbm, owners_hbm, otile_hbm, cent_hbm, w_hbm, ocean_hbm,
    out,
    rows_next, rows_back, atm, owners, otile, cent, w, ocean,
    val, part, pick, pick_t, spread, oc, table, col_inverse, lhs,
    send0, recv0, ends_sent, ends_got, send1a, recv1a, send1, recv1, send2a, recv2a, send2, recv2,
    send3, recv3, send3y, recv3y, send4, recv4, send5, recv5,
    in_sem, w_sem, halo_send, halo_recv, ssem, rsem, psend, precv,
):
    cols = ring * ring
    chips = samples // 2
    slots = MOST * ring
    rows = ring * slots
    entries = reach * PAD
    ends = 2 * reach
    col = lax.axis_index("cols")
    fld = lax.axis_index("fld")
    x, z = col // ring, col % ring
    chip, core = fld // 2, fld % 2
    first = (1 - core) * x + core * z
    second = (1 - core) * z + core * x

    def on_first(p):
        return ((1 - core) * (p * ring + second) + core * (second * ring + p), fld)

    def on_second(p):
        return ((1 - core) * (first * ring + p) + core * (p * ring + first), fld)

    def on_chip(p):
        return (col, p * 2 + core)

    sibling = (col, chip * 2 + 1 - core)
    left, right = (col + cols - 1) % cols, (col + 1) % cols

    barrier = pltpu.get_barrier_semaphore()

    def greet(device):
        pl.semaphore_signal(barrier, inc=1, device_id=device, device_id_type=MESH)

    def far_first(count):
        return sorted(range(1, count), key=lambda d: -min(d, count - d))

    def greet_all(far):
        for d in far_first(ring):
            if (min(d, ring - d) >= 3) == far:
                greet(on_first((first + d) % ring))
                greet(on_second((second + d) % ring))
        for d in far_first(chips):
            if (min(d, chips - d) >= 3) == far:
                greet(on_chip((chip + d) % chips))

    greet_all(True)

    small = [
        pltpu.make_async_copy(source, target, in_sem.at[i])
        for i, (source, target) in enumerate(
            ((atm_hbm, atm), (owners_hbm, owners), (otile_hbm, otile), (cent_hbm, cent), (ocean_hbm, ocean))
        )
    ]
    for copy in small:
        copy.start()
    groups, rest = (tiles - 2) // 4, (tiles - 2) % 4
    spans = [(1 + 4 * c, 4) for c in range(groups)] + [(1 + 4 * groups, rest + 1), (0, 1)]

    def weights(c):
        at = pl.ds(*spans[c]) if isinstance(c, int) else pl.ds(1 + 4 * c, 4)
        return pltpu.make_async_copy(w_hbm.at[at], w.at[at], w_sem.at[c])

    for c in (groups + 1, groups, *range(groups)):
        weights(c).start()

    greet_all(False)
    greet((left, fld))
    greet((right, fld))
    greet(sibling)

    def exchange(stage, count, me, device, source, target):
        def send():
            for d in far_first(count):
                pltpu.make_async_remote_copy(
                    src_ref=source((me + d) % count),
                    dst_ref=target.at[me],
                    send_sem=ssem.at[stage],
                    recv_sem=rsem.at[stage],
                    device_id=device((me + d) % count),
                    device_id_type=MESH,
                ).start()

        others = target.at[pl.ds(0, count - 1)]
        everything = pltpu.make_async_remote_copy(
            src_ref=others, dst_ref=others, send_sem=ssem.at[stage], recv_sem=rsem.at[stage],
            device_id=device((me + 1) % count), device_id_type=MESH,
        )
        return send, everything.wait_recv, everything.wait_send

    def to_sibling(i, source, target):
        return pltpu.make_async_remote_copy(
            src_ref=source, dst_ref=target, send_sem=psend.at[i], recv_sem=precv.at[i],
            device_id=sibling, device_id_type=MESH,
        )

    part[...] = jnp.zeros_like(part)
    col_inverse[...] = jnp.ones_like(col_inverse)
    small[0].wait()
    for t in range(tiles):
        val[t + 1] = atm[0, :, t * TILE : (t + 1) * TILE].astype(F32)
    to_right = pltpu.make_async_remote_copy(
        src_ref=val.at[tiles], dst_ref=val.at[0], send_sem=halo_send.at[0], recv_sem=halo_recv.at[0],
        device_id=(right, fld), device_id_type=MESH,
    )
    to_left = pltpu.make_async_remote_copy(
        src_ref=val.at[1], dst_ref=val.at[tiles + 1], send_sem=halo_send.at[1], recv_sem=halo_recv.at[1],
        device_id=(left, fld), device_id_type=MESH,
    )
    small[1].wait()
    small[2].wait()
    lane = lax.broadcasted_iota(I32, (FIELDS, TILE), 1)

    def across(ref, fill):
        table[...] = jnp.full((8, TILE), fill, F32)
        table[:reach, :tiles] = ref[...].astype(F32)
        line = jnp.broadcast_to(table[0:1], (8, TILE))
        for k in range(1, reach):
            shifted = pltpu.roll(jnp.broadcast_to(table[k : k + 1], (8, TILE)), k * PAD, 1)
            line = jnp.where(lane >= k * PAD, shifted, line)
        return line[:1]

    owner_across = across(owners, float(cols))
    tile_across = across(otile, 0.0)
    owner_down = jnp.broadcast_to(owner_across, (entries, entries)).T
    at_row = lax.broadcasted_iota(I32, (entries, entries), 0)
    at_lane = lax.broadcasted_iota(I32, (entries, entries), 1)
    same = owner_down == owner_across
    rank_down = jnp.sum((same & (at_lane < at_row)).astype(F32), axis=1, keepdims=True).astype(I32)
    rank_across = jnp.sum((same & (at_row < at_lane)).astype(F32), axis=0, keepdims=True).astype(I32)

    def slot(owner, rank):
        owner = owner.astype(I32)
        high = owner // ring
        low = owner - high * ring
        group = (1 - core) * high + core * low
        place = (1 - core) * low + core * high
        return jnp.where(owner < cols, group * slots + rank * ring + place, -1)

    def place_of(owner):
        owner = owner.astype(I32)
        high = owner // ring
        low = owner - high * ring
        return (1 - core) * high + core * low, (1 - core) * low + core * high

    group_across, place_across = place_of(owner_across)
    group_down, place_down = place_of(owner_down)
    slot_across = jnp.where(owner_across < cols, group_across * slots + rank_across * ring + place_across, -1)
    seat_down = rank_down * ring + place_down
    slot_down = jnp.where(owner_down < cols, group_down * slots + seat_down, -1)[:, :1]
    pick_f = (lax.broadcasted_iota(I32, (rows, entries), 0) == slot_across).astype(F32)
    pick[...] = twice(pick_f.astype(BF16))
    pick_b = (lax.broadcasted_iota(I32, (entries, rows), 1) == slot_down).astype(F32).astype(BF16)
    pick_t[...] = twice(pick_b)

    stride = slots + ends
    per_line = TILE // stride
    base = (first % per_line) * stride
    ocean_row = place_across * 8 + tile_across.astype(I32) + 1
    group_row = lax.broadcasted_iota(I32, (8, entries), 0) == group_across
    marked = jnp.where(group_row & (owner_across < cols), ocean_row, 0).astype(F32).astype(BF16)
    tile_at, k_at = at_row % PAD, at_row // PAD
    seated = (at_lane == base + seat_down) & (owner_down < cols)
    seated = seated | (tile_at == 0) & (at_lane == base + slots + k_at)
    seated = seated | (tile_at == tiles - 1) & (at_lane == base + slots + reach + k_at)
    named = jnp.dot(marked, seated.astype(F32).astype(BF16), preferred_element_type=F32)
    line_of = lax.broadcasted_iota(I32, (8, TILE), 0) == first // per_line
    for g in range(ring):
        send0[g, :8] = jnp.where(line_of, named[g : g + 1], 0.0)
    send_named, arrive0, leave0 = exchange(0, ring, first, on_first, lambda p: send0.at[p], recv0)

    small[4].wait()
    for r in range(4):
        oc[r] = jnp.zeros((8, TILE), F32)
        for t in range(otiles):
            oc[r, t : t + 1, :] = ocean[r : r + 1, t * TILE : (t + 1) * TILE]

    small[3].wait()
    zeros = jnp.zeros((16, TILE), F32)
    row8 = lax.broadcasted_iota(I32, (8, TILE), 0)
    last_lane = TILE - 1
    extra = jnp.where(row8 == 0, 1.0, 0.0)
    extra = jnp.where((row8 == 1) & (lane == 0) | (row8 == 2) & (lane == last_lane), 1.0, extra)

    def rebuild(t, before, here, after):
        low = jnp.where(lane == 0, pltpu.roll(before, 1, 1), pltpu.roll(here, 1, 1))
        high = jnp.where(lane == last_lane, pltpu.roll(after, last_lane, 1), pltpu.roll(here, last_lane, 1))
        slope = 0.5 * (high - low)
        return [here + cent[t, k : k + 1, :] * slope for k in range(reach)]

    def tile_sums(t, rebuilt):
        operand, operator = [], []
        for k in range(reach):
            block = jnp.concatenate([rebuilt[k], extra], axis=0)
            operand.append(jnp.concatenate([zeros, block] if k % 2 else [block, zeros], axis=1))
        for k in range(0, reach, 2):
            operator.append(jnp.concatenate([w[t, k], w[t, k + 1]], axis=1))
        product = lax.dot_general(
            jnp.concatenate(operand, axis=0).astype(BF16), jnp.concatenate(operator, axis=0),
            (((1,), (1,)), ((), ())), preferred_element_type=F32,
        )
        for k in range(reach):
            sums = product[16 * k : 16 * k + 16, k // 2 * TILE : (k // 2 + 1) * TILE]
            part[pl.ds(k * PAD + t, FIELDS, stride=entries), :] = sums[:FIELDS]
            part[pl.ds(FIELDS * entries + k * PAD + t, 1), :] = sums[FIELDS : FIELDS + 1]
        return [product[16 * k : 16 * k + 16, k // 2 * TILE : (k // 2 + 1) * TILE] for k in range(reach)]

    def inner_sums(t):
        return tile_sums(t, rebuild(t, val[t], val[t + 1], val[t + 2]))

    def group_sums(c, carry):
        weights(c).wait()
        for q in range(4):
            inner_sums(1 + 4 * c + q)
        return carry

    weights(groups + 1).wait()
    here = val[1]
    cut = [jnp.where(lane == 0, 0.0, x) for x in rebuild(0, here, here, val[2])]
    low_weights = [x[FIELDS + 1 : FIELDS + 2] for x in tile_sums(0, cut)]
    weights(groups).wait()
    here = val[tiles]
    cut = [jnp.where(lane == last_lane, 0.0, x) for x in rebuild(tiles - 1, val[tiles - 1], here, here)]
    high_weights = [x[FIELDS + 2 : FIELDS + 3] for x in tile_sums(tiles - 1, cut)]
    end_weights = jnp.concatenate(low_weights + high_weights, axis=0)
    for g in range(ring):
        send0[g, 8:] = end_weights
    for q in range(rest):
        inner_sums(1 + 4 * groups + q)

    early = min(groups, 5)
    lax.fori_loop(0, early, group_sums, 0)
    pl.semaphore_wait(barrier, 3 + 2 * (ring - 1) + chips - 1)
    send_named()
    to_right.start()
    to_left.start()
    recv0[first] = send0[first]
    lax.fori_loop(early, groups, group_sums, 0)

    area_code = jnp.maximum(part[FIELDS * entries :], SMALLEST)
    area_code = jnp.round((jnp.log(area_code) - MIDDLE) * (1.0 / STEP))
    area_code = jnp.clip(area_code, -32767.0, 32767.0)
    scale = LEVELS / jnp.exp(area_code * STEP + MIDDLE)
    sent1 = []
    for m, (source, target) in enumerate(((send1a, recv1a), (send1, recv1))):
        codes = [jnp.round(part[f * entries : (f + 1) * entries] * scale) for f in range(4 * m, 4 * m + 4)]
        if m == 0:
            codes.append(area_code)
        count = len(codes)
        codes = mixed(pick[...], jnp.concatenate(codes, axis=1))
        codes = [codes[:, i * TILE : (i + 1) * TILE] for i in range(count)]
        for g in range(ring):
            block = [x[g * slots : (g + 1) * slots] for x in codes]
            if source.shape[1] > count * slots:
                block.append(jnp.zeros((source.shape[1] - count * slots, TILE), F32))
            source[g] = jnp.concatenate(block, axis=0).astype(I32).astype(I16)
        send, *done = exchange(1 + m, ring, first, on_first, lambda p: source.at[p], target)
        send()
        sent1.append(done)
    recv1a[first] = send1a[first]
    recv1[first] = send1[first]

    to_right.wait_recv()
    to_left.wait_recv()
    end_values = jnp.zeros((8, TILE), F32)
    low = rebuild(0, val[0], val[1], val[2])
    high = rebuild(tiles - 1, val[tiles - 1], val[tiles], val[tiles + 1])
    for k in range(reach):
        moved = pltpu.roll(low[k], k, 1) if k else low[k]
        end_values = jnp.where(lane == k, moved, end_values)
        end_values = jnp.where(lane == reach + k, pltpu.roll(high[k], reach + 1 + k, 1), end_values)
    end_values = end_values.astype(BF16).astype(F32)
    ends_sent[...] = jnp.concatenate([end_values, jnp.zeros((TILE - 8, TILE), F32)], axis=0).T[:ends]
    send, arrive_ends, leave_ends = exchange(4, ring, first, on_first, lambda p: ends_sent, ends_got)
    send()
    ends_got[first] = ends_sent[...]

    arrive0()
    lines = jnp.zeros((8, TILE), F32)
    for p in range(ring):
        lines = lines + recv0[p, :8]
    want = (lax.broadcasted_iota(I32, (TILE, TILE), 0) + 1).astype(F32)
    member = [(want == lines[i : i + 1]).astype(F32) for i in range(-(-ring // per_line))]
    gather = jnp.concatenate(member, axis=1)[: 8 * ring, : ring * stride]
    gather = twice(gather.astype(BF16))
    back_rows = jnp.concatenate([x.T for x in member], axis=0)[: ring * stride, : 8 * ring]
    spread[...] = twice(back_rows.astype(BF16))
    end_weights = recv0[:, 8:] * LEVELS

    def stacked(of_slots, of_ends):
        return jnp.concatenate([of_slots, of_ends], axis=1).reshape(ring * stride, TILE)

    def column_area(c, carry):
        for q in range(chunk):
            t = c * chunk + q
            area = jnp.sum(w[t].reshape(reach * TILE, TILE).astype(F32), axis=0, keepdims=True)
            col_inverse[pl.ds(t, 1), :] = 1.0 / area
        return carry

    chunk = 4 if tiles % 4 == 0 else 1
    lax.fori_loop(0, tiles // chunk, column_area, 0)

    send, arrive2a, leave2a = exchange(5, ring, second, on_second, lambda p: send2a.at[p], recv2a)
    sent1[0][0]()
    codes1 = recv1a[...].astype(I32).astype(F32)
    areas = jnp.exp(codes1[:, 4 * slots : 5 * slots] * STEP + MIDDLE)
    dense_area = mixed(gather, stacked(areas, jnp.zeros((ring, ends, TILE), F32)))
    send2a[...] = dense_area.reshape(ring, 8, TILE)
    send()
    recv2a[second] = send2a[second]
    per_area = 1.0 / jnp.maximum(dense_area, LEAST)
    arrive_ends()
    end_values = ends_got[...]
    sent2 = []
    for m in range(2):
        if m == 1:
            sent1[1][0]()
            codes1 = recv1[...].astype(I32).astype(F32)
        sums = []
        for i in range(4):
            f = 4 * m + i
            field = codes1[:, i * slots : (i + 1) * slots] * areas
            sums.append(stacked(field, end_values[:, :, f : f + 1] * end_weights))
        dense = mixed(gather, jnp.concatenate(sums, axis=1))
        means = [(dense[:, i * TILE : (i + 1) * TILE] * per_area).reshape(ring, 8, TILE) for i in range(4)]
        send2[m] = jnp.round(jnp.concatenate(means, axis=1)).astype(I32).astype(I16)
        send, *done = exchange(6 + m, ring, second, on_second, lambda p: send2.at[m, p], recv2.at[m])
        send()
        sent2.append(done)
        recv2[m, second] = send2[m, second]
    arrive2a()

    coverage = jnp.zeros((8, TILE), F32)
    for p in range(ring):
        coverage = coverage + recv2a[p]
    per_coverage = 1.0 / (LEVELS * jnp.maximum(coverage, 1.0))

    def half_forcing(m):
        arrive, _ = sent2[m]
        arrive()
        total = jnp.zeros((4, 8, TILE), F32)
        for p in range(ring):
            total = total + recv2[m, p].astype(I32).astype(F32).reshape(4, 8, TILE) * recv2a[p][None]
        return total * per_coverage[None]

    def softplus(v):
        return jnp.maximum(v, 0.0) + jnp.log1p(jnp.exp(-jnp.abs(v)))

    sst, uo, vo = oc[0], oc[1], oc[2]
    insolation = 0.5 + 1.5 * fld.astype(F32) / (samples - 1)
    wind_u, wind_v, air, vapour = half_forcing(0)
    slip_u = wind_u - uo
    slip_v = wind_v - vo
    wind_speed = jnp.sqrt(slip_u * slip_u + slip_v * slip_v + 0.25)
    sensible = 0.4 * wind_speed * (sst - air)
    stress_u = 0.5 * wind_speed * slip_u
    stress_v = 0.5 * wind_speed * slip_v
    pressure, short, long, rain = half_forcing(1)
    saturation = 0.9 * jnp.exp(0.07 * sst - 0.1 * pressure)
    latent = 0.4 * wind_speed * (saturation - vapour)
    net_heat = insolation * softplus(short) + 0.3 * long - 0.1 * sst - sensible - latent
    freshwater = softplus(rain) - latent
    send3[0] = net_heat
    send3[1] = stress_u
    send3[2] = stress_v
    send3[3] = -freshwater

    mine, other = pl.ds(2 * core, 2), pl.ds(2 - 2 * core, 2)
    pair_copy = to_sibling(0, send3.at[other], recv3)
    pair_copy.start()
    pair_copy.wait_recv()
    send3y[...] = send3[mine] + recv3[...]
    send, arrive, leave3 = exchange(8, chips, chip, on_chip, lambda p: send3y, recv3y)
    send()
    recv3y[chip] = send3y[...]
    for i, flux in enumerate((stress_u, stress_v, net_heat, freshwater)):
        for t in range(otiles):
            out[i : i + 1, t * TILE : (t + 1) * TILE] = flux[t : t + 1]
    for leave in (leave0, leave_ends, leave2a, to_right.wait_send, to_left.wait_send):
        leave()
    for _, leave in sent1 + sent2:
        leave()
    pair_copy.wait_send()
    arrive()
    flux_sum = recv3y[0]
    for p in range(1, chips):
        flux_sum = flux_sum + recv3y[p]
    state = oc[mine] + (0.5 / samples) * flux_sum
    send4[...] = state

    send, arrive, leave4 = exchange(9, ring, second, on_second, lambda p: send4, recv4)
    send()
    recv4[second] = state
    rows_next[mine] = state
    ocean_copy = to_sibling(1, rows_next.at[mine], rows_next.at[mine])
    ocean_copy.start()
    leave3()
    arrive()

    states = [recv4[:, r].reshape(ring * 8, TILE) for r in range(2)]
    slotted = mixed(spread[...], jnp.concatenate(states, axis=1))
    for p in range(ring):
        for r in range(2):
            send5[p, r] = slotted[p * stride : p * stride + slots, r * TILE : (r + 1) * TILE]
    send, arrive, leave5 = exchange(10, ring, first, on_first, lambda p: send5.at[p], recv5)
    send()
    recv5[first] = send5[first]
    to_sibling(1, rows_next.at[mine], rows_next.at[other]).wait_recv()
    for r in range(4):
        for t in range(otiles):
            out[r : r + 1, (otiles + t) * TILE : (otiles + t + 1) * TILE] = rows_next[r, t : t + 1]
    ocean_copy.wait_send()
    leave4()
    arrive()

    states = [recv5[:, r].reshape(rows, TILE) for r in range(2)]
    entry = mixed(pick_t[...], jnp.concatenate(states, axis=1))
    high, low = split(entry)
    high, low = high.astype(F32), low.astype(F32)
    for k in range(reach):
        for j in range(PAD // 8):
            at = slice(k * PAD + j * 8, k * PAD + j * 8 + 8)
            block = [high[at, :TILE], low[at, :TILE], high[at, TILE:], low[at, TILE:]]
            lhs[j, :, k * TILE : (k + 1) * TILE] = jnp.concatenate(block, axis=0).astype(BF16)


    def results(j):
        at = pl.ds(j * 8, 8)
        return to_sibling(2 + j, rows_back.at[mine, at], rows_back.at[mine, at])

    def remap(j, count):
        operand = lhs[j]
        one = two = jnp.zeros((8, TILE), F32)
        for q in range(count):
            sums = jnp.dot(operand, w[j * 8 + q].reshape(reach * TILE, TILE), preferred_element_type=F32)
            one = jnp.where(row8 == q, sums[0:8] + sums[8:16], one)
            two = jnp.where(row8 == q, sums[16:24] + sums[24:32], two)
        at = pl.ds(j * 8, 8)
        inverse = col_inverse[at]
        rows_back[2 * core, at] = one * inverse
        rows_back[2 * core + 1, at] = two * inverse
        results(j).start()

    def full_remap(j, carry):
        remap(j, 8)
        return carry

    whole, last = tiles // 8, tiles % 8
    lax.fori_loop(0, whole, full_remap, 0)
    if last:
        remap(whole, last)
    leave5()
    for j in range(whole + (last > 0)):
        at = pl.ds(j * 8, 8)
        to_sibling(2 + j, rows_back.at[mine, at], rows_back.at[other, at]).wait_recv()
        for r in range(4):
            for t in range(8 * j, min(8 * j + 8, tiles)):
                out[r : r + 1, (2 * otiles + t) * TILE : (2 * otiles + t + 1) * TILE] = rows_back[r, t : t + 1]
    for j in range(whole + (last > 0)):
        results(j).wait_send()


def shards(atm_state, owners, ocean_tile, centroid_offset, remap_weight, ocean_state):
    ring = math.isqrt(lax.axis_size("cols"))
    samples = lax.axis_size("fld")
    cells = atm_state.shape[2]
    tiles = cells // TILE
    reach = owners.shape[1]
    ocells = ocean_state.shape[1]
    otiles = ocells // TILE
    chips = samples // 2
    slots = MOST * ring
    rows = ring * slots
    entries = reach * PAD
    hbm = pl.BlockSpec(memory_space=pltpu.HBM)
    vmem = pl.BlockSpec(memory_space=pltpu.VMEM)
    results = pl.pallas_call(
        functools.partial(kernel, ring, samples, tiles, reach, otiles),
        out_shape=pltpu.VMEM((4, 2 * ocells + cells), F32),
        in_specs=[hbm] * 6,
        out_specs=vmem,
        scratch_shapes=[
            pltpu.VMEM((4, 8, TILE), F32),
            pltpu.VMEM((4, PAD, TILE), F32),
            pltpu.VMEM(atm_state.shape, BF16),
            pltpu.VMEM((reach, tiles), I32),
            pltpu.VMEM((reach, tiles), I32),
            pltpu.VMEM((tiles, reach, TILE), F32),
            pltpu.VMEM((tiles, reach, TILE, TILE), BF16),
            pltpu.VMEM((4, ocells), F32),
            pltpu.VMEM((tiles + 2, FIELDS, TILE), F32),
            pltpu.VMEM(((FIELDS + 1) * entries, TILE), F32),
            pltpu.VMEM((rows, 2 * entries), BF16),
            pltpu.VMEM((entries, 2 * rows), BF16),
            pltpu.VMEM((ring * (slots + 2 * reach), 16 * ring), BF16),
            pltpu.VMEM((4, 8, TILE), F32),
            pltpu.VMEM((8, TILE), F32),
            pltpu.VMEM((PAD, TILE), F32),
            pltpu.VMEM((PAD // 8, 32, reach * TILE), BF16),
            pltpu.VMEM((ring, 8 + 2 * reach, TILE), F32),
            pltpu.VMEM((ring, 8 + 2 * reach, TILE), F32),
            pltpu.VMEM((2 * reach, TILE), F32),
            pltpu.VMEM((ring, 2 * reach, TILE), F32),
            pltpu.VMEM((ring, -(-5 * slots // 16) * 16, TILE), I16),
            pltpu.VMEM((ring, -(-5 * slots // 16) * 16, TILE), I16),
            pltpu.VMEM((ring, 4 * slots, TILE), I16),
            pltpu.VMEM((ring, 4 * slots, TILE), I16),
            pltpu.VMEM((ring, 8, TILE), F32),
            pltpu.VMEM((ring, 8, TILE), F32),
            pltpu.VMEM((2, ring, 4 * 8, TILE), I16),
            pltpu.VMEM((2, ring, 4 * 8, TILE), I16),
            pltpu.VMEM((4, 8, TILE), F32),
            pltpu.VMEM((2, 8, TILE), F32),
            pltpu.VMEM((2, 8, TILE), F32),
            pltpu.VMEM((chips, 2, 8, TILE), F32),
            pltpu.VMEM((2, 8, TILE), F32),
            pltpu.VMEM((ring, 2, 8, TILE), F32),
            pltpu.VMEM((ring, 2, slots, TILE), F32),
            pltpu.VMEM((ring, 2, slots, TILE), F32),
            pltpu.SemaphoreType.DMA((5,)),
            pltpu.SemaphoreType.DMA((tiles,)),
            pltpu.SemaphoreType.DMA((2,)),
            pltpu.SemaphoreType.DMA((2,)),
            pltpu.SemaphoreType.DMA((11,)),
            pltpu.SemaphoreType.DMA((11,)),
            pltpu.SemaphoreType.DMA((2 + PAD // 8,)),
            pltpu.SemaphoreType.DMA((2 + PAD // 8,)),
        ],
        compiler_params=pltpu.CompilerParams(
            collective_id=0, has_side_effects=True, vmem_limit_bytes=60 * 1024 * 1024
        ),
        name="coupling",
    )(atm_state, owners.T, ocean_tile.T, centroid_offset, remap_weight, ocean_state)
    return results[None, :, :ocells], results[:, ocells : 2 * ocells], results[:, 2 * ocells :]


def solution(mesh):
    return jax.shard_map(
        shards,
        mesh=mesh,
        in_specs=(
            P("fld", None, "cols"),
            P("cols", None),
            P("cols", None),
            P("cols", None, None),
            P("cols", None, None, None),
            P(None, "cols"),
        ),
        out_specs=(P("fld", None, "cols"), P(None, "cols"), P(None, "cols")),
        check_vma=False,
    )
```

```python
import functools
import math

import jax
import jax.numpy as jnp
from jax import lax
from jax.experimental import pallas as pl
from jax.experimental.pallas import tpu as pltpu
from jax.sharding import PartitionSpec as P

TILE = 128
FIELDS = 8
MOST = 3
PAD = 32
LEVELS = 5400.0
LEAST = 1e-30
SMALLEST = 2.0**-24
STEP = 31.0 * math.log(2.0) / 65534.0
MIDDLE = -8.5 * math.log(2.0)
MESH = pl.DeviceIdType.MESH
F32 = jnp.float32
BF16 = jnp.bfloat16
I32 = jnp.int32
I16 = jnp.int16


def split(x):
    high = x.astype(BF16)
    return high, (x - high.astype(F32)).astype(BF16)


def mixed(matrix, x):
    high, low = split(x)
    return jnp.dot(matrix, jnp.concatenate([high, low], axis=0), preferred_element_type=F32)


def twice(matrix):
    return jnp.concatenate([matrix, matrix], axis=1)


def kernel(
    ring, samples, tiles, reach, otiles,
    atm_hbm, owners_hbm, otile_hbm, cent_hbm, w_hbm, ocean_hbm,
    out,
    rows_next, rows_back, atm, owners, otile, cent, w, ocean,
    val, part, pick, pick_t, spread, oc, table, col_inverse, lhs,
    send0, recv0, ends_sent, ends_got, send1a, recv1a, send1, recv1, send2a, recv2a, send2, recv2,
    send3, recv3, send3y, recv3y, send4, recv4, send5, recv5,
    in_sem, w_sem, halo_send, halo_recv, ssem, rsem, psend, precv,
):
    cols = ring * ring
    chips = samples // 2
    slots = MOST * ring
    rows = ring * slots
    entries = reach * PAD
    ends = 2 * reach
    col = lax.axis_index("cols")
    fld = lax.axis_index("fld")
    x, z = col // ring, col % ring
    chip, core = fld // 2, fld % 2
    first = (1 - core) * x + core * z
    second = (1 - core) * z + core * x

    def on_first(p):
        return ((1 - core) * (p * ring + second) + core * (second * ring + p), fld)

    def on_second(p):
        return ((1 - core) * (first * ring + p) + core * (p * ring + first), fld)

    def on_chip(p):
        return (col, p * 2 + core)

    sibling = (col, chip * 2 + 1 - core)
    left, right = (col + cols - 1) % cols, (col + 1) % cols

    barrier = pltpu.get_barrier_semaphore()

    def greet(device):
        pl.semaphore_signal(barrier, inc=1, device_id=device, device_id_type=MESH)

    def far_first(count):
        return sorted(range(1, count), key=lambda d: -min(d, count - d))

    def greet_all(far):
        for d in far_first(ring):
            if (min(d, ring - d) >= 3) == far:
                greet(on_first((first + d) % ring))
                greet(on_second((second + d) % ring))
        for d in far_first(chips):
            if (min(d, chips - d) >= 3) == far:
                greet(on_chip((chip + d) % chips))

    greet_all(True)

    small = [
        pltpu.make_async_copy(source, target, in_sem.at[i])
        for i, (source, target) in enumerate(
            ((atm_hbm, atm), (owners_hbm, owners), (otile_hbm, otile), (cent_hbm, cent), (ocean_hbm, ocean))
        )
    ]
    for copy in small:
        copy.start()
    groups, rest = (tiles - 2) // 4, (tiles - 2) % 4
    spans = [(1 + 4 * c, 4) for c in range(groups)] + [(1 + 4 * groups, rest + 1), (0, 1)]

    def weights(c):
        at = pl.ds(*spans[c]) if isinstance(c, int) else pl.ds(1 + 4 * c, 4)
        return pltpu.make_async_copy(w_hbm.at[at], w.at[at], w_sem.at[c])

    for c in (groups + 1, groups, *range(groups)):
        weights(c).start()

    greet_all(False)
    greet((left, fld))
    greet((right, fld))
    greet(sibling)

    def exchange(stage, count, me, device, source, target):
        def send():
            for d in far_first(count):
                pltpu.make_async_remote_copy(
                    src_ref=source((me + d) % count),
                    dst_ref=target.at[me],
                    send_sem=ssem.at[stage],
                    recv_sem=rsem.at[stage],
                    device_id=device((me + d) % count),
                    device_id_type=MESH,
                ).start()

        others = target.at[pl.ds(0, count - 1)]
        everything = pltpu.make_async_remote_copy(
            src_ref=others, dst_ref=others, send_sem=ssem.at[stage], recv_sem=rsem.at[stage],
            device_id=device((me + 1) % count), device_id_type=MESH,
        )
        return send, everything.wait_recv, everything.wait_send

    def to_sibling(i, source, target):
        return pltpu.make_async_remote_copy(
            src_ref=source, dst_ref=target, send_sem=psend.at[i], recv_sem=precv.at[i],
            device_id=sibling, device_id_type=MESH,
        )

    part[...] = jnp.zeros_like(part)
    col_inverse[...] = jnp.ones_like(col_inverse)
    small[0].wait()
    for t in range(tiles):
        val[t + 1] = atm[0, :, t * TILE : (t + 1) * TILE].astype(F32)
    to_right = pltpu.make_async_remote_copy(
        src_ref=val.at[tiles], dst_ref=val.at[0], send_sem=halo_send.at[0], recv_sem=halo_recv.at[0],
        device_id=(right, fld), device_id_type=MESH,
    )
    to_left = pltpu.make_async_remote_copy(
        src_ref=val.at[1], dst_ref=val.at[tiles + 1], send_sem=halo_send.at[1], recv_sem=halo_recv.at[1],
        device_id=(left, fld), device_id_type=MESH,
    )
    small[1].wait()
    small[2].wait()
    lane = lax.broadcasted_iota(I32, (FIELDS, TILE), 1)

    def across(ref, fill):
        table[...] = jnp.full((8, TILE), fill, F32)
        table[:reach, :tiles] = ref[...].astype(F32)
        line = jnp.broadcast_to(table[0:1], (8, TILE))
        for k in range(1, reach):
            shifted = pltpu.roll(jnp.broadcast_to(table[k : k + 1], (8, TILE)), k * PAD, 1)
            line = jnp.where(lane >= k * PAD, shifted, line)
        return line[:1]

    owner_across = across(owners, float(cols))
    tile_across = across(otile, 0.0)
    owner_down = jnp.broadcast_to(owner_across, (entries, entries)).T
    at_row = lax.broadcasted_iota(I32, (entries, entries), 0)
    at_lane = lax.broadcasted_iota(I32, (entries, entries), 1)
    same = owner_down == owner_across
    rank_down = jnp.sum((same & (at_lane < at_row)).astype(F32), axis=1, keepdims=True).astype(I32)
    rank_across = jnp.sum((same & (at_row < at_lane)).astype(F32), axis=0, keepdims=True).astype(I32)

    def slot(owner, rank):
        owner = owner.astype(I32)
        high = owner // ring
        low = owner - high * ring
        group = (1 - core) * high + core * low
        place = (1 - core) * low + core * high
        return jnp.where(owner < cols, group * slots + rank * ring + place, -1)

    def place_of(owner):
        owner = owner.astype(I32)
        high = owner // ring
        low = owner - high * ring
        return (1 - core) * high + core * low, (1 - core) * low + core * high

    group_across, place_across = place_of(owner_across)
    group_down, place_down = place_of(owner_down)
    slot_across = jnp.where(owner_across < cols, group_across * slots + rank_across * ring + place_across, -1)
    seat_down = rank_down * ring + place_down
    slot_down = jnp.where(owner_down < cols, group_down * slots + seat_down, -1)[:, :1]
    pick_f = (lax.broadcasted_iota(I32, (rows, entries), 0) == slot_across).astype(F32)
    pick[...] = twice(pick_f.astype(BF16))
    pick_b = (lax.broadcasted_iota(I32, (entries, rows), 1) == slot_down).astype(F32).astype(BF16)
    pick_t[...] = twice(pick_b)

    stride = slots + ends
    per_line = TILE // stride
    base = (first % per_line) * stride
    ocean_row = place_across * 8 + tile_across.astype(I32) + 1
    group_row = lax.broadcasted_iota(I32, (8, entries), 0) == group_across
    marked = jnp.where(group_row & (owner_across < cols), ocean_row, 0).astype(F32).astype(BF16)
    tile_at, k_at = at_row % PAD, at_row // PAD
    seated = (at_lane == base + seat_down) & (owner_down < cols)
    seated = seated | (tile_at == 0) & (at_lane == base + slots + k_at)
    seated = seated | (tile_at == tiles - 1) & (at_lane == base + slots + reach + k_at)
    named = jnp.dot(marked, seated.astype(F32).astype(BF16), preferred_element_type=F32)
    line_of = lax.broadcasted_iota(I32, (8, TILE), 0) == first // per_line
    for g in range(ring):
        send0[g, :8] = jnp.where(line_of, named[g : g + 1], 0.0)
    send_named, arrive0, leave0 = exchange(0, ring, first, on_first, lambda p: send0.at[p], recv0)

    small[4].wait()
    for r in range(4):
        oc[r] = jnp.zeros((8, TILE), F32)
        for t in range(otiles):
            oc[r, t : t + 1, :] = ocean[r : r + 1, t * TILE : (t + 1) * TILE]

    small[3].wait()
    zeros = jnp.zeros((16, TILE), F32)
    row8 = lax.broadcasted_iota(I32, (8, TILE), 0)
    last_lane = TILE - 1
    extra = jnp.where(row8 == 0, 1.0, 0.0)
    extra = jnp.where((row8 == 1) & (lane == 0) | (row8 == 2) & (lane == last_lane), 1.0, extra)

    def rebuild(t, before, here, after):
        low = jnp.where(lane == 0, pltpu.roll(before, 1, 1), pltpu.roll(here, 1, 1))
        high = jnp.where(lane == last_lane, pltpu.roll(after, last_lane, 1), pltpu.roll(here, last_lane, 1))
        slope = 0.5 * (high - low)
        return [here + cent[t, k : k + 1, :] * slope for k in range(reach)]

    def tile_sums(t, rebuilt):
        operand, operator = [], []
        for k in range(reach):
            block = jnp.concatenate([rebuilt[k], extra], axis=0)
            operand.append(jnp.concatenate([zeros, block] if k % 2 else [block, zeros], axis=1))
        for k in range(0, reach, 2):
            operator.append(jnp.concatenate([w[t, k], w[t, k + 1]], axis=1))
        product = lax.dot_general(
            jnp.concatenate(operand, axis=0).astype(BF16), jnp.concatenate(operator, axis=0),
            (((1,), (1,)), ((), ())), preferred_element_type=F32,
        )
        for k in range(reach):
            sums = product[16 * k : 16 * k + 16, k // 2 * TILE : (k // 2 + 1) * TILE]
            part[pl.ds(k * PAD + t, FIELDS, stride=entries), :] = sums[:FIELDS]
            part[pl.ds(FIELDS * entries + k * PAD + t, 1), :] = sums[FIELDS : FIELDS + 1]
        return [product[16 * k : 16 * k + 16, k // 2 * TILE : (k // 2 + 1) * TILE] for k in range(reach)]

    def inner_sums(t):
        return tile_sums(t, rebuild(t, val[t], val[t + 1], val[t + 2]))

    def group_sums(c, carry):
        weights(c).wait()
        for q in range(4):
            inner_sums(1 + 4 * c + q)
        return carry

    weights(groups + 1).wait()
    here = val[1]
    cut = [jnp.where(lane == 0, 0.0, x) for x in rebuild(0, here, here, val[2])]
    low_weights = [x[FIELDS + 1 : FIELDS + 2] for x in tile_sums(0, cut)]
    weights(groups).wait()
    here = val[tiles]
    cut = [jnp.where(lane == last_lane, 0.0, x) for x in rebuild(tiles - 1, val[tiles - 1], here, here)]
    high_weights = [x[FIELDS + 2 : FIELDS + 3] for x in tile_sums(tiles - 1, cut)]
    end_weights = jnp.concatenate(low_weights + high_weights, axis=0)
    for g in range(ring):
        send0[g, 8:] = end_weights
    for q in range(rest):
        inner_sums(1 + 4 * groups + q)

    early = min(groups, 5)
    lax.fori_loop(0, early, group_sums, 0)
    pl.semaphore_wait(barrier, 3 + 2 * (ring - 1) + chips - 1)
    send_named()
    to_right.start()
    to_left.start()
    recv0[first] = send0[first]
    lax.fori_loop(early, groups, group_sums, 0)

    area_code = jnp.maximum(part[FIELDS * entries :], SMALLEST)
    area_code = jnp.round((jnp.log(area_code) - MIDDLE) * (1.0 / STEP))
    area_code = jnp.clip(area_code, -32767.0, 32767.0)
    scale = LEVELS / jnp.exp(area_code * STEP + MIDDLE)
    sent1 = []
    for m, (source, target) in enumerate(((send1a, recv1a), (send1, recv1))):
        codes = [jnp.round(part[f * entries : (f + 1) * entries] * scale) for f in range(4 * m, 4 * m + 4)]
        if m == 0:
            codes.append(area_code)
        count = len(codes)
        codes = mixed(pick[...], jnp.concatenate(codes, axis=1))
        codes = [codes[:, i * TILE : (i + 1) * TILE] for i in range(count)]
        for g in range(ring):
            block = [x[g * slots : (g + 1) * slots] for x in codes]
            if source.shape[1] > count * slots:
                block.append(jnp.zeros((source.shape[1] - count * slots, TILE), F32))
            source[g] = jnp.concatenate(block, axis=0).astype(I32).astype(I16)
        send, *done = exchange(1 + m, ring, first, on_first, lambda p: source.at[p], target)
        send()
        sent1.append(done)
    recv1a[first] = send1a[first]
    recv1[first] = send1[first]

    to_right.wait_recv()
    to_left.wait_recv()
    end_values = jnp.zeros((8, TILE), F32)
    low = rebuild(0, val[0], val[1], val[2])
    high = rebuild(tiles - 1, val[tiles - 1], val[tiles], val[tiles + 1])
    for k in range(reach):
        moved = pltpu.roll(low[k], k, 1) if k else low[k]
        end_values = jnp.where(lane == k, moved, end_values)
        end_values = jnp.where(lane == reach + k, pltpu.roll(high[k], reach + 1 + k, 1), end_values)
    end_values = end_values.astype(BF16).astype(F32)
    ends_sent[...] = jnp.concatenate([end_values, jnp.zeros((TILE - 8, TILE), F32)], axis=0).T[:ends]
    send, arrive_ends, leave_ends = exchange(4, ring, first, on_first, lambda p: ends_sent, ends_got)
    send()
    ends_got[first] = ends_sent[...]

    arrive0()
    lines = jnp.zeros((8, TILE), F32)
    for p in range(ring):
        lines = lines + recv0[p, :8]
    want = (lax.broadcasted_iota(I32, (TILE, TILE), 0) + 1).astype(F32)
    member = [(want == lines[i : i + 1]).astype(F32) for i in range(-(-ring // per_line))]
    gather = jnp.concatenate(member, axis=1)[: 8 * ring, : ring * stride]
    gather = twice(gather.astype(BF16))
    back_rows = jnp.concatenate([x.T for x in member], axis=0)[: ring * stride]
    spread[...] = twice(back_rows[:, : 8 * ring].astype(BF16))
    end_rows_back = back_rows.reshape(ring, stride, TILE)[:, slots:].reshape(ring * ends, TILE)
    end_rows_back = [end_rows_back, jnp.zeros((TILE - ring * ends, TILE), F32)]
    gather_ends = jnp.concatenate(end_rows_back, axis=0).T[: 8 * ring, : ring * ends]
    gather_ends = twice(gather_ends.astype(BF16))
    end_weights = recv0[:, 8:] * LEVELS

    def stacked(of_slots, of_ends):
        return jnp.concatenate([of_slots, of_ends], axis=1).reshape(ring * stride, TILE)

    def column_area(c, carry):
        for q in range(chunk):
            t = c * chunk + q
            area = jnp.sum(w[t].reshape(reach * TILE, TILE).astype(F32), axis=0, keepdims=True)
            col_inverse[pl.ds(t, 1), :] = 1.0 / area
        return carry

    chunk = 4 if tiles % 4 == 0 else 1
    lax.fori_loop(0, tiles // chunk, column_area, 0)

    send, arrive2a, leave2a = exchange(5, ring, second, on_second, lambda p: send2a.at[p], recv2a)
    sent1[0][0]()
    codes1 = recv1a[...].astype(I32).astype(F32)
    areas = jnp.exp(codes1[:, 4 * slots : 5 * slots] * STEP + MIDDLE)
    dense_area = mixed(gather, stacked(areas, jnp.zeros((ring, ends, TILE), F32)))
    send2a[...] = dense_area.reshape(ring, 8, TILE)
    send()
    recv2a[second] = send2a[second]
    per_area = 1.0 / jnp.maximum(dense_area, LEAST)
    no_ends = jnp.zeros((ring, ends, TILE), F32)

    def dense_sums(codes):
        sums = [stacked(codes[:, i * slots : (i + 1) * slots] * areas, no_ends) for i in range(4)]
        return mixed(gather, jnp.concatenate(sums, axis=1))

    def dense_ends(m):
        sums = [ends_got[:, :, f : f + 1] * end_weights for f in range(4 * m, 4 * m + 4)]
        return mixed(gather_ends, jnp.concatenate([x.reshape(ring * ends, TILE) for x in sums], axis=1))

    dense = [dense_sums(codes1)]
    sent1[1][0]()
    dense.append(dense_sums(recv1[...].astype(I32).astype(F32)))
    arrive_ends()
    sent2 = []
    for m in range(2):
        total = dense[m] + dense_ends(m)
        means = [(total[:, i * TILE : (i + 1) * TILE] * per_area).reshape(ring, 8, TILE) for i in range(4)]
        send2[m] = jnp.round(jnp.concatenate(means, axis=1)).astype(I32).astype(I16)
        send, *done = exchange(6 + m, ring, second, on_second, lambda p: send2.at[m, p], recv2.at[m])
        send()
        sent2.append(done)
        recv2[m, second] = send2[m, second]
    arrive2a()

    coverage = jnp.zeros((8, TILE), F32)
    for p in range(ring):
        coverage = coverage + recv2a[p]
    per_coverage = 1.0 / (LEVELS * jnp.maximum(coverage, 1.0))

    def half_forcing(m):
        arrive, _ = sent2[m]
        arrive()
        total = jnp.zeros((4, 8, TILE), F32)
        for p in range(ring):
            total = total + recv2[m, p].astype(I32).astype(F32).reshape(4, 8, TILE) * recv2a[p][None]
        return total * per_coverage[None]

    def softplus(v):
        return jnp.maximum(v, 0.0) + jnp.log1p(jnp.exp(-jnp.abs(v)))

    sst, uo, vo = oc[0], oc[1], oc[2]
    insolation = 0.5 + 1.5 * fld.astype(F32) / (samples - 1)
    wind_u, wind_v, air, vapour = half_forcing(0)
    slip_u = wind_u - uo
    slip_v = wind_v - vo
    wind_speed = jnp.sqrt(slip_u * slip_u + slip_v * slip_v + 0.25)
    sensible = 0.4 * wind_speed * (sst - air)
    stress_u = 0.5 * wind_speed * slip_u
    stress_v = 0.5 * wind_speed * slip_v
    pressure, short, long, rain = half_forcing(1)
    saturation = 0.9 * jnp.exp(0.07 * sst - 0.1 * pressure)
    latent = 0.4 * wind_speed * (saturation - vapour)
    net_heat = insolation * softplus(short) + 0.3 * long - 0.1 * sst - sensible - latent
    freshwater = softplus(rain) - latent
    send3[0] = net_heat
    send3[1] = stress_u
    send3[2] = stress_v
    send3[3] = -freshwater

    mine, other = pl.ds(2 * core, 2), pl.ds(2 - 2 * core, 2)
    pair_copy = to_sibling(0, send3.at[other], recv3)
    pair_copy.start()
    pair_copy.wait_recv()
    send3y[...] = send3[mine] + recv3[...]
    send, arrive, leave3 = exchange(8, chips, chip, on_chip, lambda p: send3y, recv3y)
    send()
    recv3y[chip] = send3y[...]
    for i, flux in enumerate((stress_u, stress_v, net_heat, freshwater)):
        for t in range(otiles):
            out[i : i + 1, t * TILE : (t + 1) * TILE] = flux[t : t + 1]
    for leave in (leave0, leave_ends, leave2a, to_right.wait_send, to_left.wait_send):
        leave()
    for _, leave in sent1 + sent2:
        leave()
    pair_copy.wait_send()
    arrive()
    flux_sum = recv3y[0]
    for p in range(1, chips):
        flux_sum = flux_sum + recv3y[p]
    state = oc[mine] + (0.5 / samples) * flux_sum
    send4[...] = state

    send, arrive, leave4 = exchange(9, ring, second, on_second, lambda p: send4, recv4)
    send()
    recv4[second] = state
    rows_next[mine] = state
    ocean_copy = to_sibling(1, rows_next.at[mine], rows_next.at[mine])
    ocean_copy.start()
    leave3()
    arrive()

    states = [recv4[:, r].reshape(ring * 8, TILE) for r in range(2)]
    slotted = mixed(spread[...], jnp.concatenate(states, axis=1))
    for p in range(ring):
        for r in range(2):
            send5[p, r] = slotted[p * stride : p * stride + slots, r * TILE : (r + 1) * TILE]
    send, arrive, leave5 = exchange(10, ring, first, on_first, lambda p: send5.at[p], recv5)
    send()
    recv5[first] = send5[first]
    to_sibling(1, rows_next.at[mine], rows_next.at[other]).wait_recv()
    for r in range(4):
        for t in range(otiles):
            out[r : r + 1, (otiles + t) * TILE : (otiles + t + 1) * TILE] = rows_next[r, t : t + 1]
    ocean_copy.wait_send()
    leave4()
    arrive()

    states = [recv5[:, r].reshape(rows, TILE) for r in range(2)]
    entry = mixed(pick_t[...], jnp.concatenate(states, axis=1))
    high, low = split(entry)
    high, low = high.astype(F32), low.astype(F32)
    for k in range(reach):
        for j in range(PAD // 8):
            at = slice(k * PAD + j * 8, k * PAD + j * 8 + 8)
            block = [high[at, :TILE], low[at, :TILE], high[at, TILE:], low[at, TILE:]]
            lhs[j, :, k * TILE : (k + 1) * TILE] = jnp.concatenate(block, axis=0).astype(BF16)


    def results(j):
        at = pl.ds(j * 8, 8)
        return to_sibling(2 + j, rows_back.at[mine, at], rows_back.at[mine, at])

    def remap(j, count):
        operand = lhs[j]
        one = two = jnp.zeros((8, TILE), F32)
        for q in range(count):
            sums = jnp.dot(operand, w[j * 8 + q].reshape(reach * TILE, TILE), preferred_element_type=F32)
            one = jnp.where(row8 == q, sums[0:8] + sums[8:16], one)
            two = jnp.where(row8 == q, sums[16:24] + sums[24:32], two)
        at = pl.ds(j * 8, 8)
        inverse = col_inverse[at]
        rows_back[2 * core, at] = one * inverse
        rows_back[2 * core + 1, at] = two * inverse
        results(j).start()

    def full_remap(j, carry):
        remap(j, 8)
        return carry

    whole, last = tiles // 8, tiles % 8
    lax.fori_loop(0, whole, full_remap, 0)
    if last:
        remap(whole, last)
    leave5()
    for j in range(whole + (last > 0)):
        at = pl.ds(j * 8, 8)
        to_sibling(2 + j, rows_back.at[mine, at], rows_back.at[other, at]).wait_recv()
        for r in range(4):
            for t in range(8 * j, min(8 * j + 8, tiles)):
                out[r : r + 1, (2 * otiles + t) * TILE : (2 * otiles + t + 1) * TILE] = rows_back[r, t : t + 1]
    for j in range(whole + (last > 0)):
        results(j).wait_send()


def shards(atm_state, owners, ocean_tile, centroid_offset, remap_weight, ocean_state):
    ring = math.isqrt(lax.axis_size("cols"))
    samples = lax.axis_size("fld")
    cells = atm_state.shape[2]
    tiles = cells // TILE
    reach = owners.shape[1]
    ocells = ocean_state.shape[1]
    otiles = ocells // TILE
    chips = samples // 2
    slots = MOST * ring
    rows = ring * slots
    entries = reach * PAD
    hbm = pl.BlockSpec(memory_space=pltpu.HBM)
    vmem = pl.BlockSpec(memory_space=pltpu.VMEM)
    results = pl.pallas_call(
        functools.partial(kernel, ring, samples, tiles, reach, otiles),
        out_shape=pltpu.VMEM((4, 2 * ocells + cells), F32),
        in_specs=[hbm] * 6,
        out_specs=vmem,
        scratch_shapes=[
            pltpu.VMEM((4, 8, TILE), F32),
            pltpu.VMEM((4, PAD, TILE), F32),
            pltpu.VMEM(atm_state.shape, BF16),
            pltpu.VMEM((reach, tiles), I32),
            pltpu.VMEM((reach, tiles), I32),
            pltpu.VMEM((tiles, reach, TILE), F32),
            pltpu.VMEM((tiles, reach, TILE, TILE), BF16),
            pltpu.VMEM((4, ocells), F32),
            pltpu.VMEM((tiles + 2, FIELDS, TILE), F32),
            pltpu.VMEM(((FIELDS + 1) * entries, TILE), F32),
            pltpu.VMEM((rows, 2 * entries), BF16),
            pltpu.VMEM((entries, 2 * rows), BF16),
            pltpu.VMEM((ring * (slots + 2 * reach), 16 * ring), BF16),
            pltpu.VMEM((4, 8, TILE), F32),
            pltpu.VMEM((8, TILE), F32),
            pltpu.VMEM((PAD, TILE), F32),
            pltpu.VMEM((PAD // 8, 32, reach * TILE), BF16),
            pltpu.VMEM((ring, 8 + 2 * reach, TILE), F32),
            pltpu.VMEM((ring, 8 + 2 * reach, TILE), F32),
            pltpu.VMEM((2 * reach, TILE), F32),
            pltpu.VMEM((ring, 2 * reach, TILE), F32),
            pltpu.VMEM((ring, -(-5 * slots // 16) * 16, TILE), I16),
            pltpu.VMEM((ring, -(-5 * slots // 16) * 16, TILE), I16),
            pltpu.VMEM((ring, 4 * slots, TILE), I16),
            pltpu.VMEM((ring, 4 * slots, TILE), I16),
            pltpu.VMEM((ring, 8, TILE), F32),
            pltpu.VMEM((ring, 8, TILE), F32),
            pltpu.VMEM((2, ring, 4 * 8, TILE), I16),
            pltpu.VMEM((2, ring, 4 * 8, TILE), I16),
            pltpu.VMEM((4, 8, TILE), F32),
            pltpu.VMEM((2, 8, TILE), F32),
            pltpu.VMEM((2, 8, TILE), F32),
            pltpu.VMEM((chips, 2, 8, TILE), F32),
            pltpu.VMEM((2, 8, TILE), F32),
            pltpu.VMEM((ring, 2, 8, TILE), F32),
            pltpu.VMEM((ring, 2, slots, TILE), F32),
            pltpu.VMEM((ring, 2, slots, TILE), F32),
            pltpu.SemaphoreType.DMA((5,)),
            pltpu.SemaphoreType.DMA((tiles,)),
            pltpu.SemaphoreType.DMA((2,)),
            pltpu.SemaphoreType.DMA((2,)),
            pltpu.SemaphoreType.DMA((11,)),
            pltpu.SemaphoreType.DMA((11,)),
            pltpu.SemaphoreType.DMA((2 + PAD // 8,)),
            pltpu.SemaphoreType.DMA((2 + PAD // 8,)),
        ],
        compiler_params=pltpu.CompilerParams(
            collective_id=0, has_side_effects=True, vmem_limit_bytes=60 * 1024 * 1024
        ),
        name="coupling",
    )(atm_state, owners.T, ocean_tile.T, centroid_offset, remap_weight, ocean_state)
    return results[None, :, :ocells], results[:, ocells : 2 * ocells], results[:, 2 * ocells :]


def solution(mesh):
    return jax.shard_map(
        shards,
        mesh=mesh,
        in_specs=(
            P("fld", None, "cols"),
            P("cols", None),
            P("cols", None),
            P("cols", None, None),
            P("cols", None, None, None),
            P(None, "cols"),
        ),
        out_specs=(P("fld", None, "cols"), P(None, "cols"), P(None, "cols")),
        check_vma=False,
    )
```
